128 devices in a mesh: dp: 64 (over z, y, x), tensor: 2 (over core).
Axes of the slice: x: 4, y: 4, z: 4, core: 2. Of those that a mesh axis runs over, the one named last changes fastest.
Arguments:
- byte_input: bfloat16 [128, 512, 768], P('dp', 'tensor'), may hold values from -6 to 6
- item_lengths: int32 [128, 2], P('dp'), may hold values from 128 to 384, as said below
- latent_array: bfloat16 [256, 1280], P('tensor'), may hold values from -6 to 6
- in_gain: float32 [768], replicated, may hold values from 0.5 to 1.5
- in_bias: float32 [768], replicated, may hold values from -3 to 3
- lat_gain: float32 [1280], replicated, may hold values from 0.5 to 1.5
- lat_bias: float32 [1280], replicated, may hold values from -3 to 3
- w_query: bfloat16 [1280, 256], P(None, 'tensor'), may hold values from -0.15625 to 0.15625
- w_key: bfloat16 [768, 256], P(None, 'tensor'), may hold values from -0.21875 to 0.21875
- w_value: bfloat16 [768, 1280], P(None, 'tensor'), may hold values from -0.21875 to 0.21875
- w_out: bfloat16 [1280, 1280], P('tensor'), may hold values from -1.5 to 1.5
- b_out: float32 [1280], replicated, may hold values from -3 to 3
- mlp_gain: float32 [1280], replicated, may hold values from 0.5 to 1.5
- mlp_bias: float32 [1280], replicated, may hold values from -3 to 3
- w_up: bfloat16 [1280, 1280], P(None, 'tensor'), may hold values from -0.15625 to 0.15625
- b_up: float32 [1280], P('tensor'), may hold values from -3 to 3
- w_down: bfloat16 [1280, 1280], P('tensor'), may hold values from -0.25 to 0.25
- b_down: float32 [1280], replicated, may hold values from -3 to 3
- grad_out: bfloat16 [128, 256, 2, 1280], P('dp', 'tensor'), may hold values from -6 to 6
Outputs:
- encoded: bfloat16 [128, 256, 2, 1280], P('dp', 'tensor')
- byte_grad: float32 [128, 512, 768], P('dp', 'tensor')
- latent_grad: float32 [256, 1280], P('tensor')
- in_gain_grad: float32 [768], replicated
- in_bias_grad: float32 [768], replicated
- lat_gain_grad: float32 [1280], replicated
- lat_bias_grad: float32 [1280], replicated
- w_query_grad: float32 [1280, 256], P(None, 'tensor')
- w_key_grad: float32 [768, 256], P(None, 'tensor')
- w_value_grad: float32 [768, 1280], P(None, 'tensor')
- w_out_grad: float32 [1280, 1280], P('tensor')
- b_out_grad: float32 [1280], replicated
- mlp_gain_grad: float32 [1280], replicated
- mlp_bias_grad: float32 [1280], replicated
- w_up_grad: float32 [1280, 1280], P(None, 'tensor')
- b_up_grad: float32 [1280], P('tensor')
- w_down_grad: float32 [1280, 1280], P('tensor')
- b_down_grad: float32 [1280], replicated
The draws below stay inside these ranges and needn't reach their ends.
Inputs may be any that keep to these rules, and one draw needn't show every extreme that they name: `item_lengths`: each pack holds one item of 384 bytes and one of 128 bytes, in either order.
All inputs are finite; a program needn't handle non-finite values.
Results may differ from the reference program's by a relative error of at most 0.014.
Values may be sent and summed in bfloat16 or wider, within the bound.
No kernel may reach another device: no remote copies, remote signals or barrier semaphores. Data moves between devices by JAX's collectives and lax.ppermute only.
A program may use at most 128 MiB of HBM per device.

```python
import jax
import jax.numpy as jnp
from jax import lax

D_IN = 768
D_LAT = 1280
NUM_LAT = 256
HEADS = 8
QK_W = 256
V_W = 1280
TOK_DEV = 256
ITEMS = 2
PACK = 512
PACKS = 128


def draw_item_lengths(key, part):
    key = jax.random.fold_in(key, 11)
    flipped = jax.random.randint(key, (PACKS, 1), 0, 2, dtype=jnp.int32)
    shorter = TOK_DEV // 2
    longer = PACK - shorter
    first_len = flipped * shorter + (1 - flipped) * longer
    return jnp.concatenate([first_len, PACK - first_len], axis=1).astype(jnp.int32)


def steps_of(own_key, shape, shards, low, largest):
    loudness = 1.0
    for axis_at, shards_of in shards:
        draws = jax.random.uniform(jax.random.fold_in(jax.random.fold_in(own_key, 6), axis_at), (shards_of,), jnp.float32, low / len(shards), largest / len(shards))
        loudness = loudness * jnp.repeat(jnp.exp(draws), shape[axis_at] // shards_of).reshape((-1,) + (1,) * (len(shape) - 1 - axis_at))
    return loudness


def centred(own_key, dims, width, bound, pieces=(), held_as=jnp.bfloat16):
    array = width * jax.random.normal(own_key, dims, jnp.float32)
    if pieces:
        array = array * steps_of(own_key, dims, pieces, -0.22, 0.18)
    return jnp.clip(array, -bound, bound).astype(held_as)


def setup_inputs(seed: int = 0) -> dict:
    key_list = jax.random.split(jax.random.key(seed), 20)
    byte_input = centred(key_list[0], (PACKS, PACK, D_IN), 1.0, 6.0, ((0, 64), (1, 2)))
    item_lengths = draw_item_lengths(jax.random.fold_in(key_list[19], 71), 0)
    latent_array = centred(key_list[2], (NUM_LAT, D_LAT), 1.0, 6.0, ((0, 2),))
    in_gain = jnp.clip(1.0 + 0.1 * jax.random.normal(key_list[3], (D_IN,), jnp.float32), 0.5, 1.5)
    in_bias = centred(key_list[4], (D_IN,), 0.3, 3.0, (), jnp.float32)
    lat_gain = jnp.clip(1.0 + 0.1 * jax.random.normal(key_list[5], (D_LAT,), jnp.float32), 0.5, 1.5)
    lat_bias = centred(key_list[6], (D_LAT,), 0.3, 3.0, (), jnp.float32)
    w_query = centred(key_list[7], (D_LAT, QK_W), D_LAT ** -0.5, 0.15625, ((1, 2),))
    w_key = centred(key_list[8], (D_IN, QK_W), D_IN ** -0.5, 0.21875, ((1, 2),))
    w_value = centred(key_list[9], (D_IN, V_W), D_IN ** -0.5, 0.21875, ((1, 2),))
    w_out = centred(key_list[10], (V_W, D_LAT), (max(1, 6 * V_W // PACK)) ** -0.5, 1.5, ((0, 2),))
    b_out = centred(key_list[11], (D_LAT,), 0.3, 3.0, (), jnp.float32)
    mlp_gain = jnp.clip(1.0 + 0.1 * jax.random.normal(key_list[12], (D_LAT,), jnp.float32), 0.5, 1.5)
    mlp_bias = centred(key_list[13], (D_LAT,), 0.3, 3.0, (), jnp.float32)
    w_up = centred(key_list[14], (D_LAT, D_LAT), D_LAT ** -0.5, 0.15625, ((1, 2),))
    b_up = centred(key_list[15], (D_LAT,), 0.3, 3.0, ((0, 2),), jnp.float32)
    w_down = centred(key_list[16], (D_LAT, D_LAT), (D_LAT // 2) ** -0.5, 0.25, ((0, 2),))
    b_down = centred(key_list[17], (D_LAT,), 0.3, 3.0, (), jnp.float32)
    grad_out = centred(key_list[18], (PACKS, NUM_LAT, ITEMS, D_LAT), 1.0, 6.0, ((0, 64), (1, 2)))
    return dict(byte_input=byte_input, item_lengths=item_lengths, latent_array=latent_array, in_gain=in_gain, in_bias=in_bias, lat_gain=lat_gain, lat_bias=lat_bias, w_query=w_query, w_key=w_key, w_value=w_value, w_out=w_out, b_out=b_out, mlp_gain=mlp_gain, mlp_bias=mlp_bias, w_up=w_up, b_up=b_up, w_down=w_down, b_down=b_down, grad_out=grad_out)


@jax.custom_vjp
def low(v):
    return lax.optimization_barrier(v.astype(jnp.bfloat16)).astype(jnp.float32)

@jax.custom_vjp
def low_back(v):
    return v

def low_keep(v):
    return (low(v), None)

def low_pass(kept, grad):
    return (grad,)

def back_keep(v):
    return (v, None)

def back_low(kept, grad):
    return (low(grad),)
low.defvjp(low_keep, low_pass)
low_back.defvjp(back_keep, back_low)
epsilon = 1e-05
highest = lax.Precision.HIGHEST

def layer_norm(rows, gain, bias):
    average = lax.optimization_barrier(jnp.mean(rows, axis=-1, keepdims=True))
    centered = rows - average
    variance = lax.optimization_barrier(jnp.mean(centered * centered, axis=-1, keepdims=True))
    return centered * lax.rsqrt(variance + epsilon) * gain + bias

def forward(byte_input, latent_array, in_gain, in_bias, lat_gain, lat_bias, w_query, w_key, w_value, w_out, b_out, mlp_gain, mlp_bias, w_up, b_up, w_down, b_down, item_lengths):
    qk_dim = QK_W // HEADS
    v_dim = V_W // HEADS
    score_scale = qk_dim ** (-0.5)
    latent_norm = low(layer_norm(latent_array, lat_gain, lat_bias))
    queries = low(jnp.dot(latent_norm, w_query, precision=highest))
    position = jnp.arange(PACK, dtype=jnp.int32)

    def one_pack(packed):
        byte_rows, lengths = packed
        query_heads = low_back(queries).reshape(NUM_LAT, HEADS, qk_dim)
        byte_norm = low(layer_norm(byte_rows, in_gain, in_bias))
        key_heads = low(low_back(jnp.dot(byte_norm, w_key, precision=highest))).reshape(PACK, HEADS, qk_dim)
        value_heads = low(low_back(jnp.dot(byte_norm, w_value, precision=highest))).reshape(PACK, HEADS, v_dim)
        raw_scores = low_back(jnp.einsum('lhd,jhd->hlj', query_heads, key_heads, precision=highest) * score_scale)
        item_end = jnp.cumsum(lengths).astype(jnp.int32)
        starts = (item_end - lengths).astype(jnp.int32)
        chosen = ((position[None, :] >= starts[:, None]) & (position[None, :] < item_end[:, None]))[:, None, None, :]
        masked = jnp.where(chosen, raw_scores[None], -1e+30)
        row_max = lax.optimization_barrier(jnp.max(masked, axis=-1, keepdims=True))
        exponent = jnp.where(chosen, jnp.exp(masked - row_max), 0.0)
        soft_low = low(exponent / lax.optimization_barrier(jnp.sum(exponent, axis=-1, keepdims=True)))
        attended = jnp.einsum('ihlj,jhd->lihd', soft_low, value_heads, precision=highest)
        attended = low(low_back(attended.reshape(NUM_LAT * ITEMS, V_W)))
        branch = low_back(jnp.dot(attended, w_out, precision=highest))
        hidden_in = latent_array[:, None, :] + branch.reshape(NUM_LAT, ITEMS, D_LAT) + b_out
        flat_hidden = hidden_in.reshape(NUM_LAT * ITEMS, D_LAT)
        mlp_norm = low(layer_norm(flat_hidden, mlp_gain, mlp_bias))
        hidden_pre = low_back(jnp.dot(mlp_norm, w_up, precision=highest) + b_up)
        activated = low(jax.nn.gelu(hidden_pre, approximate=False))
        down_branch = low_back(jnp.dot(activated, w_down, precision=highest))
        return (flat_hidden + down_branch + b_down).reshape(NUM_LAT, ITEMS, D_LAT)
    return lax.map(jax.checkpoint(one_pack), (byte_input, item_lengths))

def reference(byte_input, item_lengths, latent_array, in_gain, in_bias, lat_gain, lat_bias, w_query, w_key, w_value, w_out, b_out, mlp_gain, mlp_bias, w_up, b_up, w_down, b_down, grad_out):
    floats = [member.astype(jnp.float32) for member in (byte_input, latent_array, in_gain, in_bias, lat_gain, lat_bias, w_query, w_key, w_value, w_out, b_out, mlp_gain, mlp_bias, w_up, b_up, w_down, b_down)]

    def wrapped(*params):
        return forward(*params, item_lengths)
    encoded, pullback = jax.vjp(wrapped, *floats)
    grads = pullback(grad_out.astype(jnp.float32))
    return (encoded.astype(jnp.bfloat16), grads[0], grads[1], grads[2], grads[3], grads[4], grads[5], grads[6], grads[7], grads[8], grads[9], grads[10], grads[11], grads[12], grads[13], grads[14], grads[15], grads[16])
```

```python
import jax
import jax.numpy as jnp
from jax import lax
from jax.experimental import pallas as pl
from jax.experimental.pallas import tpu as pltpu
from jax.sharding import PartitionSpec as P

F32 = jnp.float32
BF16 = jnp.bfloat16
EPS = 1e-05
HEAD_QK = 32
HEAD_V = 160
SCALE = HEAD_QK ** (-0.5)
MB = 1 << 20

SMEM = pl.BlockSpec(memory_space=pltpu.SMEM)
VMEM = pl.BlockSpec(memory_space=pltpu.VMEM)


def shape(rows, columns, dtype=BF16):
    return jax.ShapeDtypeStruct((rows, columns), dtype)


def call(kernel, outs, *args, scalars=0, flops=0, limit=24, scratch=()):
    specs = [SMEM] * scalars + [VMEM] * (len(args) - scalars)
    moved = sum(a.size * a.dtype.itemsize for a in args[scalars:])
    moved += sum(o.size * o.dtype.itemsize for o in jax.tree.leaves(outs))
    return pl.pallas_call(
        kernel,
        out_shape=outs,
        in_specs=specs,
        out_specs=jax.tree.map(lambda _: VMEM, outs),
        scratch_shapes=list(scratch),
        compiler_params=pltpu.CompilerParams(vmem_limit_bytes=limit * MB),
        cost_estimate=pl.CostEstimate(flops=flops, bytes_accessed=moved, transcendentals=0),
    )(*args)


def nn(a, b):
    return jnp.dot(a, b, preferred_element_type=F32)


def nt(a, b):
    return lax.dot_general(a, b, (((1,), (1,)), ((), ())), preferred_element_type=F32)


def tn(a, b):
    return lax.dot_general(a, b, (((0,), (0,)), ((), ())), preferred_element_type=F32)


def norm(rows):
    average = jnp.mean(rows, axis=-1, keepdims=True)
    centered = rows - average
    variance = jnp.mean(centered * centered, axis=-1, keepdims=True)
    inverse = lax.rsqrt(variance + EPS)
    return centered * inverse, inverse


def norm_back(grad, normed, inverse, gain):
    scaled = grad * gain
    mean_term = jnp.mean(scaled, axis=-1, keepdims=True)
    cross_term = jnp.mean(scaled * normed, axis=-1, keepdims=True)
    return inverse * (scaled - mean_term - normed * cross_term)


def column_sum(x):
    return jnp.sum(x, axis=0, keepdims=True)


def latent_kernel(lat_o, lat_x, gain, bias, wq_o, wq_x, latn, q):
    half = lat_o.shape[0]
    for i, ref in enumerate((lat_o, lat_x)):
        u, _ = norm(ref[...].astype(F32))
        latn[i * half : (i + 1) * half, :] = (u * gain[...] + bias[...]).astype(BF16)
    width = wq_o.shape[1]
    q[:, :width] = nn(latn[...], wq_o[...]).astype(BF16)
    q[:, width:] = nn(latn[...], wq_x[...]).astype(BF16)


def bytes_kernel(s, own, oth, gain, bias, wk_o, wk_x, wv_o, wv_x, raw, bn, k, v):
    flip, side = s[0], s[1]
    for b in range(4):
        a = (b + flip) & 3
        off = pl.multiple_of((a & 1) * 128, 128)
        mine = own[pl.ds(off, 128), :].astype(F32)
        other = oth[pl.ds(off, 128), :].astype(F32)
        rows = jnp.where((a >> 1) == side, mine, other)
        here = slice(b * 128, (b + 1) * 128)
        raw[here, :] = rows.astype(BF16)
        u, _ = norm(rows)
        bn[here, :] = (u * gain[...] + bias[...]).astype(BF16)
    x = bn[...]
    qk, vw = wk_o.shape[1], wv_o.shape[1]
    k[:, :qk] = nn(x, wk_o[...]).astype(BF16)
    k[:, qk:] = nn(x, wk_x[...]).astype(BF16)
    v[:, :vw] = nn(x, wv_o[...]).astype(BF16)
    v[:, vw:] = nn(x, wv_x[...]).astype(BF16)


SEGMENTS = ((0, 384), (384, 512))


def join_heads(parts):
    rows = parts[0].shape[0]
    lane = lax.broadcasted_iota(jnp.int32, (rows, 128), 1)
    blocks = [parts[0][:, :128]]
    for c in range(1, 4):
        blocks.append(jnp.where(lane < 32 * c, parts[c - 1][:, 128:], parts[c][:, :128]))
    blocks.append(parts[3][:, 128:])
    return blocks


def attend_kernel(q, k, v, att):
    lats = q.shape[0]
    lane = lax.broadcasted_iota(jnp.int32, (lats, 128), 1)
    for g in range(2):
        qh = q[:, g * 128 : (g + 1) * 128]
        kh = k[:, g * 128 : (g + 1) * 128]
        outs = [[], []]
        for h in range(4):
            qm = jnp.where((lane >= 32 * h) & (lane < 32 * h + 32), qh.astype(F32), 0.0).astype(BF16)
            s = nt(qm, kh) * SCALE
            base = g * 640 + h * 128
            for i, (lo, hi) in enumerate(SEGMENTS):
                part = s[:, lo:hi]
                e = jnp.exp(part - jnp.max(part, axis=-1, keepdims=True))
                p = (e / jnp.sum(e, axis=-1, keepdims=True)).astype(BF16)
                outs[i].append(nn(p, v[lo:hi, base : base + 256]))
        for i in range(2):
            for c, block in enumerate(join_heads(outs[i])):
                at = g * 640 + c * 128
                att[i * lats : (i + 1) * lats, at : at + 128] = block.astype(BF16)


def out_kernel(att, wo_o, wo_x, lat_o, lat_x, b_out, gain, bias, hidden, mn):
    rows = lat_o.shape[0]
    half = wo_o.shape[0]
    hidden[...] = nn(att[:, :half], wo_o[...]) + nn(att[:, half:], wo_x[...]) + b_out[...]
    for i in range(4):
        here = slice(i * rows, (i + 1) * rows)
        x = hidden[here, :] + (lat_x if i % 2 else lat_o)[...].astype(F32)
        hidden[here, :] = x
        u, _ = norm(x)
        mn[here, :] = (u * gain[...] + bias[...]).astype(BF16)


def top_kernel(s, own, oth, gt):
    flip = s[0]
    half = own.shape[0] // 2
    row = lax.broadcasted_iota(jnp.int32, (half, 2 * half), 0)
    column = lax.broadcasted_iota(jnp.int32, (half, 2 * half), 1)
    for i in range(2):
        pick = jnp.where(column == 2 * row + (i ^ flip), 1.0, 0.0).astype(BF16)
        for j, ref in enumerate((own, oth)):
            at = (2 * i + j) * half
            gt[at : at + half, :] = nn(pick, ref[...]).astype(BF16)


def gelu_parts(x):
    t = 1.0 / (1.0 + 0.3275911 * 0.7071067811865476 * jnp.abs(x))
    poly = t * (
        0.254829592
        + t * (-0.284496736 + t * (1.421413741 + t * (-1.453152027 + t * 1.061405429)))
    )
    e = jnp.exp(-0.5 * x * x)
    tail = 0.5 * poly * e
    cumulative = jnp.where(x >= 0.0, 1.0 - tail, tail)
    return x * cumulative, cumulative + x * e * 0.3989422804014327


TILES = ((0, 256), (256, 512), (512, 640))


def up_kernel(mn, gt, wu_o, wu_x, bu_o, bu_x, wd_o, wd_x, act_o, act_x, gp_o, gp_x, bsum_o, bsum_x):
    for wu, bu, wd, act, gp, bsum in (
        (wu_o, bu_o, wd_o, act_o, gp_o, bsum_o),
        (wu_x, bu_x, wd_x, act_x, gp_x, bsum_x),
    ):
        for lo, hi in TILES:
            pre = nn(mn[...], wu[:, lo:hi]) + bu[:, lo:hi]
            back = nt(gt[...], wd[lo:hi, :])
            active, slope = gelu_parts(pre)
            act[:, lo:hi] = active.astype(BF16)
            low = (back * slope).astype(BF16)
            gp[:, lo:hi] = low
            bsum[:, lo:hi] = column_sum(low.astype(F32))


def down_grad_kernel(act_o, act_x, gt, keep, send):
    keep[...] = tn(act_o[...], gt[...]).astype(BF16)
    send[...] = tn(act_x[...], gt[...]).astype(BF16)


def up_grad_kernel(mn, gp_o, gp_x, keep, send):
    keep[...] = tn(mn[...], gp_o[...]).astype(BF16)
    send[...] = tn(mn[...], gp_x[...]).astype(BF16)


def encode_kernel(s, act_o, act_x, wd_o, wd_x, hidden, b_down, enc_o, enc_x, low):
    flip = s[0]
    low[...] = (
        nn(act_o[...], wd_o[...]) + nn(act_x[...], wd_x[...]) + hidden[...] + b_down[...]
    ).astype(BF16)
    half = enc_o.shape[0] // 2
    row = lax.broadcasted_iota(jnp.int32, (2 * half, half), 0)
    column = lax.broadcasted_iota(jnp.int32, (2 * half, half), 1)
    for j, ref in enumerate((enc_o, enc_x)):
        total = None
        for i in range(2):
            pick = jnp.where(row == 2 * column + (i ^ flip), 1.0, 0.0).astype(BF16)
            at = (2 * i + j) * half
            part = nn(pick, low[at : at + half, :])
            total = part if total is None else total + part
        ref[...] = total.astype(BF16)


def hidden_grad_kernel(gp_o, gp_x, wu_o, wu_x, hidden, gt, gain, ghl, res_o, res_x, vec, g):
    g[...] = nt(gp_o[...], wu_o[...]) + nt(gp_x[...], wu_x[...])
    rows = res_o.shape[0]
    sums = [0.0, 0.0, 0.0, 0.0]
    res = [0.0, 0.0]
    for i in range(4):
        here = slice(i * rows, (i + 1) * rows)
        grad = g[here, :]
        top = gt[here, :].astype(F32)
        u, inverse = norm(hidden[here, :])
        total = top + norm_back(grad, u, inverse, gain[...])
        ghl[here, :] = total.astype(BF16)
        res[i % 2] = res[i % 2] + total
        for n, x in enumerate((top, grad * u, grad, total)):
            sums[n] = sums[n] + column_sum(x)
    res_o[...] = res[0].astype(BF16)
    res_x[...] = res[1].astype(BF16)
    for n in range(4):
        vec[n : n + 1, :] = sums[n]


def out_grad_kernel(att, ghl, res_o, res_x, keep, send):
    half = att.shape[1] // 2
    keep[:half, :] = tn(att[:, :half], ghl[...]).astype(BF16)
    send[:half, :] = tn(att[:, half:], ghl[...]).astype(BF16)
    keep[half:, :] = res_o[...]
    send[half:, :] = res_x[...]


def attended_grad_kernel(ghl, wo_o, wo_x, ga):
    half = wo_o.shape[0]
    ga[:, :half] = nt(ghl[...], wo_o[...]).astype(BF16)
    ga[:, half:] = nt(ghl[...], wo_x[...]).astype(BF16)


def attend_back_kernel(q, k, v, ga, gq, gkv):
    lats = q.shape[0]
    lane = lax.broadcasted_iota(jnp.int32, (lats, 128), 1)
    wide = lax.broadcasted_iota(jnp.int32, (lats, 256), 1)
    gq_rows = []
    for g in range(2):
        qh = q[:, g * 128 : (g + 1) * 128]
        kt = k[:, g * 128 : (g + 1) * 128].astype(F32).T.astype(BF16)
        for i, (lo, hi) in enumerate(SEGMENTS):
            kh = k[lo:hi, g * 128 : (g + 1) * 128]
            gk = None
            gv = []
            for h in range(4):
                inside = (lane >= 32 * h) & (lane < 32 * h + 32)
                qm = jnp.where(inside, qh.astype(F32), 0.0).astype(BF16)
                s = nt(kh, qm) * SCALE
                e = jnp.exp(s - jnp.max(s, axis=0, keepdims=True))
                p = e / jnp.sum(e, axis=0, keepdims=True)
                base = g * 640 + h * 128
                gw = ga[i * lats : (i + 1) * lats, base : base + 256]
                gm = jnp.where(
                    (wide >= 32 * h) & (wide < 32 * h + 160), gw.astype(F32), 0.0
                ).astype(BF16)
                gp = nt(v[lo:hi, base : base + 256], gm)
                gv.append(nn(p.astype(BF16), gw))
                inner = jnp.sum(p * gp, axis=0, keepdims=True)
                gs = (p * (gp - inner)).astype(BF16)
                part = nn(gs, qm)
                gk = part if gk is None else gk + part
                gq_rows.append(nn(kt[32 * h : 32 * h + 32, lo:hi], gs))
            at = g * 768
            gkv[lo:hi, at : at + 128] = (gk * SCALE).astype(BF16)
            for c, block in enumerate(join_heads(gv)):
                to = at + 128 + c * 128
                gkv[lo:hi, to : to + 128] = block.astype(BF16)
    rows = []
    for g in range(2):
        for h in range(4):
            rows.append(gq_rows[g * 8 + h] + gq_rows[g * 8 + 4 + h])
    gq[...] = (jnp.concatenate(rows, axis=0).T * SCALE).astype(BF16)


def byte_grad_kernel(
    s, gkv, wk_o, wv_o, wk_x, wv_x, raw, bn, gain, gq, vec, bsum_o, bsum_x,
    back_o, back_x, keep, send, g,
):
    flip, side = s[0], s[1]
    g[...] = (
        nt(gkv[:, 0:128], wk_o[...])
        + nt(gkv[:, 128:768], wv_o[...])
        + nt(gkv[:, 768:896], wk_x[...])
        + nt(gkv[:, 896:1536], wv_x[...])
    )
    gain_sum = 0.0
    bias_sum = 0.0
    for b in range(4):
        here = slice(b * 128, (b + 1) * 128)
        grad = g[here, :]
        u, inverse = norm(raw[here, :].astype(F32))
        gain_sum = gain_sum + column_sum(grad * u)
        bias_sum = bias_sum + column_sum(grad)
        back = norm_back(grad, u, inverse, gain[...])
        a = (b + flip) & 3
        off = pl.multiple_of((a & 1) * 128, 128)

        @pl.when((a >> 1) == side)
        def _():
            back_o[pl.ds(off, 128), :] = back

        @pl.when((a >> 1) != side)
        def _():
            back_x[pl.ds(off, 128), :] = back.astype(BF16)

    x = bn[...]
    width = keep.shape[1] - 128
    keep[:, :width] = tn(x, gkv[:, :width]).astype(BF16)
    send[:, :width] = tn(x, gkv[:, width:]).astype(BF16)
    own_q, oth_q = gq[:, :128], gq[:, 128:]
    lats = gq.shape[0]
    half = lats // 2
    keep[:lats, width:] = own_q
    keep[lats : 2 * lats, width:] = oth_q
    send[:half, width:] = oth_q[half:, :]
    send[half:lats, width:] = oth_q[:half, :]
    send[lats : lats + half, width:] = own_q[half:, :]
    send[lats + half : 2 * lats, width:] = own_q[:half, :]
    keep[2 * lats :, width:] = jnp.zeros((keep.shape[0] - 2 * lats, 128), BF16)
    send[2 * lats :, width:] = jnp.zeros((keep.shape[0] - 2 * lats, 128), BF16)

    def lines(values, refs):
        return [
            (ref, values[:, c * 128 : (c + 1) * 128])
            for c in range(values.shape[1] // 128)
            for ref in refs
        ]

    both = [vec[n : n + 1, :] for n in range(4)]
    tail = [gain_sum, bias_sum]
    for ref, middle in (
        (keep, [bsum_o[...], bsum_x[...]]),
        (send, [bsum_x[...], bsum_o[...]]),
    ):
        flat = []
        for value in both + middle + tail:
            for c in range(value.shape[1] // 128):
                flat.append(value[:, c * 128 : (c + 1) * 128])
        while len(flat) % 16:
            flat.append(jnp.zeros((1, 128), F32))
        ref[2 * lats : 2 * lats + len(flat), width:] = jnp.concatenate(flat, axis=0).astype(BF16)


CHIPS = 4


def chip_axes(index):
    return (index // (CHIPS * CHIPS), (index // CHIPS) % CHIPS, index % CHIPS)


def partner_pairs(axis, mask):
    pairs = []
    for chip in range(CHIPS**3):
        for side in range(2):
            where = list(chip_axes(chip))
            where[axis] ^= mask ^ (2 * side)
            other = (where[0] * CHIPS + where[1]) * CHIPS + where[2]
            pairs.append((chip * 2 + side, other * 2 + side))
    return pairs


def half_kept(axis, mask):
    place = chip_axes(lax.axis_index("dp"))[axis]
    side = lax.axis_index("tensor")
    low, high = (place ^ (place >> 1)) & 1, place >> 1
    first, second = (low, high) if mask == 1 else (high, low)
    return jnp.where(side == 0, first, second).astype(jnp.int32).reshape(1)


def pair_swap(x, dim):
    return lax.ppermute(x, ("dp", "tensor"), partner_pairs(*dim))


def core_swap(x):
    return lax.ppermute(x, "tensor", [(0, 1), (1, 0)])


def add_low(a, b):
    return (a.astype(F32) + b.astype(F32)).astype(BF16)


def split_kernel(b, x, r, keep, send):
    rows = keep.shape[0]
    mine = pl.multiple_of(b[0] * rows, 16)
    other = pl.multiple_of((1 - b[0]) * rows, 16)
    send[...] = add_low(x[pl.ds(other, rows), :], r[pl.ds(other, rows), :])
    keep[...] = add_low(x[pl.ds(mine, rows), :], r[pl.ds(mine, rows), :])


def add_kernel(x, r, out):
    out[...] = add_low(x[...], r[...])


def join_kernel(b, x, r, out):
    rows = x.shape[0]
    out[pl.ds(pl.multiple_of(b[0] * rows, 16), rows), :] = x[...].astype(out.dtype)
    out[pl.ds(pl.multiple_of((1 - b[0]) * rows, 16), rows), :] = r[...].astype(out.dtype)


SCATTERS = 3


def chip_sum(keep, received, order, last):
    dims = [(axis, mask) for axis in order for mask in (1, 3)]
    bits = [half_kept(*dim) for dim in dims[:SCATTERS]]
    width = keep.shape[1]
    x, r = keep, received
    for n in range(SCATTERS):
        rows = x.shape[0] // 2
        x, send = call(split_kernel, (shape(rows, width), shape(rows, width)), bits[n], x, r, scalars=1)
        r = pair_swap(send, dims[n])
    for n in range(SCATTERS, len(dims)):
        x = call(add_kernel, shape(x.shape[0], width), x, r)
        r = pair_swap(x, dims[n])
    x = call(add_kernel, shape(x.shape[0], width), x, r)
    for n in reversed(range(SCATTERS)):
        r = pair_swap(x, dims[n])
        if n:
            x = call(join_kernel, shape(2 * x.shape[0], width), bits[n], x, r, scalars=1)
    return last(bits[0], x, r)


def plain_join(b, x, r):
    return call(join_kernel, shape(2 * x.shape[0], x.shape[1], F32), b, x, r, scalars=1)


def byte_join_kernel(b, x, r, key, value, rest):
    rows = x.shape[0]
    width = value.shape[1]
    for ref, at in ((x, b[0] * rows), (r, (1 - b[0]) * rows)):
        here = pl.ds(pl.multiple_of(at, 16), rows)
        key[here, :] = ref[:, :128].astype(F32)
        value[here, :] = ref[:, 128 : 128 + width].astype(F32)
        rest[here, :] = ref[:, 128 + width :]


def byte_join(b, x, r):
    rows = 2 * x.shape[0]
    return call(
        byte_join_kernel,
        (shape(rows, 128, F32), shape(rows, 640, F32), shape(rows, 128)),
        b, x, r, scalars=1,
    )


def out_join_kernel(b, x, r, weight, res):
    rows = x.shape[0]
    split = weight.shape[0]
    for n in range(2):
        lo = n * rows
        ours = jnp.where(b[0] == n, x[...].astype(F32), r[...].astype(F32))
        if n == 0:
            weight[:rows, :] = ours
        else:
            weight[rows:, :] = ours[: split - rows, :]
            res[...] = ours[split - rows :, :]


def out_join(b, x, r):
    rows = 2 * x.shape[0]
    return call(out_join_kernel, (shape(640, 1280, F32), shape(rows - 640, 1280, F32)), b, x, r, scalars=1)


def finish_kernel(rest, latn, lat_o, lat_x, gain, wq_o, wq_x, res, wq_grad, lat_grad, vecs):
    lats = latn.shape[0]
    half = lats // 2
    own_q = rest[:lats, :]
    oth_q = rest[lats : 2 * lats, :]
    wq_grad[...] = tn(latn[...], own_q)
    g = nt(own_q, wq_o[...]) + nt(oth_q, wq_x[...])
    gain_sum = 0.0
    bias_sum = 0.0
    for i, ref in enumerate((lat_o, lat_x)):
        grad = g[i * half : (i + 1) * half, :]
        u, inverse = norm(ref[...].astype(F32))
        gain_sum = gain_sum + column_sum(grad * u)
        bias_sum = bias_sum + column_sum(grad)
        if i == 0:
            lat_grad[...] = res[...] + norm_back(grad, u, inverse, gain[...])
    at = 2 * lats
    for n in range(4):
        for c in range(10):
            vecs[n : n + 1, c * 128 : (c + 1) * 128] = rest[at + c : at + c + 1, :].astype(F32)
        at += 10
    vecs[4:5, :] = gain_sum
    vecs[5:6, :] = bias_sum
    for c in range(10):
        vecs[6:7, c * 128 : (c + 1) * 128] = rest[at + c : at + c + 1, :].astype(F32)
    at += 10
    for n in range(2):
        for c in range(6):
            vecs[7 + n : 8 + n, c * 128 : (c + 1) * 128] = rest[at + c : at + c + 1, :].astype(F32)
        at += 6


def per_device(
    byte_input, item_lengths, latent_array, in_gain, in_bias, lat_gain, lat_bias, w_query,
    w_key, w_value, w_out, b_out, mlp_gain, mlp_bias, w_up, b_up, w_down, b_down, grad_out,
):
    side = lax.axis_index("tensor")
    packs, tok_rows, in_width = byte_input.shape
    lat_rows, width = latent_array.shape
    items = item_lengths.shape[1]
    lats, toks, rows = 2 * lat_rows, 2 * tok_rows, 2 * lat_rows * items

    def row(v):
        return v.reshape(1, -1)

    in_gain, in_bias, lat_gain, lat_bias = row(in_gain), row(in_bias), row(lat_gain), row(lat_bias)
    b_out, mlp_gain, mlp_bias, b_down = row(b_out), row(mlp_gain), row(mlp_bias), row(b_down)
    b_up = row(b_up)

    def mine(x):
        return lax.dynamic_index_in_dim(x, side, 0, keepdims=False)

    def others(x):
        return lax.dynamic_index_in_dim(x, 1 - side, 0, keepdims=False)

    lengths = mine(item_lengths)
    flip = (lengths[0] < lengths[1]).astype(jnp.int32)
    scalars = jnp.stack([flip, side.astype(jnp.int32)])

    byte_o = mine(byte_input)
    byte_x = core_swap(others(byte_input))
    wk_x = core_swap(w_key)
    wv_x = core_swap(w_value)
    lat_x = core_swap(latent_array)
    wq_x = core_swap(w_query)
    wo_x = core_swap(w_out)
    top = grad_out.reshape(packs, lat_rows * items, width)
    top_o = mine(top)
    top_x = core_swap(others(top))
    wu_x = core_swap(w_up)
    bu_x = core_swap(b_up)
    wd_x = core_swap(w_down)

    G = 1 << 30
    latn, q = call(
        latent_kernel, (shape(lats, width), shape(lats, 256)),
        latent_array, lat_x, lat_gain, lat_bias, w_query, wq_x, flops=G // 6,
    )
    raw, bn, k, v = call(
        bytes_kernel,
        (shape(toks, in_width), shape(toks, in_width), shape(toks, 256), shape(toks, width)),
        scalars, byte_o, byte_x, in_gain, in_bias, w_key, wk_x, w_value, wv_x,
        scalars=1, flops=G,
    )
    att = call(attend_kernel, shape(rows, width), q, k, v, flops=G // 2)
    hidden, mn = call(
        out_kernel, (shape(rows, width, F32), shape(rows, width)),
        att, w_out, wo_x, latent_array, lat_x, b_out, mlp_gain, mlp_bias, flops=2 * G,
    )
    gt = call(top_kernel, shape(rows, width), scalars, top_o, top_x, scalars=1)
    half = shape(rows, 640)
    act_o, act_x, gp_o, gp_x, bsum_o, bsum_x = call(
        up_kernel, (half, half, half, half, shape(1, 640, F32), shape(1, 640, F32)),
        mn, gt, w_up, wu_x, b_up, bu_x, w_down, wd_x, flops=4 * G,
    )
    wd_keep, wd_send = call(
        down_grad_kernel, (shape(640, width), shape(640, width)), act_o, act_x, gt, flops=2 * G
    )
    wd_got = core_swap(wd_send)
    wu_keep, wu_send = call(
        up_grad_kernel, (shape(width, 640), shape(width, 640)), mn, gp_o, gp_x, flops=2 * G
    )
    wu_got = core_swap(wu_send)
    ghl, res_o, res_x, vec = call(
        hidden_grad_kernel,
        (shape(rows, width), shape(lat_rows, width), shape(lat_rows, width), shape(4, width, F32)),
        gp_o, gp_x, w_up, wu_x, hidden, gt, mlp_gain, flops=2 * G,
        scratch=[pltpu.VMEM((rows, width), F32)],
    )
    wo_keep, wo_send = call(
        out_grad_kernel, (shape(768, width), shape(768, width)), att, ghl, res_o, res_x, flops=2 * G
    )
    wo_got = core_swap(wo_send)
    ga = call(attended_grad_kernel, shape(rows, width), ghl, w_out, wo_x, flops=2 * G)
    gq, gkv = call(
        attend_back_kernel, (shape(lats, 256), shape(toks, 2 * 768)), q, k, v, ga, flops=G
    )
    back_o, back_x, kv_keep, kv_send = call(
        byte_grad_kernel,
        (
            shape(tok_rows, in_width, F32), shape(tok_rows, in_width),
            shape(in_width, 896), shape(in_width, 896),
        ),
        scalars, gkv, w_key, w_value, wk_x, wv_x, raw, bn, in_gain, gq, vec, bsum_o, bsum_x,
        scalars=1, flops=2 * G, scratch=[pltpu.VMEM((toks, in_width), F32)],
    )
    kv_got = core_swap(kv_send)
    back_got = core_swap(back_x)
    enc_o, enc_x = call(
        encode_kernel, (shape(lat_rows * items, width), shape(lat_rows * items, width)),
        scalars, act_o, act_x, w_down, wd_x, hidden, b_down, scalars=1, flops=2 * G,
        scratch=[pltpu.VMEM((rows, width), BF16)],
    )
    enc_got = core_swap(enc_x)

    z, y, x = 0, 1, 2
    w_down_grad = chip_sum(wd_keep, wd_got, (x, y, z), plain_join)
    w_up_grad = chip_sum(wu_keep, wu_got, (y, z, x), plain_join)
    w_out_grad, res = chip_sum(wo_keep, wo_got, (z, x, y), out_join)
    w_key_grad, w_value_grad, rest = chip_sum(kv_keep, kv_got, (x, z, y), byte_join)
    w_query_grad, latent_grad, vecs = call(
        finish_kernel,
        (shape(width, 128, F32), shape(lat_rows, width, F32), shape(16, width, F32)),
        rest, latn, latent_array, lat_x, lat_gain, w_query, wq_x, res, flops=G // 3,
    )

    def both_packs(own, got):
        return jnp.where(side == 0, jnp.stack([own, got]), jnp.stack([got, own]))

    encoded = both_packs(enc_o, enc_got).reshape(packs, lat_rows, items, width)
    byte_grad = both_packs(back_o, back_got.astype(F32))
    return (
        encoded,
        byte_grad,
        latent_grad,
        vecs[7, :in_width],
        vecs[8, :in_width],
        vecs[4],
        vecs[5],
        w_query_grad,
        w_key_grad,
        w_value_grad,
        w_out_grad,
        vecs[3],
        vecs[1],
        vecs[2],
        w_up_grad,
        vecs[6, :640],
        w_down_grad,
        vecs[0],
    )


def solution(mesh):
    packs = P("dp", "tensor", None)
    columns = P(None, "tensor")
    lines = P("tensor", None)
    return jax.shard_map(
        per_device,
        mesh=mesh,
        in_specs=(
            packs, P("dp", None), lines, P(), P(), P(), P(), columns, columns, columns, lines,
            P(), P(), P(), columns, P("tensor"), lines, P(), P("dp", "tensor", None, None),
        ),
        out_specs=(
            P("dp", "tensor", None, None), packs, lines, P(), P(), P(), P(), columns, columns,
            columns, lines, P(), P(), P(), columns, P("tensor"), lines, P(),
        ),
        check_vma=False,
    )
```

```python
import jax
import jax.numpy as jnp
from jax import lax
from jax.experimental import pallas as pl
from jax.experimental.pallas import tpu as pltpu
from jax.sharding import PartitionSpec as P

F32 = jnp.float32
BF16 = jnp.bfloat16
EPS = 1e-05
HEAD_QK = 32
HEAD_V = 160
SCALE = HEAD_QK ** (-0.5)
MB = 1 << 20

SMEM = pl.BlockSpec(memory_space=pltpu.SMEM)
VMEM = pl.BlockSpec(memory_space=pltpu.VMEM)
HBM = pl.BlockSpec(memory_space=pltpu.HBM)


def shape(rows, columns, dtype=BF16):
    return jax.ShapeDtypeStruct((rows, columns), dtype)


def line(width):
    return jax.ShapeDtypeStruct((width,), F32)


def call(kernel, outs, *args, scalars=0, limit=12, scratch=(), after=(), far=(), place=None):
    if after:
        args = (*args[:-1], lax.optimization_barrier((args[-1], *after))[0])
    specs = [SMEM] * scalars + [HBM if n in far else VMEM for n in range(scalars, len(args))]
    return pl.pallas_call(
        kernel,
        out_shape=outs,
        in_specs=specs,
        out_specs=jax.tree.map(lambda _: VMEM, outs) if place is None else place,
        scratch_shapes=list(scratch),
        compiler_params=pltpu.CompilerParams(vmem_limit_bytes=limit * MB),
        cost_estimate=pl.CostEstimate(flops=0, bytes_accessed=0, transcendentals=0),
    )(*args)


def nn(a, b):
    return jnp.dot(a, b, preferred_element_type=F32)


def nt(a, b):
    return lax.dot_general(a, b, (((1,), (1,)), ((), ())), preferred_element_type=F32)


def tn(a, b):
    return lax.dot_general(a, b, (((0,), (0,)), ((), ())), preferred_element_type=F32)


def columns_of(o, x, lo, hi):
    width = o.shape[-1]
    if hi <= width:
        return o[:, lo:hi]
    if lo >= width:
        return x[:, lo - width : hi - width]
    return jnp.concatenate([o[:, lo:], x[:, : hi - width]], axis=1)


def rows_of(o, x, lo, hi):
    height = o.shape[0]
    if hi <= height:
        return o[lo:hi, :]
    if lo >= height:
        return x[lo - height : hi - height, :]
    return jnp.concatenate([o[lo:, :], x[: hi - height, :]], axis=0)


def store_columns(o, x, lo, hi, value):
    width = o.shape[-1]
    if hi <= width:
        o[:, lo:hi] = value
    elif lo >= width:
        x[:, lo - width : hi - width] = value
    else:
        o[:, lo:] = value[:, : width - lo]
        x[:, : hi - width] = value[:, width - lo :]


def norm(rows):
    average = jnp.mean(rows, axis=-1, keepdims=True)
    centered = rows - average
    variance = jnp.mean(centered * centered, axis=-1, keepdims=True)
    inverse = lax.rsqrt(variance + EPS)
    return centered * inverse, inverse


def norm_back(grad, normed, inverse, gain):
    scaled = grad * gain
    mean_term = jnp.mean(scaled, axis=-1, keepdims=True)
    cross_term = jnp.mean(scaled * normed, axis=-1, keepdims=True)
    return inverse * (scaled - mean_term - normed * cross_term)


def column_sum(x):
    return jnp.sum(x, axis=0, keepdims=True)


def flat(ref):
    return ref[...].reshape(1, -1)


def own_side():
    return lax.axis_index("tensor")


def long_second(lengths):
    side = own_side()
    return (lengths[side, 0] < lengths[side, 1]).astype(jnp.int32)


def send_kernel(byte_packs, top_packs, byte_s, top_s, sems):
    theirs = 1 - own_side()
    first = pltpu.make_async_copy(byte_packs.at[theirs], byte_s, sems.at[0])
    second = pltpu.make_async_copy(top_packs.at[theirs], top_s, sems.at[1])
    first.start()
    second.start()
    first.wait()
    second.wait()


def place_kernel(own, got, packs, wide, sems):
    mine = pltpu.make_async_copy(own, packs.at[own_side()], sems.at[0])
    mine.start()
    if wide is None:
        source = got
    else:
        wide[...] = got[...].astype(wide.dtype)
        source = wide
    theirs = pltpu.make_async_copy(source, packs.at[1 - own_side()], sems.at[1])
    theirs.start()
    mine.wait()
    theirs.wait()


def place(own, got, after):
    wide = own.dtype != got.dtype

    def body(own, got, packs, *rest):
        place_kernel(own, got, packs, rest[0] if wide else None, rest[-1])

    return call(
        body, jax.ShapeDtypeStruct((2, *own.shape), own.dtype), own, got,
        limit=4, after=after, place=pl.BlockSpec(memory_space=pl.ANY),
        scratch=([pltpu.VMEM(own.shape, own.dtype)] if wide else []) + [sems(2)],
    )


def load_all(sem, *pairs):
    copies = [pltpu.make_async_copy(*pair, sem.at[n]) for n, pair in enumerate(pairs)]
    for copy in copies:
        copy.start()
    return copies


def wait_all(copies):
    for copy in copies:
        copy.wait()


def rooms(*arrays):
    return [pltpu.VMEM(a.shape, a.dtype) for a in arrays] + [sems(len(arrays))]


def sems(count):
    return pltpu.SemaphoreType.DMA((count,))


def latent_kernel(
    far_o, far_x, far_gain, far_bias, far_wq_o, far_wq_x, latn, q,
    lat_o, lat_x, gain, bias, wq_o, wq_x, sem,
):
    loads = load_all(
        sem, (far_gain, gain), (far_bias, bias), (far_o, lat_o), (far_x, lat_x),
        (far_wq_o, wq_o), (far_wq_x, wq_x),
    )
    half = lat_o.shape[0]
    wait_all(loads[:3])
    for i, ref in enumerate((lat_o, lat_x)):
        if i == 1:
            loads[3].wait()
        u, _ = norm(ref[...].astype(F32))
        latn[i * half : (i + 1) * half, :] = (u * flat(gain) + flat(bias)).astype(BF16)
    wait_all(loads[4:])
    q[...] = nn(latn[...], columns_of(wq_o, wq_x, 0, q.shape[1])).astype(BF16)


def bytes_kernel(
    s, packs, far_oth, far_gain, far_bias, far_wk_o, far_wk_x, far_wv_o, far_wv_x, raw, bn, k, v,
    own, oth, gain, bias, wk_o, wk_x, wv_o, wv_x, sem,
):
    flip, side = long_second(s), own_side()
    loads = load_all(
        sem, (far_gain, gain), (far_bias, bias), (packs.at[side], own), (far_oth, oth),
        (far_wk_o, wk_o), (far_wk_x, wk_x), (far_wv_o, wv_o), (far_wv_x, wv_x),
    )
    wait_all(loads[:4])
    for b in range(4):
        a = (b + flip) & 3
        off = pl.multiple_of((a & 1) * 128, 128)
        mine = own[pl.ds(off, 128), :].astype(F32)
        other = oth[pl.ds(off, 128), :].astype(F32)
        rows = jnp.where((a >> 1) == side, mine, other)
        here = slice(b * 128, (b + 1) * 128)
        raw[here, :] = rows.astype(BF16)
        u, _ = norm(rows)
        bn[here, :] = (u * flat(gain) + flat(bias)).astype(BF16)
    x = bn[...]
    wait_all(loads[4:])
    k[...] = nn(x, columns_of(wk_o, wk_x, 0, k.shape[1])).astype(BF16)
    for lo in range(0, v.shape[1], 256):
        v[:, lo : lo + 256] = nn(x, columns_of(wv_o, wv_x, lo, lo + 256)).astype(BF16)


SEGMENTS = ((0, 384), (384, 512))


def join_heads(parts):
    rows = parts[0].shape[0]
    lane = lax.broadcasted_iota(jnp.int32, (rows, 128), 1)
    blocks = [parts[0][:, :128]]
    for c in range(1, 4):
        blocks.append(jnp.where(lane < 32 * c, parts[c - 1][:, 128:], parts[c][:, :128]))
    blocks.append(parts[3][:, 128:])
    return blocks


def attend_kernel(q, k, v, att):
    lats = q.shape[0]
    lane = lax.broadcasted_iota(jnp.int32, (lats, 128), 1)
    for g in range(2):
        qh = q[:, g * 128 : (g + 1) * 128]
        kh = k[:, g * 128 : (g + 1) * 128]
        outs = [[], []]
        for h in range(4):
            qm = jnp.where((lane >= 32 * h) & (lane < 32 * h + 32), qh.astype(F32), 0.0).astype(BF16)
            s = nt(qm, kh) * SCALE
            base = g * 640 + h * 128
            for i, (lo, hi) in enumerate(SEGMENTS):
                part = s[:, lo:hi]
                e = jnp.exp(part - jnp.max(part, axis=-1, keepdims=True))
                p = (e / jnp.sum(e, axis=-1, keepdims=True)).astype(BF16)
                outs[i].append(nn(p, v[lo:hi, base : base + 256]))
        for i in range(2):
            for c, block in enumerate(join_heads(outs[i])):
                at = g * 640 + c * 128
                att[i * lats : (i + 1) * lats, at : at + 128] = block.astype(BF16)


def out_kernel(att, wo_o, wo_x, lat_o, lat_x, b_out, gain, bias, hidden, mn):
    rows = lat_o.shape[0]
    width = hidden.shape[1]
    for lo in range(0, width, 256):
        weight = jnp.concatenate([wo_o[:, lo : lo + 256], wo_x[:, lo : lo + 256]], axis=0)
        hidden[:, lo : lo + 256] = nn(att[...], weight)
    for i in range(4):
        here = slice(i * rows, (i + 1) * rows)
        x = hidden[here, :] + (lat_x if i % 2 else lat_o)[...].astype(F32) + flat(b_out)
        hidden[here, :] = x
        u, _ = norm(x)
        mn[here, :] = (u * flat(gain) + flat(bias)).astype(BF16)


def top_kernel(s, packs, oth, gt, own, sem):
    flip = long_second(s)
    load = pltpu.make_async_copy(packs.at[own_side()], own, sem.at[0])
    load.start()
    half = own.shape[0]
    row = lax.broadcasted_iota(jnp.int32, (half, 2 * half), 0)
    column = lax.broadcasted_iota(jnp.int32, (half, 2 * half), 1)
    for j, ref in ((1, oth), (0, own)):
        if j == 0:
            load.wait()
        pairs = ref[...].reshape(2 * half, ref.shape[2])
        for i in range(2):
            chosen = jnp.where(column == 2 * row + (i ^ flip), 1.0, 0.0).astype(BF16)
            at = (2 * i + j) * half
            gt[at : at + half, :] = nn(chosen, pairs).astype(BF16)


def gelu_parts(x):
    cumulative = 0.5 * (1.0 + lax.erf(x * 0.7071067811865476))
    return x * cumulative, cumulative + x * (jnp.exp(-0.5 * x * x) * 0.3989422804014327)


def up_kernel(mn, gt, wu_o, wu_x, bu_o, bu_x, wd_o, wd_x, act, gp, bsum):
    bias = jnp.concatenate([flat(bu_o), flat(bu_x)], axis=1)
    for lo in range(0, act.shape[1], 256):
        hi = lo + 256
        pre = nn(mn[...], columns_of(wu_o, wu_x, lo, hi)) + bias[:, lo:hi]
        back = nt(gt[...], rows_of(wd_o, wd_x, lo, hi))
        active, slope = gelu_parts(pre)
        act[:, lo:hi] = active.astype(BF16)
        low = (back * slope).astype(BF16)
        gp[:, lo:hi] = low
        bsum[:, lo:hi] = column_sum(low.astype(F32))


def down_grad_kernel(act, gt, keep, send):
    half = keep.shape[0]
    send[...] = tn(act[:, half:], gt[...]).astype(BF16)
    keep[...] = tn(act[:, :half], gt[...]).astype(BF16)


def up_grad_kernel(mn, gp, keep, send):
    half = keep.shape[0]
    send[...] = tn(gp[:, half:], mn[...]).astype(BF16)
    keep[...] = tn(gp[:, :half], mn[...]).astype(BF16)


def encode_kernel(s, act, wd_o, wd_x, hidden, b_down, enc_o, enc_x, low):
    flip = long_second(s)
    for lo in range(0, low.shape[1], 256):
        hi = lo + 256
        weight = jnp.concatenate([wd_o[:, lo:hi], wd_x[:, lo:hi]], axis=0)
        out = nn(act[...], weight) + hidden[:, lo:hi] + flat(b_down)[:, lo:hi]
        low[:, lo:hi] = out.astype(BF16)
    half = enc_o.shape[0]
    row = lax.broadcasted_iota(jnp.int32, (2 * half, 2 * half), 0)
    column = lax.broadcasted_iota(jnp.int32, (2 * half, 2 * half), 1)
    item = (column // half) ^ flip
    chosen = jnp.where(row == 2 * (column % half) + item, 1.0, 0.0).astype(BF16)
    for j, ref in enumerate((enc_o, enc_x)):
        at = j * half
        both = jnp.concatenate([low[at : at + half, :], low[at + 2 * half : at + 3 * half, :]], axis=0)
        ref[...] = nn(chosen, both).astype(BF16).reshape(ref.shape)


def hidden_grad_kernel(gp, wu_o, wu_x, hidden, gt, gain, ghl, res_o, res_x, vec, g):
    for lo in range(0, g.shape[1], 256):
        weight = jnp.concatenate([wu_o[lo : lo + 256, :], wu_x[lo : lo + 256, :]], axis=1)
        g[:, lo : lo + 256] = nt(gp[...], weight)
    rows = res_o.shape[0]
    sums = [0.0, 0.0, 0.0, 0.0]
    res = [0.0, 0.0]
    for i in range(4):
        here = slice(i * rows, (i + 1) * rows)
        grad = g[here, :]
        top = gt[here, :].astype(F32)
        u, inverse = norm(hidden[here, :])
        total = top + norm_back(grad, u, inverse, flat(gain))
        ghl[here, :] = total.astype(BF16)
        res[i % 2] = res[i % 2] + total
        for n, x in enumerate((top, grad * u, grad, total)):
            sums[n] = sums[n] + column_sum(x)
    res_o[...] = res[0].astype(BF16)
    res_x[...] = res[1].astype(BF16)
    for n in range(4):
        vec[n : n + 1, :] = sums[n]


def out_grad_kernel(att, ghl, res_o, res_x, keep, send):
    half = att.shape[1] // 2
    keep[:half, :] = tn(att[:, :half], ghl[...]).astype(BF16)
    send[:half, :] = tn(att[:, half:], ghl[...]).astype(BF16)
    keep[half:, :] = res_o[...]
    send[half:, :] = res_x[...]


def attended_grad_kernel(ghl, wo_o, wo_x, ga):
    for lo in range(0, ga.shape[1], 256):
        ga[:, lo : lo + 256] = nt(ghl[...], rows_of(wo_o, wo_x, lo, lo + 256)).astype(BF16)


def attend_back_kernel(q, k, v, ga, gq, gkv):
    lats = q.shape[0]
    lane = lax.broadcasted_iota(jnp.int32, (lats, 128), 1)
    wide = lax.broadcasted_iota(jnp.int32, (lats, 256), 1)
    gq_rows = []
    for g in range(2):
        qh = q[:, g * 128 : (g + 1) * 128]
        kt = k[:, g * 128 : (g + 1) * 128].astype(F32).T.astype(BF16)
        for i, (lo, hi) in enumerate(SEGMENTS):
            kh = k[lo:hi, g * 128 : (g + 1) * 128]
            gk = None
            gv = []
            for h in range(4):
                inside = (lane >= 32 * h) & (lane < 32 * h + 32)
                qm = jnp.where(inside, qh.astype(F32), 0.0).astype(BF16)
                s = nt(kh, qm) * SCALE
                e = jnp.exp(s - jnp.max(s, axis=0, keepdims=True))
                p = e / jnp.sum(e, axis=0, keepdims=True)
                base = g * 640 + h * 128
                gw = ga[i * lats : (i + 1) * lats, base : base + 256]
                gm = jnp.where(
                    (wide >= 32 * h) & (wide < 32 * h + 160), gw.astype(F32), 0.0
                ).astype(BF16)
                gp = nt(v[lo:hi, base : base + 256], gm)
                gv.append(nn(p.astype(BF16), gw))
                inner = jnp.sum(p * gp, axis=0, keepdims=True)
                gs = (p * (gp - inner)).astype(BF16)
                part = nn(gs, qm)
                gk = part if gk is None else gk + part
                gq_rows.append(nn(kt[32 * h : 32 * h + 32, lo:hi], gs))
            at = g * 768
            gkv[lo:hi, at : at + 128] = (gk * SCALE).astype(BF16)
            for c, block in enumerate(join_heads(gv)):
                to = at + 128 + c * 128
                gkv[lo:hi, to : to + 128] = block.astype(BF16)
    rows = []
    for g in range(2):
        for h in range(4):
            rows.append(gq_rows[g * 8 + h] + gq_rows[g * 8 + 4 + h])
    gq[...] = (jnp.concatenate(rows, axis=0).T * SCALE).astype(BF16)


def block_at(i, c):
    n = 7 * i + c
    return n // 10, n % 10


def put(ref, i, c, value):
    band, at = block_at(i, c)
    ref[band * 128 : (band + 1) * 128, at * 128 : (at + 1) * 128] = value


def byte_grad_kernel(
    s, gkv, wk_o, wv_o, wk_x, wv_x, raw, bn, gain, gq, vec, bsum,
    back_o, back_x, keep, send, g,
):
    flip, side = long_second(s), own_side()
    g[...] = (
        nt(gkv[:, 0:128], wk_o[...])
        + nt(gkv[:, 128:768], wv_o[...])
        + nt(gkv[:, 768:896], wk_x[...])
        + nt(gkv[:, 896:1536], wv_x[...])
    )
    gain_sum = 0.0
    bias_sum = 0.0
    for b in range(4):
        here = slice(b * 128, (b + 1) * 128)
        grad = g[here, :]
        u, inverse = norm(raw[here, :].astype(F32))
        gain_sum = gain_sum + column_sum(grad * u)
        bias_sum = bias_sum + column_sum(grad)
        back = norm_back(grad, u, inverse, flat(gain))
        a = (b + flip) & 3
        off = pl.multiple_of((a & 1) * 128, 128)

        @pl.when((a >> 1) == side)
        def _():
            back_o[pl.ds(off, 128), :] = back

        @pl.when((a >> 1) != side)
        def _():
            back_x[pl.ds(off, 128), :] = back.astype(BF16)

    x = bn[...]
    width = gkv.shape[1] // 2
    for out, part in ((send, gkv[:, width:]), (keep, gkv[:, :width])):
        for c in range(0, width, 256):
            grad = tn(x, part[:, c : c + 256]).astype(BF16)
            for i in range(6):
                for n in range(2):
                    put(out, i, c // 128 + n, grad[i * 128 : (i + 1) * 128, n * 128 : (n + 1) * 128])
        out[512:, 256:] = jnp.zeros((128, out.shape[1] - 256), BF16)
    own_q, oth_q = gq[:, :128], gq[:, 128:]
    half = gq.shape[0] // 2
    for n, part in enumerate((own_q, oth_q)):
        put(keep, 2 * n, 6, part[:half, :])
        put(keep, 2 * n + 1, 6, part[half:, :])
    for n, part in enumerate((oth_q, own_q)):
        put(send, 2 * n, 6, part[half:, :])
        put(send, 2 * n + 1, 6, part[:half, :])
    both = [vec[n : n + 1, :] for n in range(4)]
    tail = [gain_sum, bias_sum]
    for ref, middle in (
        (keep, [bsum[:, :640], bsum[:, 640:]]),
        (send, [bsum[:, 640:], bsum[:, :640]]),
    ):
        lines = []
        for value in both + middle + tail:
            for c in range(value.shape[1] // 128):
                lines.append(value[:, c * 128 : (c + 1) * 128])
        lines += [jnp.zeros((1, 128), F32)] * (128 - len(lines))
        put(ref, 4, 6, jnp.concatenate(lines, axis=0).astype(BF16))
        put(ref, 5, 6, jnp.zeros((128, 128), BF16))


CHIPS = 4


def chip_axes(index):
    return (index // (CHIPS * CHIPS), (index // CHIPS) % CHIPS, index % CHIPS)


def partner_pairs(axis, mask):
    pairs = []
    for chip in range(CHIPS**3):
        for side in range(2):
            where = list(chip_axes(chip))
            where[axis] ^= mask ^ (2 * side)
            other = (where[0] * CHIPS + where[1]) * CHIPS + where[2]
            pairs.append((chip * 2 + side, other * 2 + side))
    return pairs


def half_kept(dim):
    axis, mask = dim
    chip = lax.axis_index("dp")
    place = (chip >> (4, 2, 0)[axis]) & 3
    low, high = (place ^ (place >> 1)) & 1, place >> 1
    first, second = (low, high) if mask == 1 else (high, low)
    return jnp.where(lax.axis_index("tensor") == 0, first, second)


def with_half(kernel, dim):
    return lambda *refs: kernel(half_kept(dim), *refs)


def pair_swap(x, dim):
    return lax.ppermute(x, ("dp", "tensor"), partner_pairs(*dim))


def core_swap(x):
    return lax.ppermute(x, "tensor", [(0, 1), (1, 0)])


def add_low(a, b):
    return (a.astype(F32) + b.astype(F32)).astype(BF16)


def halve_parts(b, parts, keep, send):
    for out, half in ((send, 1 - b), (keep, b)):
        to = 0
        for x, r, at, rows in parts:
            from_ = pl.ds(pl.multiple_of(at + half * (rows // 2), 16), rows // 2)
            out[to : to + rows // 2, :] = add_low(x[from_, :], r[from_, :])
            to += rows // 2


def add_kernel(x, r, out):
    out[...] = add_low(x[...], r[...])


def join_kernel(low, b, x, r, out):
    rows = x.shape[0] - low
    for ref, half in ((x, b), (r, 1 - b)):
        out[pl.ds(pl.multiple_of(half * rows, 16), rows), :] = ref[:rows, :]
        out[pl.ds(pl.multiple_of(2 * rows + half * low, 16), low), :] = ref[rows:, :]


def last_down_kernel(b, x, r, out):
    rows = out.shape[0] // 2
    out[pl.ds(pl.multiple_of(b * rows, 16), rows), :] = x[:rows, :].astype(F32)
    out[pl.ds(pl.multiple_of((1 - b) * rows, 16), rows), :] = r[:rows, :].astype(F32)


def last_up_kernel(b, x, r, out):
    rows = out.shape[1] // 2
    for n in range(2):
        ours = jnp.where(b == n, x[:rows, :].astype(F32), r[:rows, :].astype(F32))
        out[:, n * rows : (n + 1) * rows] = ours.T


def last_out_kernel(b, x, r, weight, res):
    split = weight.shape[0]
    rows = (split + res.shape[0]) // 2
    for n in range(2):
        ours = jnp.where(b == n, x[:rows, :].astype(F32), r[:rows, :].astype(F32))
        if n == 0:
            weight[:rows, :] = ours
        else:
            weight[rows:, :] = ours[: split - rows, :]
            res[...] = ours[split - rows :, :]


def last_keys_kernel(lows, halves, *refs):
    *groups, key, value, rest = refs
    bands = []
    for n, b in enumerate(halves):
        x, r = groups[2 * n : 2 * n + 2]
        xs, rs = x[x.shape[0] - lows[n] :, :], r[r.shape[0] - lows[n] :, :]
        pair = [jnp.where(b == h, xs.astype(F32), rs.astype(F32)) for h in range(2)]
        bands += pair if lows[n] == 128 else [jnp.concatenate(pair, axis=0)]
    for i in range(6):
        here = slice(i * 128, (i + 1) * 128)
        for c in range(7):
            band, at = block_at(i, c)
            block = bands[band][:, at * 128 : (at + 1) * 128]
            if c == 0:
                key[here, :] = block
            elif c < 6:
                value[here, (c - 1) * 128 : c * 128] = block
            else:
                rest[here, :] = block.astype(BF16)


class Group:
    def __init__(self, order, band, bands):
        self.dims = [(axis, mask) for axis in order for mask in (1, 3)]
        self.band, self.low = band, bands

    def first(self, x, r, keys, keys_r, after):
        rows, width, low, band = x.shape[0], x.shape[1], self.low, self.band

        def kernel(x, r, kx, kr, keep, send):
            parts = ((x, r, 0, rows), (kx, kr, band, low))
            halve_parts(half_kept(self.dims[0]), parts, keep, send)

        half = shape((rows + low) // 2, width)
        self.x, sent = call(kernel, (half, half), x, r, keys, keys_r, limit=4, after=after)
        self.low = low // 2
        self.r = pair_swap(sent, self.dims[0])
        return sent

    def halve(self, n, after):
        rows, low = self.x.shape[0] - self.low, self.low

        def kernel(x, r, keep, send):
            parts = ((x, r, 0, rows), (x, r, rows, low))
            halve_parts(half_kept(self.dims[n]), parts, keep, send)

        half = shape((rows + low) // 2, self.x.shape[1])
        self.x, sent = call(kernel, (half, half), self.x, self.r, limit=4, after=after)
        self.low = low // 2
        self.r = pair_swap(sent, self.dims[n])
        return sent

    def double(self, n, after):
        self.x = call(add_kernel, shape(*self.x.shape), self.x, self.r, limit=4, after=after)
        self.r = pair_swap(self.x, self.dims[n])
        return self.x

    def gather(self, n, after):
        rows, width = self.x.shape
        low = self.low

        def kernel(*refs):
            join_kernel(low, half_kept(self.dims[n + 1]), *refs)

        self.x = call(kernel, shape(2 * rows, width), self.x, self.r, limit=4, after=after)
        self.low = 2 * low
        self.r = pair_swap(self.x, self.dims[n])
        return self.x

    def end(self, kernel, outs, after):
        return call(with_half(kernel, self.dims[0]), outs, self.x, self.r, limit=8, after=after)


def finish_kernel(
    rest, latn, lat_o, lat_x, gain, wq_o, wq_x, res,
    wq_grad, lat_grad, lat_gain, lat_bias, b_down, mlp_gain, mlp_bias, b_out, b_up, in_gain, in_bias,
):
    lats = latn.shape[0]
    half = lats // 2
    own_q = rest[:lats, :]
    both_q = jnp.concatenate([own_q, rest[lats : 2 * lats, :]], axis=1)
    wq_grad[...] = tn(latn[...], own_q)
    g = nt(both_q, columns_of(wq_o, wq_x, 0, both_q.shape[1]))
    gain_sum = 0.0
    bias_sum = 0.0
    for i, ref in enumerate((lat_o, lat_x)):
        grad = g[i * half : (i + 1) * half, :]
        u, inverse = norm(ref[...].astype(F32))
        gain_sum = gain_sum + column_sum(grad * u)
        bias_sum = bias_sum + column_sum(grad)
        if i == 0:
            lat_grad[...] = res[...] + norm_back(grad, u, inverse, flat(gain))
    lat_gain[...] = gain_sum.reshape(lat_gain.shape)
    lat_bias[...] = bias_sum.reshape(lat_bias.shape)
    at = 2 * lats
    lines = rest[at : at + 64, :].astype(F32)
    at = 0
    for ref, count in (
        (b_down, 10), (mlp_gain, 10), (mlp_bias, 10), (b_out, 10), (b_up, 5), (None, 5),
        (in_gain, 6), (in_bias, 6),
    ):
        if ref is not None:
            parts = [lines[at + c : at + c + 1, :] for c in range(count)]
            ref[...] = jnp.concatenate(parts, axis=1).reshape(ref.shape)
        at += count


def per_device(
    byte_input, item_lengths, latent_array, in_gain, in_bias, lat_gain, lat_bias, w_query,
    w_key, w_value, w_out, b_out, mlp_gain, mlp_bias, w_up, b_up, w_down, b_down, grad_out,
):
    side = lax.axis_index("tensor")
    packs, tok_rows, in_width = byte_input.shape
    lat_rows, width = latent_array.shape
    items = item_lengths.shape[1]
    lats, toks, rows = 2 * lat_rows, 2 * tok_rows, 2 * lat_rows * items

    byte_s, top_s = call(
        send_kernel,
        (
            jax.ShapeDtypeStruct((tok_rows, in_width), BF16),
            jax.ShapeDtypeStruct((lat_rows, items, width), BF16),
        ),
        byte_input, grad_out, limit=56, far=(0, 1), scratch=[sems(2)],
    )
    byte_x = core_swap(byte_s)

    def swap_after(x, *first):
        return core_swap(lax.optimization_barrier((x, *first))[0])

    wk_x = swap_after(w_key, byte_s)
    wv_x = swap_after(w_value, byte_s)
    lat_x = swap_after(latent_array, byte_s)
    wq_x = swap_after(w_query, byte_s)
    early = (byte_x, wk_x, wv_x, lat_x, wq_x)
    wo_x = swap_after(w_out, *early)
    top_x = swap_after(top_s, *early)
    wu_x = swap_after(w_up, *early)
    bu_x = swap_after(b_up, *early)
    wd_x = swap_after(w_down, *early)

    operands = (latent_array, lat_x, lat_gain, lat_bias, w_query, wq_x)
    latn, q = call(
        latent_kernel, (shape(lats, width), shape(lats, 256)), *operands, far=range(6),
        scratch=rooms(*operands), limit=52,
    )
    operands = (byte_x, in_gain, in_bias, w_key, wk_x, w_value, wv_x)
    raw, bn, k, v = call(
        bytes_kernel,
        (shape(toks, in_width), shape(toks, in_width), shape(toks, 256), shape(toks, width)),
        item_lengths, byte_input, *operands, scalars=1, far=range(1, 9),
        scratch=rooms(byte_x, *operands), limit=52,
    )
    gt = call(
        top_kernel, shape(rows, width), item_lengths, grad_out, top_x, scalars=1, far=(1,),
        scratch=[pltpu.VMEM((lat_rows, items, width), BF16), sems(1)],
    )
    att = call(attend_kernel, shape(rows, width), q, k, v)
    hidden, mn = call(
        out_kernel, (shape(rows, width, F32), shape(rows, width)),
        att, w_out, wo_x, latent_array, lat_x, b_out, mlp_gain, mlp_bias,
    )
    act, gp, bsum = call(
        up_kernel, (shape(rows, width), shape(rows, width), shape(1, width, F32)),
        mn, gt, w_up, wu_x, b_up, bu_x, w_down, wd_x,
    )

    z, y, x = 0, 1, 2
    out, down, up = groups = (
        Group((z, x, y), 0, 128), Group((x, y, z), 128, 256), Group((y, z, x), 384, 256)
    )
    matrix = shape(640, width)
    keep, send = call(down_grad_kernel, (matrix, matrix), act, gt)
    d = (keep, core_swap(send))
    keep, send = call(up_grad_kernel, (matrix, matrix), mn, gp, after=(send,))
    u = (keep, core_swap(send))
    ghl, res_o, res_x, vec = call(
        hidden_grad_kernel,
        (shape(rows, width), shape(lat_rows, width), shape(lat_rows, width), shape(4, width, F32)),
        gp, w_up, wu_x, hidden, gt, mlp_gain,
        scratch=[pltpu.VMEM((rows, width), F32)], after=(send,),
    )
    keep, send = call(
        out_grad_kernel, (shape(768, width), shape(768, width)), att, ghl, res_o, res_x,
        after=(vec, d[1], u[1]),
    )
    o = (keep, core_swap(send))
    ga = call(attended_grad_kernel, shape(rows, width), ghl, w_out, wo_x, after=(send,))
    gq, gkv = call(
        attend_back_kernel, (shape(lats, 256), shape(toks, 2 * 768)), q, k, v, ga, after=(ga,)
    )
    back, back_s, keep, send = call(
        byte_grad_kernel,
        (shape(tok_rows, in_width, F32), shape(tok_rows, in_width), matrix, matrix),
        item_lengths, gkv, w_key, w_value, wk_x, wv_x, raw, bn, in_gain, gq, vec, bsum,
        scalars=1, scratch=[pltpu.VMEM((toks, in_width), F32)], after=(gq, o[1]),
    )
    keys = (keep, core_swap(send))
    back_x = core_swap(back_s)
    enc, enc_s = call(
        encode_kernel,
        tuple(jax.ShapeDtypeStruct((lat_rows, items, width), BF16) for _ in range(2)),
        item_lengths, act, w_down, wd_x, hidden, b_down, scalars=1,
        scratch=[pltpu.VMEM((rows, width), BF16)], after=(send,),
    )
    enc_x = core_swap(enc_s)
    last = enc_s
    for group, main in zip(groups, (o, d, u)):
        last = group.first(*main, *keys, (last,))
    byte_grad = place(back, back_x, (last,))
    encoded = last = place(enc, enc_x, (byte_grad,))
    for n in (1, 2):
        for group in groups:
            last = group.halve(n, (last,))
    for n in (3, 4, 5):
        for group in groups:
            last = group.double(n, (last,))
    for group in groups:
        group.x = last = call(
            add_kernel, shape(*group.x.shape), group.x, group.r, limit=4, after=(last,)
        )
        group.r = pair_swap(group.x, group.dims[2])
    for n in (1, 0):
        for group in groups:
            last = group.gather(n, (last,))
    w_out_grad, res = out.end(
        last_out_kernel, (shape(640, width, F32), shape(lat_rows, width, F32)), (last,)
    )
    w_down_grad = down.end(last_down_kernel, shape(640, width, F32), (res,))
    w_up_grad = up.end(last_up_kernel, shape(width, 640, F32), (w_down_grad,))

    def keys_kernel(*refs):
        halves = [half_kept(group.dims[0]) for group in groups]
        last_keys_kernel([group.low for group in groups], halves, *refs)

    w_key_grad, w_value_grad, rest = call(
        keys_kernel,
        (shape(in_width, 128, F32), shape(in_width, 640, F32), shape(in_width, 128)),
        *(a for group in groups for a in (group.x, group.r)), limit=8, after=(w_up_grad,),
    )
    (
        w_query_grad, latent_grad, lat_gain_grad, lat_bias_grad, b_down_grad, mlp_gain_grad,
        mlp_bias_grad, b_out_grad, b_up_grad, in_gain_grad, in_bias_grad,
    ) = call(
        finish_kernel,
        (
            shape(width, 128, F32), shape(lat_rows, width, F32), *(line(width) for _ in range(6)),
            line(640), line(in_width), line(in_width),
        ),
        rest, latn, latent_array, lat_x, lat_gain, w_query, wq_x, res,
    )
    return (
        encoded,
        byte_grad,
        latent_grad,
        in_gain_grad,
        in_bias_grad,
        lat_gain_grad,
        lat_bias_grad,
        w_query_grad,
        w_key_grad,
        w_value_grad,
        w_out_grad,
        b_out_grad,
        mlp_gain_grad,
        mlp_bias_grad,
        w_up_grad,
        b_up_grad,
        w_down_grad,
        b_down_grad,
    )


def solution(mesh):
    packs = P("dp", "tensor", None)
    columns = P(None, "tensor")
    lines = P("tensor", None)
    return jax.shard_map(
        per_device,
        mesh=mesh,
        in_specs=(
            packs, P("dp", None), lines, P(), P(), P(), P(), columns, columns, columns, lines,
            P(), P(), P(), columns, P("tensor"), lines, P(), P("dp", "tensor", None, None),
        ),
        out_specs=(
            P("dp", "tensor", None, None), packs, lines, P(), P(), P(), P(), columns, columns,
            columns, lines, P(), P(), P(), columns, P("tensor"), lines, P(),
        ),
        check_vma=False,
    )
```

```python
import jax
import jax.numpy as jnp
from jax import lax
from jax.experimental import pallas as pl
from jax.experimental.pallas import tpu as pltpu
from jax.sharding import PartitionSpec as P

F32 = jnp.float32
BF16 = jnp.bfloat16
EPS = 1e-05
HEAD_QK = 32
HEAD_V = 160
SCALE = HEAD_QK ** (-0.5)
MB = 1 << 20

SMEM = pl.BlockSpec(memory_space=pltpu.SMEM)
VMEM = pl.BlockSpec(memory_space=pltpu.VMEM)
HBM = pl.BlockSpec(memory_space=pltpu.HBM)


def shape(rows, columns, dtype=BF16):
    return jax.ShapeDtypeStruct((rows, columns), dtype)


def line(width):
    return jax.ShapeDtypeStruct((width,), F32)


def call(kernel, outs, *args, scalars=0, limit=12, scratch=(), after=(), far=(), place=None):
    if after:
        args = (*args[:-1], lax.optimization_barrier((args[-1], *after))[0])
    specs = [SMEM] * scalars + [HBM if n in far else VMEM for n in range(scalars, len(args))]
    return pl.pallas_call(
        kernel,
        out_shape=outs,
        in_specs=specs,
        out_specs=jax.tree.map(lambda _: VMEM, outs) if place is None else place,
        scratch_shapes=list(scratch),
        compiler_params=pltpu.CompilerParams(vmem_limit_bytes=limit * MB),
        cost_estimate=pl.CostEstimate(flops=0, bytes_accessed=0, transcendentals=0),
    )(*args)


def nn(a, b):
    return jnp.dot(a, b, preferred_element_type=F32)


def nt(a, b):
    return lax.dot_general(a, b, (((1,), (1,)), ((), ())), preferred_element_type=F32)


def tn(a, b):
    return lax.dot_general(a, b, (((0,), (0,)), ((), ())), preferred_element_type=F32)


def columns_of(o, x, lo, hi):
    width = o.shape[-1]
    if hi <= width:
        return o[:, lo:hi]
    if lo >= width:
        return x[:, lo - width : hi - width]
    return jnp.concatenate([o[:, lo:], x[:, : hi - width]], axis=1)


def rows_of(o, x, lo, hi):
    height = o.shape[0]
    if hi <= height:
        return o[lo:hi, :]
    if lo >= height:
        return x[lo - height : hi - height, :]
    return jnp.concatenate([o[lo:, :], x[: hi - height, :]], axis=0)


def store_columns(o, x, lo, hi, value):
    width = o.shape[-1]
    if hi <= width:
        o[:, lo:hi] = value
    elif lo >= width:
        x[:, lo - width : hi - width] = value
    else:
        o[:, lo:] = value[:, : width - lo]
        x[:, : hi - width] = value[:, width - lo :]


def norm(rows):
    average = jnp.mean(rows, axis=-1, keepdims=True)
    centered = rows - average
    variance = jnp.mean(centered * centered, axis=-1, keepdims=True)
    inverse = lax.rsqrt(variance + EPS)
    return centered * inverse, inverse


def norm_back(grad, normed, inverse, gain):
    scaled = grad * gain
    mean_term = jnp.mean(scaled, axis=-1, keepdims=True)
    cross_term = jnp.mean(scaled * normed, axis=-1, keepdims=True)
    return inverse * (scaled - mean_term - normed * cross_term)


def column_sum(x):
    return jnp.sum(x, axis=0, keepdims=True)


def flat(ref):
    return ref[...].reshape(1, -1)


def own_side():
    return lax.axis_index("tensor")


def long_second(lengths):
    side = own_side()
    return (lengths[side, 0] < lengths[side, 1]).astype(jnp.int32)


def place_kernel(own, got, packs, wide, sems):
    mine = pltpu.make_async_copy(own, packs.at[own_side()], sems.at[0])
    mine.start()
    if wide is None:
        source = got
    else:
        wide[...] = got[...].astype(wide.dtype)
        source = wide
    theirs = pltpu.make_async_copy(source, packs.at[1 - own_side()], sems.at[1])
    theirs.start()
    mine.wait()
    theirs.wait()


def place(own, got, after):
    wide = own.dtype != got.dtype

    def body(own, got, packs, *rest):
        place_kernel(own, got, packs, rest[0] if wide else None, rest[-1])

    return call(
        body, jax.ShapeDtypeStruct((2, *own.shape), own.dtype), own, got,
        limit=4, after=after, place=pl.BlockSpec(memory_space=pl.ANY),
        scratch=([pltpu.VMEM(own.shape, own.dtype)] if wide else []) + [sems(2)],
    )


def load_all(sem, *pairs):
    copies = [pltpu.make_async_copy(*pair, sem.at[n]) for n, pair in enumerate(pairs)]
    for copy in copies:
        copy.start()
    return copies


def wait_all(copies):
    for copy in copies:
        copy.wait()


def rooms(*arrays):
    return [pltpu.VMEM(a.shape, a.dtype) for a in arrays] + [sems(len(arrays))]


def sems(count):
    return pltpu.SemaphoreType.DMA((count,))


def latent_kernel(
    far_o, far_x, far_gain, far_bias, far_wq_o, far_wq_x, latn, q,
    lat_o, lat_x, gain, bias, wq_o, wq_x, sem,
):
    loads = load_all(
        sem, (far_gain, gain), (far_bias, bias), (far_o, lat_o), (far_x, lat_x),
        (far_wq_o, wq_o), (far_wq_x, wq_x),
    )
    half = lat_o.shape[0]
    wait_all(loads[:3])
    for i, ref in enumerate((lat_o, lat_x)):
        if i == 1:
            loads[3].wait()
        u, _ = norm(ref[...].astype(F32))
        latn[i * half : (i + 1) * half, :] = (u * flat(gain) + flat(bias)).astype(BF16)
    wait_all(loads[4:])
    q[...] = nn(latn[...], columns_of(wq_o, wq_x, 0, q.shape[1])).astype(BF16)


def bytes_kernel(
    s, packs, far_oth, far_gain, far_bias, far_wk_o, far_wk_x, far_wv_o, far_wv_x, raw, bn, k, v,
    own, oth, gain, bias, wk_o, wk_x, wv_o, wv_x, sem,
):
    flip, side = long_second(s), own_side()
    loads = load_all(
        sem, (far_gain, gain), (far_bias, bias), (packs.at[side], own), (far_oth.at[side], oth),
        (far_wk_o, wk_o), (far_wk_x, wk_x), (far_wv_o, wv_o), (far_wv_x, wv_x),
    )
    wait_all(loads[:4])
    for b in range(4):
        a = (b + flip) & 3
        off = pl.multiple_of((a & 1) * 128, 128)
        mine = own[pl.ds(off, 128), :].astype(F32)
        other = oth[pl.ds(off, 128), :].astype(F32)
        rows = jnp.where((a >> 1) == side, mine, other)
        here = slice(b * 128, (b + 1) * 128)
        raw[here, :] = rows.astype(BF16)
        u, _ = norm(rows)
        bn[here, :] = (u * flat(gain) + flat(bias)).astype(BF16)
    x = bn[...]
    wait_all(loads[4:])
    k[...] = nn(x, columns_of(wk_o, wk_x, 0, k.shape[1])).astype(BF16)
    for lo in range(0, v.shape[1], 256):
        v[:, lo : lo + 256] = nn(x, columns_of(wv_o, wv_x, lo, lo + 256)).astype(BF16)


SEGMENTS = ((0, 384), (384, 512))


def join_heads(parts):
    rows = parts[0].shape[0]
    lane = lax.broadcasted_iota(jnp.int32, (rows, 128), 1)
    blocks = [parts[0][:, :128]]
    for c in range(1, 4):
        blocks.append(jnp.where(lane < 32 * c, parts[c - 1][:, 128:], parts[c][:, :128]))
    blocks.append(parts[3][:, 128:])
    return blocks


def attend_kernel(q, k, v, att):
    lats = q.shape[0]
    lane = lax.broadcasted_iota(jnp.int32, (lats, 128), 1)

    def scores(g, h):
        of_group = slice(g * 128, (g + 1) * 128)
        inside = (lane >= 32 * h) & (lane < 32 * h + 32)
        masked = jnp.where(inside, q[:, of_group].astype(F32), 0.0).astype(BF16)
        return nt(masked, k[:, of_group])

    heads = [(g, h) for g in range(2) for h in range(4)]
    following = scores(*heads[0])
    outs = [[], []]
    for n, (g, h) in enumerate(heads):
        s = following
        if n + 1 < len(heads):
            following = scores(*heads[n + 1])
        base = g * 640 + h * 128
        for i, (lo, hi) in enumerate(SEGMENTS):
            part = s[:, lo:hi]
            e = jnp.exp((part - jnp.max(part, axis=-1, keepdims=True)) * SCALE)
            total = jnp.sum(e, axis=-1, keepdims=True)
            outs[i].append(nn(e.astype(BF16), v[lo:hi, base : base + 256]) * (1.0 / total))
        if h == 3:
            for i in range(2):
                for c, block in enumerate(join_heads(outs[i])):
                    at = g * 640 + c * 128
                    att[i * lats : (i + 1) * lats, at : at + 128] = block.astype(BF16)
            outs = [[], []]


def out_kernel(att, wo_o, wo_x, lat_o, lat_x, b_out, gain, bias, hidden, mn):
    rows = lat_o.shape[0]

    def product(half):
        here = slice(half * 2 * rows, (half + 1) * 2 * rows)
        for lo in range(0, hidden.shape[1], 256):
            weight = jnp.concatenate([wo_o[:, lo : lo + 256], wo_x[:, lo : lo + 256]], axis=0)
            hidden[here, lo : lo + 256] = nn(att[here, :], weight)

    product(0)
    product(1)
    for i in range(4):
        here = slice(i * rows, (i + 1) * rows)
        x = hidden[here, :] + (lat_x if i % 2 else lat_o)[...].astype(F32) + flat(b_out)
        hidden[here, :] = x
        u, _ = norm(x)
        mn[here, :] = (u * flat(gain) + flat(bias)).astype(BF16)


def top_kernel(s, packs, far_oth, gt, own, oth, sem):
    flip, side = long_second(s), own_side()
    loads = load_all(sem, (packs.at[side], own), (far_oth.at[side], oth))
    half = own.shape[0]
    row = lax.broadcasted_iota(jnp.int32, (half, 2 * half), 0)
    column = lax.broadcasted_iota(jnp.int32, (half, 2 * half), 1)
    for j, ref in enumerate((own, oth)):
        loads[j].wait()
        pairs = ref[...].reshape(2 * half, ref.shape[2])
        for i in range(2):
            chosen = jnp.where(column == 2 * row + (i ^ flip), 1.0, 0.0).astype(BF16)
            at = (2 * i + j) * half
            gt[at : at + half, :] = nn(chosen, pairs).astype(BF16)


def gelu_parts(x):
    cumulative = 0.5 * (1.0 + lax.erf(x * 0.7071067811865476))
    return x * cumulative, cumulative + x * (jnp.exp(-0.5 * x * x) * 0.3989422804014327)


def up_kernel(mn, gt, wu_o, wu_x, bu_o, bu_x, wd_o, wd_x, act, gp, bsum):
    bias = jnp.concatenate([flat(bu_o), flat(bu_x)], axis=1)
    for lo in range(0, act.shape[1], 256):
        hi = lo + 256
        pre = nn(mn[...], columns_of(wu_o, wu_x, lo, hi)) + bias[:, lo:hi]
        back = nt(gt[...], rows_of(wd_o, wd_x, lo, hi))
        active, slope = gelu_parts(pre)
        act[:, lo:hi] = active.astype(BF16)
        low = (back * slope).astype(BF16)
        gp[:, lo:hi] = low
        bsum[:, lo:hi] = column_sum(low.astype(F32))


def down_grad_kernel(act, gt, keep, send):
    half = keep.shape[0]
    send[...] = tn(act[:, half:], gt[...]).astype(BF16)
    keep[...] = tn(act[:, :half], gt[...]).astype(BF16)


def up_grad_kernel(mn, gp, keep, send):
    half = keep.shape[0]
    send[...] = tn(gp[:, half:], mn[...]).astype(BF16)
    keep[...] = tn(gp[:, :half], mn[...]).astype(BF16)


def encode_kernel(s, act, wd_o, wd_x, hidden, b_down, enc_o, enc_x, low):
    flip = long_second(s)
    for lo in range(0, low.shape[1], 256):
        hi = lo + 256
        weight = jnp.concatenate([wd_o[:, lo:hi], wd_x[:, lo:hi]], axis=0)
        out = nn(act[...], weight) + hidden[:, lo:hi] + flat(b_down)[:, lo:hi]
        low[:, lo:hi] = out.astype(BF16)
    half = enc_o.shape[0]
    row = lax.broadcasted_iota(jnp.int32, (2 * half, 2 * half), 0)
    column = lax.broadcasted_iota(jnp.int32, (2 * half, 2 * half), 1)
    item = (column // half) ^ flip
    chosen = jnp.where(row == 2 * (column % half) + item, 1.0, 0.0).astype(BF16)
    for j, ref in enumerate((enc_o, enc_x)):
        at = j * half
        both = jnp.concatenate([low[at : at + half, :], low[at + 2 * half : at + 3 * half, :]], axis=0)
        ref[...] = nn(chosen, both).astype(BF16).reshape(ref.shape)


def hidden_grad_kernel(gp, wu_o, wu_x, hidden, gt, gain, ghl, res_o, res_x, vec, g):
    rows = res_o.shape[0]

    def product(half):
        here = slice(half * 2 * rows, (half + 1) * 2 * rows)
        for lo in range(0, g.shape[1], 256):
            weight = jnp.concatenate([wu_o[lo : lo + 256, :], wu_x[lo : lo + 256, :]], axis=1)
            g[here, lo : lo + 256] = nt(gp[here, :], weight)

    product(0)
    product(1)
    sums = [0.0, 0.0, 0.0, 0.0]
    res = [0.0, 0.0]
    for i in range(4):
        here = slice(i * rows, (i + 1) * rows)
        grad = g[here, :]
        top = gt[here, :].astype(F32)
        u, inverse = norm(hidden[here, :])
        total = top + norm_back(grad, u, inverse, flat(gain))
        ghl[here, :] = total.astype(BF16)
        res[i % 2] = res[i % 2] + total
        for n, x in enumerate((top, grad * u, grad, total)):
            sums[n] = sums[n] + column_sum(x)
    res_o[...] = res[0].astype(BF16)
    res_x[...] = res[1].astype(BF16)
    for n in range(4):
        vec[n : n + 1, :] = sums[n]


def out_grad_kernel(att, ghl, res_o, res_x, keep, send):
    half = att.shape[1] // 2
    keep[:half, :] = tn(att[:, :half], ghl[...]).astype(BF16)
    send[:half, :] = tn(att[:, half:], ghl[...]).astype(BF16)
    keep[half:, :] = res_o[...]
    send[half:, :] = res_x[...]


def attended_grad_kernel(ghl, wo_o, wo_x, ga):
    for lo in range(0, ga.shape[1], 256):
        ga[:, lo : lo + 256] = nt(ghl[...], rows_of(wo_o, wo_x, lo, lo + 256)).astype(BF16)


def attend_back_kernel(q, k, v, ga, gq, gkv):
    lats = q.shape[0]
    lane = lax.broadcasted_iota(jnp.int32, (lats, 128), 1)
    wide = lax.broadcasted_iota(jnp.int32, (lats, 256), 1)
    groups = [slice(g * 128, (g + 1) * 128) for g in range(2)]
    masked = [
        [
            jnp.where((lane >= 32 * h) & (lane < 32 * h + 32), q[:, of].astype(F32), 0.0).astype(BF16)
            for h in range(4)
        ]
        for of in groups
    ]
    turned = [k[:, of].astype(F32).T.astype(BF16) for of in groups]
    order = [(g, i, h) for g in range(2) for i in range(2) for h in range(4)]

    def begin(g, i, h):
        lo, hi = SEGMENTS[i]
        base = g * 640 + h * 128
        gw = ga[i * lats : (i + 1) * lats, base : base + 256]
        inside = (wide >= 32 * h) & (wide < 32 * h + 160)
        gm = jnp.where(inside, gw.astype(F32), 0.0).astype(BF16)
        return nt(k[lo:hi, groups[g]], masked[g][h]), nt(v[lo:hi, base : base + 256], gm), gw

    ahead = [begin(*order[n]) for n in range(2)]
    gq_rows = {}
    gv = []
    gk = None
    for n, (g, i, h) in enumerate(order):
        lo, hi = SEGMENTS[i]
        s, gp, gw = ahead.pop(0)
        if n + 2 < len(order):
            ahead.append(begin(*order[n + 2]))
        e = jnp.exp((s - jnp.max(s, axis=0, keepdims=True)) * SCALE)
        p = e * (1.0 / jnp.sum(e, axis=0, keepdims=True))
        pg = p * gp
        gs = (pg - p * jnp.sum(pg, axis=0, keepdims=True)).astype(BF16)
        gv.append(nn(p.astype(BF16), gw))
        part = nn(gs, masked[g][h])
        gk = part if h == 0 else gk + part
        row = nn(turned[g][32 * h : 32 * h + 32, lo:hi], gs)
        gq_rows[g, h] = row if i == 0 else gq_rows[g, h] + row
        if h == 3:
            at = g * 768
            gkv[lo:hi, at : at + 128] = (gk * SCALE).astype(BF16)
            for c, block in enumerate(join_heads(gv)):
                to = at + 128 + c * 128
                gkv[lo:hi, to : to + 128] = block.astype(BF16)
            gv = []
    rows = [gq_rows[g, h] for g in range(2) for h in range(4)]
    gq[...] = (jnp.concatenate(rows, axis=0).T * SCALE).astype(BF16)


def block_at(i, c):
    n = i if c == 6 else 6 + 6 * i + c
    return n // 10, n % 10


def put(ref, i, c, value):
    band, at = block_at(i, c)
    ref[band * 128 : (band + 1) * 128, at * 128 : (at + 1) * 128] = value


def byte_grad_kernel(
    s, gkv, wk_o, wv_o, wk_x, wv_x, raw, bn, gain, gq, vec, bsum,
    back_o, back_x, keep, send, g, room,
):
    flip, side = long_second(s), own_side()
    for lo in range(0, g.shape[1], 256):
        here = slice(lo, lo + 256)
        weight = jnp.concatenate([ref[here, :] for ref in (wk_o, wv_o, wk_x, wv_x)], axis=1)
        g[:, here] = nt(gkv[...], weight)
    x = bn[...]
    width = gkv.shape[1] // 2
    tiles = [(out, at, c) for out, at in ((send, width), (keep, 0)) for c in range(0, width, 256)]

    def weights_grad(out, at, c):
        grad = tn(x, gkv[:, at + c : at + c + 256]).astype(BF16)
        for i in range(6):
            for n in range(2):
                put(out, i, c // 128 + n, grad[i * 128 : (i + 1) * 128, n * 128 : (n + 1) * 128])

    gain_sum = 0.0
    bias_sum = 0.0
    half = back_o.shape[0]
    for b in range(4):
        for tile in tiles[b * 3 // 2 : (b + 1) * 3 // 2]:
            weights_grad(*tile)
        here = slice(b * 128, (b + 1) * 128)
        grad = g[here, :]
        u, inverse = norm(raw[here, :].astype(F32))
        gain_sum = gain_sum + column_sum(grad * u)
        bias_sum = bias_sum + column_sum(grad)
        a = (b + flip) & 3
        to = (a & 1) * 128 + jnp.where((a >> 1) == side, 0, half)
        room[pl.ds(pl.multiple_of(to, 128), 128), :] = norm_back(grad, u, inverse, flat(gain))
    back_o[...] = room[:half, :]
    back_x[...] = room[half:, :].astype(BF16)
    own_q, oth_q = gq[:, :128], gq[:, 128:]
    half = gq.shape[0] // 2
    for n, part in enumerate((own_q, oth_q)):
        put(keep, 2 * n, 6, part[:half, :])
        put(keep, 2 * n + 1, 6, part[half:, :])
    for n, part in enumerate((oth_q, own_q)):
        put(send, 2 * n, 6, part[half:, :])
        put(send, 2 * n + 1, 6, part[:half, :])
    for out in (send, keep):
        out[512:, 256:] = jnp.zeros((128, out.shape[1] - 256), BF16)
    both = [vec[n : n + 1, :] for n in range(4)]
    tail = [gain_sum, bias_sum]
    for ref, middle in (
        (keep, [bsum[:, :640], bsum[:, 640:]]),
        (send, [bsum[:, 640:], bsum[:, :640]]),
    ):
        lines = []
        for value in both + middle + tail:
            for c in range(value.shape[1] // 128):
                lines.append(value[:, c * 128 : (c + 1) * 128])
        lines += [jnp.zeros((1, 128), F32)] * (128 - len(lines))
        put(ref, 4, 6, jnp.concatenate(lines, axis=0).astype(BF16))
        put(ref, 5, 6, jnp.zeros((128, 128), BF16))


CHIPS = 4


def chip_axes(index):
    return (index // (CHIPS * CHIPS), (index // CHIPS) % CHIPS, index % CHIPS)


def partner_pairs(axis, mask):
    pairs = []
    for chip in range(CHIPS**3):
        for side in range(2):
            where = list(chip_axes(chip))
            where[axis] ^= mask ^ (2 * side)
            other = (where[0] * CHIPS + where[1]) * CHIPS + where[2]
            pairs.append((chip * 2 + side, other * 2 + side))
    return pairs


def half_kept(dim):
    axis, mask = dim
    chip = lax.axis_index("dp")
    place = (chip >> (4, 2, 0)[axis]) & 3
    low, high = (place ^ (place >> 1)) & 1, place >> 1
    first, second = (low, high) if mask == 1 else (high, low)
    return jnp.where(lax.axis_index("tensor") == 0, first, second)


def with_half(kernel, dim):
    return lambda *refs: kernel(half_kept(dim), *refs)


def pair_swap(x, dim):
    return lax.ppermute(x, ("dp", "tensor"), partner_pairs(*dim))


def core_swap(x):
    return lax.ppermute(x, "tensor", [(0, 1), (1, 0)])


def add_low(a, b):
    return (a.astype(F32) + b.astype(F32)).astype(BF16)


def halve_parts(b, parts, keep, send):
    for out, half in ((send, 1 - b), (keep, b)):
        to = 0
        for x, r, at, rows in parts:
            from_ = pl.ds(pl.multiple_of(at + half * (rows // 2), 16), rows // 2)
            out[to : to + rows // 2, :] = add_low(x[from_, :], r[from_, :])
            to += rows // 2


def add_kernel(x, r, out):
    out[...] = add_low(x[...], r[...])


def join_kernel(low, b, x, r, out):
    rows = x.shape[0] - low
    for ref, half in ((x, b), (r, 1 - b)):
        out[pl.ds(pl.multiple_of(half * rows, 16), rows), :] = ref[:rows, :]
        out[pl.ds(pl.multiple_of(2 * rows + half * low, 16), low), :] = ref[rows:, :]


def last_up_kernel(b, x, r, out):
    rows = out.shape[1] // 2
    for n in range(2):
        ours = jnp.where(b == n, x[:rows, :].astype(F32), r[:rows, :].astype(F32))
        out[:, n * rows : (n + 1) * rows] = ours.T


def last_out_kernel(b, x, r, weight, res, rest):
    split = weight.shape[0]
    rows = (split + res.shape[0]) // 2
    for n in range(2):
        ours = jnp.where(b == n, x[:rows, :].astype(F32), r[:rows, :].astype(F32))
        if n == 0:
            weight[:rows, :] = ours
        else:
            weight[rows:, :] = ours[: split - rows, :]
            res[...] = ours[split - rows :, :]
    low = x.shape[0] - rows
    for n in range(2):
        part = jnp.where(b == n, x[rows:, :768].astype(F32), r[rows:, :768].astype(F32))
        for i in range(6):
            at = i * 128 + n * low
            rest[at : at + low, :] = part[:, i * 128 : (i + 1) * 128].astype(BF16)


def last_keys_kernel(lows, halves, *refs):
    *groups, down, key, value = refs
    bands = []
    for n, b in enumerate(halves):
        x, r = groups[2 * n : 2 * n + 2]
        xs, rs = x[x.shape[0] - lows[n] :, :], r[r.shape[0] - lows[n] :, :]
        pair = [jnp.where(b == h, xs.astype(F32), rs.astype(F32)) for h in range(2)]
        bands += pair if lows[n] == 128 else [jnp.concatenate(pair, axis=0)]
    for i in range(6):
        here = slice(i * 128, (i + 1) * 128)
        for c in range(6):
            band, at = block_at(i, c)
            block = bands[band][:, at * 128 : (at + 1) * 128]
            if c == 0:
                key[here, :] = block
            else:
                value[here, (c - 1) * 128 : c * 128] = block
    rows = down.shape[0] // 2
    x, r = groups[-2:]
    down[pl.ds(pl.multiple_of(halves[-1] * rows, 16), rows), :] = x[:rows, :].astype(F32)
    down[pl.ds(pl.multiple_of((1 - halves[-1]) * rows, 16), rows), :] = r[:rows, :].astype(F32)


class Group:
    def __init__(self, order, band, bands):
        self.dims = [(axis, mask) for axis in order for mask in (1, 3)]
        self.band, self.low = band, bands

    def first(self, x, r, keys, keys_r, after):
        rows, width, low, band = x.shape[0], x.shape[1], self.low, self.band

        def kernel(x, r, kx, kr, keep, send):
            parts = ((x, r, 0, rows), (kx, kr, band, low))
            halve_parts(half_kept(self.dims[0]), parts, keep, send)

        half = shape((rows + low) // 2, width)
        self.x, sent = call(kernel, (half, half), x, r, keys, keys_r, limit=4, after=after)
        self.low = low // 2
        self.r = pair_swap(sent, self.dims[0])
        return sent

    def halve(self, n, after):
        rows, low = self.x.shape[0] - self.low, self.low

        def kernel(x, r, keep, send):
            parts = ((x, r, 0, rows), (x, r, rows, low))
            halve_parts(half_kept(self.dims[n]), parts, keep, send)

        half = shape((rows + low) // 2, self.x.shape[1])
        self.x, sent = call(kernel, (half, half), self.x, self.r, limit=4, after=after)
        self.low = low // 2
        self.r = pair_swap(sent, self.dims[n])
        return sent

    def double(self, n, after):
        self.x = call(add_kernel, shape(*self.x.shape), self.x, self.r, limit=4, after=after)
        self.r = pair_swap(self.x, self.dims[n])
        return self.x

    def gather(self, n, after):
        rows, width = self.x.shape
        low = self.low

        def kernel(*refs):
            join_kernel(low, half_kept(self.dims[n + 1]), *refs)

        self.x = call(kernel, shape(2 * rows, width), self.x, self.r, limit=4, after=after)
        self.low = 2 * low
        self.r = pair_swap(self.x, self.dims[n])
        return self.x

    def end(self, kernel, outs, after):
        return call(with_half(kernel, self.dims[0]), outs, self.x, self.r, limit=8, after=after)


def finish_kernel(
    rest, latn, lat_o, lat_x, gain, wq_o, wq_x, res,
    wq_grad, lat_grad, lat_gain, lat_bias, b_down, mlp_gain, mlp_bias, b_out, b_up, in_gain, in_bias,
):
    lats = latn.shape[0]
    half = lats // 2
    own_q = rest[:lats, :]
    both_q = jnp.concatenate([own_q, rest[lats : 2 * lats, :]], axis=1)
    wq_grad[...] = tn(latn[...], own_q)
    g = nt(both_q, columns_of(wq_o, wq_x, 0, both_q.shape[1]))
    gain_sum = 0.0
    bias_sum = 0.0
    for i, ref in enumerate((lat_o, lat_x)):
        grad = g[i * half : (i + 1) * half, :]
        u, inverse = norm(ref[...].astype(F32))
        gain_sum = gain_sum + column_sum(grad * u)
        bias_sum = bias_sum + column_sum(grad)
        if i == 0:
            lat_grad[...] = res[...] + norm_back(grad, u, inverse, flat(gain))
    lat_gain[...] = gain_sum.reshape(lat_gain.shape)
    lat_bias[...] = bias_sum.reshape(lat_bias.shape)
    at = 2 * lats
    lines = rest[at : at + 64, :].astype(F32)
    at = 0
    for ref, count in (
        (b_down, 10), (mlp_gain, 10), (mlp_bias, 10), (b_out, 10), (b_up, 5), (None, 5),
        (in_gain, 6), (in_bias, 6),
    ):
        if ref is not None:
            parts = [lines[at + c : at + c + 1, :] for c in range(count)]
            ref[...] = jnp.concatenate(parts, axis=1).reshape(ref.shape)
        at += count


def per_device(
    byte_input, item_lengths, latent_array, in_gain, in_bias, lat_gain, lat_bias, w_query,
    w_key, w_value, w_out, b_out, mlp_gain, mlp_bias, w_up, b_up, w_down, b_down, grad_out,
):
    side = lax.axis_index("tensor")
    packs, tok_rows, in_width = byte_input.shape
    lat_rows, width = latent_array.shape
    items = item_lengths.shape[1]
    lats, toks, rows = 2 * lat_rows, 2 * tok_rows, 2 * lat_rows * items

    byte_x = core_swap(byte_input)
    def swap_after(x, *first):
        return core_swap(lax.optimization_barrier((x, *first))[0])

    wk_x = core_swap(w_key)
    wv_x = core_swap(w_value)
    lat_x = core_swap(latent_array)
    wq_x = core_swap(w_query)
    early = (byte_x, wk_x, wv_x, lat_x, wq_x)
    wo_x = swap_after(w_out, *early)
    top_x = swap_after(grad_out, *early)
    wu_x = swap_after(w_up, *early)
    bu_x = swap_after(b_up, *early)
    wd_x = swap_after(w_down, *early)

    operands = (latent_array, lat_x, lat_gain, lat_bias, w_query, wq_x)
    latn, q = call(
        latent_kernel, (shape(lats, width), shape(lats, 256)), *operands, far=range(6),
        scratch=rooms(*operands), limit=40,
    )
    operands = (byte_x, in_gain, in_bias, w_key, wk_x, w_value, wv_x)
    raw, bn, k, v = call(
        bytes_kernel,
        (shape(toks, in_width), shape(toks, in_width), shape(toks, 256), shape(toks, width)),
        item_lengths, byte_input, *operands, scalars=1, far=range(1, 9),
        scratch=rooms(byte_x[0], byte_x[0], *operands[1:]), limit=40,
    )
    gt = call(
        top_kernel, shape(rows, width), item_lengths, grad_out, top_x, scalars=1, far=(1, 2),
        scratch=rooms(grad_out[0], grad_out[0]),
    )
    att = call(attend_kernel, shape(rows, width), q, k, v)
    hidden, mn = call(
        out_kernel, (shape(rows, width, F32), shape(rows, width)),
        att, w_out, wo_x, latent_array, lat_x, b_out, mlp_gain, mlp_bias,
    )
    act, gp, bsum = call(
        up_kernel, (shape(rows, width), shape(rows, width), shape(1, width, F32)),
        mn, gt, w_up, wu_x, b_up, bu_x, w_down, wd_x,
    )

    z, y, x = 0, 1, 2
    out, up, down = groups = (
        Group((z, x, y), 0, 128), Group((y, z, x), 128, 256), Group((x, y, z), 384, 256)
    )
    matrix = shape(640, width)
    keep, send = call(down_grad_kernel, (matrix, matrix), act, gt)
    d = (keep, core_swap(send))
    keep, send = call(up_grad_kernel, (matrix, matrix), mn, gp, after=(send,))
    u = (keep, core_swap(send))
    ghl, res_o, res_x, vec = call(
        hidden_grad_kernel,
        (shape(rows, width), shape(lat_rows, width), shape(lat_rows, width), shape(4, width, F32)),
        gp, w_up, wu_x, hidden, gt, mlp_gain,
        scratch=[pltpu.VMEM((rows, width), F32)], after=(send,),
    )
    keep, send = call(
        out_grad_kernel, (shape(768, width), shape(768, width)), att, ghl, res_o, res_x,
        after=(vec, d[1], u[1]),
    )
    o = (keep, core_swap(send))
    ga = call(attended_grad_kernel, shape(rows, width), ghl, w_out, wo_x, after=(send,))
    gq, gkv = call(
        attend_back_kernel, (shape(lats, 256), shape(toks, 2 * 768)), q, k, v, ga, after=(ga,)
    )
    back, back_s, keep, send = call(
        byte_grad_kernel,
        (shape(tok_rows, in_width, F32), shape(tok_rows, in_width), matrix, matrix),
        item_lengths, gkv, w_key, w_value, wk_x, wv_x, raw, bn, in_gain, gq, vec, bsum,
        scalars=1, scratch=[pltpu.VMEM((toks, in_width), F32)] * 2, after=(gq, o[1]),
    )
    keys = (keep, core_swap(send))
    back_x = core_swap(back_s)
    enc, enc_s = call(
        encode_kernel,
        tuple(jax.ShapeDtypeStruct((lat_rows, items, width), BF16) for _ in range(2)),
        item_lengths, act, w_down, wd_x, hidden, b_down, scalars=1,
        scratch=[pltpu.VMEM((rows, width), BF16)], after=(send,),
    )
    enc_x = core_swap(enc_s)
    last = enc_s
    for group, main in zip(groups, (o, u, d)):
        last = group.first(*main, *keys, (last,))
    byte_grad = place(back, back_x, (last,))
    encoded = last = place(enc, enc_x, (byte_grad,))
    for n in (1, 2):
        for group in groups:
            last = group.halve(n, (last,))
    for n in (3, 4, 5):
        for group in groups:
            last = group.double(n, (last,))
    for group in groups:
        group.x = last = call(
            add_kernel, shape(*group.x.shape), group.x, group.r, limit=4, after=(last,)
        )
        group.r = pair_swap(group.x, group.dims[2])
    for n in (1, 0):
        for group in groups:
            last = group.gather(n, (last,))
    w_out_grad, res, rest = call(
        lambda *refs: last_out_kernel(half_kept(out.dims[0]), *refs),
        (shape(640, width, F32), shape(lat_rows, width, F32), shape(in_width, 128)),
        out.x, out.r, limit=8, after=(last,),
    )
    (
        w_query_grad, latent_grad, lat_gain_grad, lat_bias_grad, b_down_grad, mlp_gain_grad,
        mlp_bias_grad, b_out_grad, b_up_grad, in_gain_grad, in_bias_grad,
    ) = call(
        finish_kernel,
        (
            shape(width, 128, F32), shape(lat_rows, width, F32), *(line(width) for _ in range(6)),
            line(640), line(in_width), line(in_width),
        ),
        rest, latn, latent_array, lat_x, lat_gain, w_query, wq_x, res,
    )
    w_up_grad = call(
        lambda *refs: last_up_kernel(half_kept(up.dims[0]), *refs),
        shape(width, 640, F32), up.x, up.r, limit=8, after=(b_up_grad,),
    )

    def keys_kernel(*refs):
        halves = [half_kept(group.dims[0]) for group in groups]
        last_keys_kernel([group.low for group in groups], halves, *refs)

    w_down_grad, w_key_grad, w_value_grad = call(
        keys_kernel,
        (shape(640, width, F32), shape(in_width, 128, F32), shape(in_width, 640, F32)),
        *(a for group in groups for a in (group.x, group.r)), limit=8, after=(w_up_grad,),
    )
    return (
        encoded,
        byte_grad,
        latent_grad,
        in_gain_grad,
        in_bias_grad,
        lat_gain_grad,
        lat_bias_grad,
        w_query_grad,
        w_key_grad,
        w_value_grad,
        w_out_grad,
        b_out_grad,
        mlp_gain_grad,
        mlp_bias_grad,
        w_up_grad,
        b_up_grad,
        w_down_grad,
        b_down_grad,
    )


def solution(mesh):
    packs = P("dp", "tensor", None)
    columns = P(None, "tensor")
    lines = P("tensor", None)
    return jax.shard_map(
        per_device,
        mesh=mesh,
        in_specs=(
            packs, P("dp", None), lines, P(), P(), P(), P(), columns, columns, columns, lines,
            P(), P(), P(), columns, P("tensor"), lines, P(), P("dp", "tensor", None, None),
        ),
        out_specs=(
            P("dp", "tensor", None, None), packs, lines, P(), P(), P(), P(), columns, columns,
            columns, lines, P(), P(), P(), columns, P("tensor"), lines, P(),
        ),
        check_vma=False,
    )
```

```python
import jax
import jax.numpy as jnp
from jax import lax
from jax.experimental import pallas as pl
from jax.experimental.pallas import tpu as pltpu
from jax.sharding import PartitionSpec as P

F32 = jnp.float32
BF16 = jnp.bfloat16
EPS = 1e-05
HEAD_QK = 32
HEAD_V = 160
SCALE = HEAD_QK ** (-0.5)
MB = 1 << 20

SMEM = pl.BlockSpec(memory_space=pltpu.SMEM)
VMEM = pl.BlockSpec(memory_space=pltpu.VMEM)
HBM = pl.BlockSpec(memory_space=pltpu.HBM)


def shape(rows, columns, dtype=BF16):
    return jax.ShapeDtypeStruct((rows, columns), dtype)


def line(width):
    return jax.ShapeDtypeStruct((width,), F32)


def call(kernel, outs, *args, scalars=0, limit=12, scratch=(), after=(), far=(), place=None):
    if after:
        args = (*args[:-1], lax.optimization_barrier((args[-1], *after))[0])
    specs = [SMEM] * scalars + [HBM if n in far else VMEM for n in range(scalars, len(args))]
    return pl.pallas_call(
        kernel,
        out_shape=outs,
        in_specs=specs,
        out_specs=jax.tree.map(lambda _: VMEM, outs) if place is None else place,
        scratch_shapes=list(scratch),
        compiler_params=pltpu.CompilerParams(vmem_limit_bytes=limit * MB),
        cost_estimate=pl.CostEstimate(flops=0, bytes_accessed=0, transcendentals=0),
    )(*args)


def nn(a, b):
    return jnp.dot(a, b, preferred_element_type=F32)


def nt(a, b):
    return lax.dot_general(a, b, (((1,), (1,)), ((), ())), preferred_element_type=F32)


def tn(a, b):
    return lax.dot_general(a, b, (((0,), (0,)), ((), ())), preferred_element_type=F32)


def columns_of(o, x, lo, hi):
    width = o.shape[-1]
    if hi <= width:
        return o[:, lo:hi]
    if lo >= width:
        return x[:, lo - width : hi - width]
    return jnp.concatenate([o[:, lo:], x[:, : hi - width]], axis=1)


def rows_of(o, x, lo, hi):
    height = o.shape[0]
    if hi <= height:
        return o[lo:hi, :]
    if lo >= height:
        return x[lo - height : hi - height, :]
    return jnp.concatenate([o[lo:, :], x[: hi - height, :]], axis=0)


def store_columns(o, x, lo, hi, value):
    width = o.shape[-1]
    if hi <= width:
        o[:, lo:hi] = value
    elif lo >= width:
        x[:, lo - width : hi - width] = value
    else:
        o[:, lo:] = value[:, : width - lo]
        x[:, : hi - width] = value[:, width - lo :]


def norm(rows):
    average = jnp.mean(rows, axis=-1, keepdims=True)
    centered = rows - average
    variance = jnp.mean(centered * centered, axis=-1, keepdims=True)
    inverse = lax.rsqrt(variance + EPS)
    return centered * inverse, inverse


def norm_back(grad, normed, inverse, gain):
    scaled = grad * gain
    mean_term = jnp.mean(scaled, axis=-1, keepdims=True)
    cross_term = jnp.mean(scaled * normed, axis=-1, keepdims=True)
    return inverse * (scaled - mean_term - normed * cross_term)


def column_sum(x):
    return jnp.sum(x, axis=0, keepdims=True)


def flat(ref):
    return ref[...].reshape(1, -1)


def own_side():
    return lax.axis_index("tensor")


def long_second(lengths):
    side = own_side()
    return (lengths[side, 0] < lengths[side, 1]).astype(jnp.int32)


def place_kernel(own, got, packs, wide, sems):
    mine = pltpu.make_async_copy(own, packs.at[own_side()], sems.at[0])
    mine.start()
    if wide is None:
        source = got
    else:
        wide[...] = got[...].astype(wide.dtype)
        source = wide
    theirs = pltpu.make_async_copy(source, packs.at[1 - own_side()], sems.at[1])
    theirs.start()
    mine.wait()
    theirs.wait()


def place(own, got, after):
    wide = own.dtype != got.dtype

    def body(own, got, packs, *rest):
        place_kernel(own, got, packs, rest[0] if wide else None, rest[-1])

    return call(
        body, jax.ShapeDtypeStruct((2, *own.shape), own.dtype), own, got,
        limit=4, after=after, place=pl.BlockSpec(memory_space=pl.ANY),
        scratch=([pltpu.VMEM(own.shape, own.dtype)] if wide else []) + [sems(2)],
    )


def sems(count):
    return pltpu.SemaphoreType.DMA((count,))


def own_latent_kernel(lat, gain, bias, wq, packs, latn):
    u, _ = norm(lat[...].astype(F32))
    latn[...] = (u * flat(gain) + flat(bias)).astype(BF16)


def latent_kernel(latn_o, lat_x, gain, bias, wq_o, wq_x, latn, q):
    half = lat_x.shape[0]
    latn[:half, :] = latn_o[...]
    u, _ = norm(lat_x[...].astype(F32))
    latn[half:, :] = (u * flat(gain) + flat(bias)).astype(BF16)
    q[...] = nn(latn[...], columns_of(wq_o, wq_x, 0, q.shape[1])).astype(BF16)


def bytes_kernel(s, packs, packs_x, gain, bias, wk_o, wk_x, wv_o, wv_x, raw, bn, k, v):
    flip, side = long_second(s), own_side()
    for b in range(4):
        a = (b + flip) & 3
        off = pl.ds(pl.multiple_of((a & 1) * 128, 128), 128)
        mine = packs[side, off, :].astype(F32)
        other = packs_x[side, off, :].astype(F32)
        rows = jnp.where((a >> 1) == side, mine, other)
        here = slice(b * 128, (b + 1) * 128)
        raw[here, :] = rows.astype(BF16)
        u, _ = norm(rows)
        bn[here, :] = (u * flat(gain) + flat(bias)).astype(BF16)
    x = bn[...]
    k[...] = nn(x, columns_of(wk_o, wk_x, 0, k.shape[1])).astype(BF16)
    for lo in range(0, v.shape[1], 256):
        v[:, lo : lo + 256] = nn(x, columns_of(wv_o, wv_x, lo, lo + 256)).astype(BF16)


SEGMENTS = ((0, 384), (384, 512))


def join_heads(parts):
    rows = parts[0].shape[0]
    lane = lax.broadcasted_iota(jnp.int32, (rows, 128), 1)
    blocks = [parts[0][:, :128]]
    for c in range(1, 4):
        blocks.append(jnp.where(lane < 32 * c, parts[c - 1][:, 128:], parts[c][:, :128]))
    blocks.append(parts[3][:, 128:])
    return blocks


def attend_kernel(q, k, v, att):
    lats = q.shape[0]
    lane = lax.broadcasted_iota(jnp.int32, (lats, 128), 1)

    def scores(g, h):
        of_group = slice(g * 128, (g + 1) * 128)
        inside = (lane >= 32 * h) & (lane < 32 * h + 32)
        masked = jnp.where(inside, q[:, of_group].astype(F32), 0.0).astype(BF16)
        return nt(masked, k[:, of_group])

    heads = [(g, h) for g in range(2) for h in range(4)]
    following = scores(*heads[0])
    outs = [[], []]
    for n, (g, h) in enumerate(heads):
        s = following
        if n + 1 < len(heads):
            following = scores(*heads[n + 1])
        base = g * 640 + h * 128
        for i, (lo, hi) in enumerate(SEGMENTS):
            part = s[:, lo:hi]
            e = jnp.exp((part - jnp.max(part, axis=-1, keepdims=True)) * SCALE)
            total = jnp.sum(e, axis=-1, keepdims=True)
            outs[i].append(nn(e.astype(BF16), v[lo:hi, base : base + 256]) * (1.0 / total))
        if h == 3:
            for i in range(2):
                for c, block in enumerate(join_heads(outs[i])):
                    at = g * 640 + c * 128
                    att[i * lats : (i + 1) * lats, at : at + 128] = block.astype(BF16)
            outs = [[], []]


def out_kernel(att, wo_o, wo_x, lat_o, lat_x, b_out, gain, bias, hidden, mn):
    rows = lat_o.shape[0]

    def product(half):
        here = slice(half * 2 * rows, (half + 1) * 2 * rows)
        for lo in range(0, hidden.shape[1], 256):
            weight = jnp.concatenate([wo_o[:, lo : lo + 256], wo_x[:, lo : lo + 256]], axis=0)
            hidden[here, lo : lo + 256] = nn(att[here, :], weight)

    product(0)
    product(1)
    for i in range(4):
        here = slice(i * rows, (i + 1) * rows)
        x = hidden[here, :] + (lat_x if i % 2 else lat_o)[...].astype(F32) + flat(b_out)
        hidden[here, :] = x
        u, _ = norm(x)
        mn[here, :] = (u * flat(gain) + flat(bias)).astype(BF16)


def top_kernel(s, tops, tops_x, gt):
    flip, side = long_second(s), own_side()
    half = tops.shape[1]
    row = lax.broadcasted_iota(jnp.int32, (half, 2 * half), 0)
    column = lax.broadcasted_iota(jnp.int32, (half, 2 * half), 1)
    for j, ref in enumerate((tops, tops_x)):
        pairs = ref[side].reshape(2 * half, ref.shape[3])
        for i in range(2):
            chosen = jnp.where(column == 2 * row + (i ^ flip), 1.0, 0.0).astype(BF16)
            at = (2 * i + j) * half
            gt[at : at + half, :] = nn(chosen, pairs).astype(BF16)


def gelu_parts(x):
    cumulative = 0.5 * (1.0 + lax.erf(x * 0.7071067811865476))
    return x * cumulative, cumulative + x * (jnp.exp(-0.5 * x * x) * 0.3989422804014327)


def up_kernel(mn, gt, wu_o, wu_x, bu_o, bu_x, wd_o, wd_x, act, gp, bsum):
    bias = jnp.concatenate([flat(bu_o), flat(bu_x)], axis=1)
    for lo in range(0, act.shape[1], 256):
        hi = lo + 256
        pre = nn(mn[...], columns_of(wu_o, wu_x, lo, hi)) + bias[:, lo:hi]
        back = nt(gt[...], rows_of(wd_o, wd_x, lo, hi))
        active, slope = gelu_parts(pre)
        act[:, lo:hi] = active.astype(BF16)
        low = (back * slope).astype(BF16)
        gp[:, lo:hi] = low
        bsum[:, lo:hi] = column_sum(low.astype(F32))


def mlp_grad_kernel(act, gt, mn, gp, down, up, send):
    half = down.shape[0]
    send[:half, :] = tn(act[:, half:], gt[...]).astype(BF16)
    send[half:, :] = tn(gp[:, half:], mn[...]).astype(BF16)
    down[...] = tn(act[:, :half], gt[...]).astype(BF16)
    up[...] = tn(gp[:, :half], mn[...]).astype(BF16)


def encode_kernel(s, act, wd_o, wd_x, hidden, b_down, enc_o, enc_x, low):
    flip = long_second(s)
    for lo in range(0, low.shape[1], 256):
        hi = lo + 256
        weight = jnp.concatenate([wd_o[:, lo:hi], wd_x[:, lo:hi]], axis=0)
        out = nn(act[...], weight) + hidden[:, lo:hi] + flat(b_down)[:, lo:hi]
        low[:, lo:hi] = out.astype(BF16)
    half = enc_o.shape[0]
    row = lax.broadcasted_iota(jnp.int32, (2 * half, 2 * half), 0)
    column = lax.broadcasted_iota(jnp.int32, (2 * half, 2 * half), 1)
    item = (column // half) ^ flip
    chosen = jnp.where(row == 2 * (column % half) + item, 1.0, 0.0).astype(BF16)
    for j, ref in enumerate((enc_o, enc_x)):
        at = j * half
        both = jnp.concatenate([low[at : at + half, :], low[at + 2 * half : at + 3 * half, :]], axis=0)
        ref[...] = nn(chosen, both).astype(BF16).reshape(ref.shape)


def hidden_grad_kernel(gp, wu_o, wu_x, hidden, gt, gain, ghl, res_o, res_x, vec, g):
    rows = res_o.shape[0]

    def product(half):
        here = slice(half * 2 * rows, (half + 1) * 2 * rows)
        for lo in range(0, g.shape[1], 256):
            weight = jnp.concatenate([wu_o[lo : lo + 256, :], wu_x[lo : lo + 256, :]], axis=1)
            g[here, lo : lo + 256] = nt(gp[here, :], weight)

    product(0)
    product(1)
    sums = [0.0, 0.0, 0.0, 0.0]
    res = [0.0, 0.0]
    for i in range(4):
        here = slice(i * rows, (i + 1) * rows)
        grad = g[here, :]
        top = gt[here, :].astype(F32)
        u, inverse = norm(hidden[here, :])
        total = top + norm_back(grad, u, inverse, flat(gain))
        ghl[here, :] = total.astype(BF16)
        res[i % 2] = res[i % 2] + total
        for n, x in enumerate((top, grad * u, grad, total)):
            sums[n] = sums[n] + column_sum(x)
    res_o[...] = res[0].astype(BF16)
    res_x[...] = res[1].astype(BF16)
    for n in range(4):
        vec[n : n + 1, :] = sums[n]


def out_grad_kernel(att, ghl, res_o, res_x, keep, send):
    half = att.shape[1] // 2
    keep[:half, :] = tn(att[:, :half], ghl[...]).astype(BF16)
    send[:half, :] = tn(att[:, half:], ghl[...]).astype(BF16)
    keep[half:, :] = res_o[...]
    send[half:, :] = res_x[...]


def attended_grad_kernel(ghl, wo_o, wo_x, ga):
    for lo in range(0, ga.shape[1], 256):
        ga[:, lo : lo + 256] = nt(ghl[...], rows_of(wo_o, wo_x, lo, lo + 256)).astype(BF16)


def attend_back_kernel(q, k, v, ga, gq, gkv):
    lats = q.shape[0]
    lane = lax.broadcasted_iota(jnp.int32, (lats, 128), 1)
    wide = lax.broadcasted_iota(jnp.int32, (lats, 256), 1)
    groups = [slice(g * 128, (g + 1) * 128) for g in range(2)]
    masked = [
        [
            jnp.where((lane >= 32 * h) & (lane < 32 * h + 32), q[:, of].astype(F32), 0.0).astype(BF16)
            for h in range(4)
        ]
        for of in groups
    ]
    turned = [k[:, of].astype(F32).T.astype(BF16) for of in groups]
    order = [(g, i, h) for g in range(2) for i in range(2) for h in range(4)]

    def begin(g, i, h):
        lo, hi = SEGMENTS[i]
        base = g * 640 + h * 128
        gw = ga[i * lats : (i + 1) * lats, base : base + 256]
        inside = (wide >= 32 * h) & (wide < 32 * h + 160)
        gm = jnp.where(inside, gw.astype(F32), 0.0).astype(BF16)
        return nt(k[lo:hi, groups[g]], masked[g][h]), nt(v[lo:hi, base : base + 256], gm), gw

    ahead = [begin(*order[n]) for n in range(2)]
    gq_rows = {}
    gv = []
    gk = None
    for n, (g, i, h) in enumerate(order):
        lo, hi = SEGMENTS[i]
        s, gp, gw = ahead.pop(0)
        if n + 2 < len(order):
            ahead.append(begin(*order[n + 2]))
        e = jnp.exp((s - jnp.max(s, axis=0, keepdims=True)) * SCALE)
        p = e * (1.0 / jnp.sum(e, axis=0, keepdims=True))
        pg = p * gp
        gs = (pg - p * jnp.sum(pg, axis=0, keepdims=True)).astype(BF16)
        gv.append(nn(p.astype(BF16), gw))
        part = nn(gs, masked[g][h])
        gk = part if h == 0 else gk + part
        row = nn(turned[g][32 * h : 32 * h + 32, lo:hi], gs)
        gq_rows[g, h] = row if i == 0 else gq_rows[g, h] + row
        if h == 3:
            at = g * 768
            gkv[lo:hi, at : at + 128] = (gk * SCALE).astype(BF16)
            for c, block in enumerate(join_heads(gv)):
                to = at + 128 + c * 128
                gkv[lo:hi, to : to + 128] = block.astype(BF16)
            gv = []
    rows = [gq_rows[g, h] for g in range(2) for h in range(4)]
    gq[...] = (jnp.concatenate(rows, axis=0).T * SCALE).astype(BF16)


def block_at(i, c):
    n = i if c == 6 else 6 + 6 * i + c
    return n // 10, n % 10


def put(ref, i, c, value):
    band, at = block_at(i, c)
    ref[band * 128 : (band + 1) * 128, at * 128 : (at + 1) * 128] = value


def byte_grad_kernel(
    s, gkv, wk_o, wv_o, wk_x, wv_x, raw, bn, gain, gq, vec, bsum,
    back_o, back_x, keep, send, g, room,
):
    flip, side = long_second(s), own_side()
    for lo in range(0, g.shape[1], 256):
        here = slice(lo, lo + 256)
        weight = jnp.concatenate([ref[here, :] for ref in (wk_o, wv_o, wk_x, wv_x)], axis=1)
        g[:, here] = nt(gkv[...], weight)
    x = bn[...]
    width = gkv.shape[1] // 2
    tiles = [(out, at, c) for out, at in ((send, width), (keep, 0)) for c in range(0, width, 256)]

    def weights_grad(out, at, c):
        grad = tn(x, gkv[:, at + c : at + c + 256]).astype(BF16)
        for i in range(6):
            for n in range(2):
                put(out, i, c // 128 + n, grad[i * 128 : (i + 1) * 128, n * 128 : (n + 1) * 128])

    gain_sum = 0.0
    bias_sum = 0.0
    half = back_o.shape[0]
    for b in range(4):
        for tile in tiles[b * 3 // 2 : (b + 1) * 3 // 2]:
            weights_grad(*tile)
        here = slice(b * 128, (b + 1) * 128)
        grad = g[here, :]
        u, inverse = norm(raw[here, :].astype(F32))
        gain_sum = gain_sum + column_sum(grad * u)
        bias_sum = bias_sum + column_sum(grad)
        a = (b + flip) & 3
        to = (a & 1) * 128 + jnp.where((a >> 1) == side, 0, half)
        room[pl.ds(pl.multiple_of(to, 128), 128), :] = norm_back(grad, u, inverse, flat(gain))
    back_o[...] = room[:half, :]
    back_x[...] = room[half:, :].astype(BF16)
    own_q, oth_q = gq[:, :128], gq[:, 128:]
    half = gq.shape[0] // 2
    for n, part in enumerate((own_q, oth_q)):
        put(keep, 2 * n, 6, part[:half, :])
        put(keep, 2 * n + 1, 6, part[half:, :])
    for n, part in enumerate((oth_q, own_q)):
        put(send, 2 * n, 6, part[half:, :])
        put(send, 2 * n + 1, 6, part[:half, :])
    for out in (send, keep):
        out[512:, 256:] = jnp.zeros((128, out.shape[1] - 256), BF16)
    both = [vec[n : n + 1, :] for n in range(4)]
    tail = [gain_sum, bias_sum]
    for ref, middle in (
        (keep, [bsum[:, :640], bsum[:, 640:]]),
        (send, [bsum[:, 640:], bsum[:, :640]]),
    ):
        lines = []
        for value in both + middle + tail:
            for c in range(value.shape[1] // 128):
                lines.append(value[:, c * 128 : (c + 1) * 128])
        lines += [jnp.zeros((1, 128), F32)] * (128 - len(lines))
        put(ref, 4, 6, jnp.concatenate(lines, axis=0).astype(BF16))
        put(ref, 5, 6, jnp.zeros((128, 128), BF16))


CHIPS = 4


def chip_axes(index):
    return (index // (CHIPS * CHIPS), (index // CHIPS) % CHIPS, index % CHIPS)


def partner_pairs(axis, mask):
    pairs = []
    for chip in range(CHIPS**3):
        for side in range(2):
            where = list(chip_axes(chip))
            where[axis] ^= mask ^ (2 * side)
            other = (where[0] * CHIPS + where[1]) * CHIPS + where[2]
            pairs.append((chip * 2 + side, other * 2 + side))
    return pairs


def half_kept(dim):
    axis, mask = dim
    chip = lax.axis_index("dp")
    place = (chip >> (4, 2, 0)[axis]) & 3
    low, high = (place ^ (place >> 1)) & 1, place >> 1
    first, second = (low, high) if mask == 1 else (high, low)
    return jnp.where(lax.axis_index("tensor") == 0, first, second)


def with_half(kernel, dim):
    return lambda *refs: kernel(half_kept(dim), *refs)


def pair_swap(x, dim):
    return lax.ppermute(x, ("dp", "tensor"), partner_pairs(*dim))


def core_swap(x):
    return lax.ppermute(x, "tensor", [(0, 1), (1, 0)])


def add_low(a, b):
    return (a.astype(F32) + b.astype(F32)).astype(BF16)


def halve_parts(b, parts, keep, send):
    for out, half in ((send, 1 - b), (keep, b)):
        to = 0
        for x, r, at, rows in parts:
            from_ = pl.ds(pl.multiple_of(at + half * (rows // 2), 16), rows // 2)
            out[to : to + rows // 2, :] = add_low(x[from_, :], r[from_, :])
            to += rows // 2


def add_kernel(x, r, out):
    out[...] = add_low(x[...], r[...])


def join_kernel(low, b, x, r, out):
    rows = x.shape[0] - low
    for ref, half in ((x, b), (r, 1 - b)):
        out[pl.ds(pl.multiple_of(half * rows, 16), rows), :] = ref[:rows, :]
        out[pl.ds(pl.multiple_of(2 * rows + half * low, 16), low), :] = ref[rows:, :]


def last_up_kernel(b, x, r, out):
    rows = out.shape[1] // 2
    for n in range(2):
        ours = jnp.where(b == n, x[:rows, :].astype(F32), r[:rows, :].astype(F32))
        out[:, n * rows : (n + 1) * rows] = ours.T


def last_out_kernel(b, x, r, weight, res, rest):
    split = weight.shape[0]
    rows = (split + res.shape[0]) // 2
    for n in range(2):
        ours = jnp.where(b == n, x[:rows, :].astype(F32), r[:rows, :].astype(F32))
        if n == 0:
            weight[:rows, :] = ours
        else:
            weight[rows:, :] = ours[: split - rows, :]
            res[...] = ours[split - rows :, :]
    low = x.shape[0] - rows
    for n in range(2):
        part = jnp.where(b == n, x[rows:, :768].astype(F32), r[rows:, :768].astype(F32))
        for i in range(6):
            at = i * 128 + n * low
            rest[at : at + low, :] = part[:, i * 128 : (i + 1) * 128].astype(BF16)


def last_keys_kernel(lows, halves, *refs):
    *groups, down, key, value = refs
    bands = []
    for n, b in enumerate(halves):
        x, r = groups[2 * n : 2 * n + 2]
        xs, rs = x[x.shape[0] - lows[n] :, :], r[r.shape[0] - lows[n] :, :]
        pair = [jnp.where(b == h, xs.astype(F32), rs.astype(F32)) for h in range(2)]
        bands += pair if lows[n] == 128 else [jnp.concatenate(pair, axis=0)]
    for i in range(6):
        here = slice(i * 128, (i + 1) * 128)
        for c in range(6):
            band, at = block_at(i, c)
            block = bands[band][:, at * 128 : (at + 1) * 128]
            if c == 0:
                key[here, :] = block
            else:
                value[here, (c - 1) * 128 : c * 128] = block
    rows = down.shape[0] // 2
    x, r = groups[-2:]
    down[pl.ds(pl.multiple_of(halves[-1] * rows, 16), rows), :] = x[:rows, :].astype(F32)
    down[pl.ds(pl.multiple_of((1 - halves[-1]) * rows, 16), rows), :] = r[:rows, :].astype(F32)


class Group:
    def __init__(self, order, band, bands):
        self.dims = [(axis, mask) for axis in order for mask in (1, 3)]
        self.band, self.low = band, bands

    def first(self, x, r, at, keys, keys_r, after):
        rows, width, low, band = x.shape[0], x.shape[1], self.low, self.band

        def kernel(x, r, kx, kr, keep, send):
            parts = ((x, r.at[at : at + rows, :], 0, rows), (kx, kr, band, low))
            halve_parts(half_kept(self.dims[0]), parts, keep, send)

        half = shape((rows + low) // 2, width)
        self.x, sent = call(kernel, (half, half), x, r, keys, keys_r, limit=4, after=after)
        self.low = low // 2
        self.r = pair_swap(sent, self.dims[0])
        return sent

    def halve(self, n, after):
        rows, low = self.x.shape[0] - self.low, self.low

        def kernel(x, r, keep, send):
            parts = ((x, r, 0, rows), (x, r, rows, low))
            halve_parts(half_kept(self.dims[n]), parts, keep, send)

        half = shape((rows + low) // 2, self.x.shape[1])
        self.x, sent = call(kernel, (half, half), self.x, self.r, limit=4, after=after)
        self.low = low // 2
        self.r = pair_swap(sent, self.dims[n])
        return sent

    def double(self, n, after):
        self.x = call(add_kernel, shape(*self.x.shape), self.x, self.r, limit=4, after=after)
        self.r = pair_swap(self.x, self.dims[n])
        return self.x

    def gather(self, n, after):
        rows, width = self.x.shape
        low = self.low

        def kernel(*refs):
            join_kernel(low, half_kept(self.dims[n + 1]), *refs)

        self.x = call(kernel, shape(2 * rows, width), self.x, self.r, limit=4, after=after)
        self.low = 2 * low
        self.r = pair_swap(self.x, self.dims[n])
        return self.x

    def end(self, kernel, outs, after):
        return call(with_half(kernel, self.dims[0]), outs, self.x, self.r, limit=8, after=after)


def finish_kernel(
    rest, latn, lat_o, lat_x, gain, wq_o, wq_x, res,
    wq_grad, lat_grad, lat_gain, lat_bias, b_down, mlp_gain, mlp_bias, b_out, b_up, in_gain, in_bias,
):
    lats = latn.shape[0]
    half = lats // 2
    own_q = rest[:lats, :]
    both_q = jnp.concatenate([own_q, rest[lats : 2 * lats, :]], axis=1)
    wq_grad[...] = tn(latn[...], own_q)
    g = nt(both_q, columns_of(wq_o, wq_x, 0, both_q.shape[1]))
    gain_sum = 0.0
    bias_sum = 0.0
    for i, ref in enumerate((lat_o, lat_x)):
        grad = g[i * half : (i + 1) * half, :]
        u, inverse = norm(ref[...].astype(F32))
        gain_sum = gain_sum + column_sum(grad * u)
        bias_sum = bias_sum + column_sum(grad)
        if i == 0:
            lat_grad[...] = res[...] + norm_back(grad, u, inverse, flat(gain))
    lat_gain[...] = gain_sum.reshape(lat_gain.shape)
    lat_bias[...] = bias_sum.reshape(lat_bias.shape)
    at = 2 * lats
    lines = rest[at : at + 64, :].astype(F32)
    at = 0
    for ref, count in (
        (b_down, 10), (mlp_gain, 10), (mlp_bias, 10), (b_out, 10), (b_up, 5), (None, 5),
        (in_gain, 6), (in_bias, 6),
    ):
        if ref is not None:
            parts = [lines[at + c : at + c + 1, :] for c in range(count)]
            ref[...] = jnp.concatenate(parts, axis=1).reshape(ref.shape)
        at += count


def per_device(
    byte_input, item_lengths, latent_array, in_gain, in_bias, lat_gain, lat_bias, w_query,
    w_key, w_value, w_out, b_out, mlp_gain, mlp_bias, w_up, b_up, w_down, b_down, grad_out,
):
    side = lax.axis_index("tensor")
    packs, tok_rows, in_width = byte_input.shape
    lat_rows, width = latent_array.shape
    items = item_lengths.shape[1]
    lats, toks, rows = 2 * lat_rows, 2 * tok_rows, 2 * lat_rows * items

    byte_x = core_swap(byte_input)
    def swap_after(x, *first):
        return core_swap(lax.optimization_barrier((x, *first))[0])

    wk_x = core_swap(w_key)
    wv_x = core_swap(w_value)
    lat_x = core_swap(latent_array)
    wq_x = core_swap(w_query)
    latn_o = call(
        own_latent_kernel, shape(lat_rows, width), latent_array, lat_gain, lat_bias, w_query,
        byte_input,
    )
    early = (byte_x, wk_x, wv_x, lat_x, wq_x, latn_o)
    wo_x = swap_after(w_out, *early)
    top_x = swap_after(grad_out, *early)
    wu_x = swap_after(w_up, *early)
    bu_x = swap_after(b_up, *early)
    wd_x = swap_after(w_down, *early)

    latn, q = call(
        latent_kernel, (shape(lats, width), shape(lats, 256)),
        latn_o, lat_x, lat_gain, lat_bias, w_query, wq_x,
    )
    raw, bn, k, v = call(
        bytes_kernel,
        (shape(toks, in_width), shape(toks, in_width), shape(toks, 256), shape(toks, width)),
        item_lengths, byte_input, byte_x, in_gain, in_bias, w_key, wk_x, w_value, wv_x,
        scalars=1,
    )
    gt = call(top_kernel, shape(rows, width), item_lengths, grad_out, top_x, scalars=1)
    att = call(attend_kernel, shape(rows, width), q, k, v)
    hidden, mn = call(
        out_kernel, (shape(rows, width, F32), shape(rows, width)),
        att, w_out, wo_x, latent_array, lat_x, b_out, mlp_gain, mlp_bias,
    )
    act, gp, bsum = call(
        up_kernel, (shape(rows, width), shape(rows, width), shape(1, width, F32)),
        mn, gt, w_up, wu_x, b_up, bu_x, w_down, wd_x,
    )

    z, y, x = 0, 1, 2
    out, up, down = groups = (
        Group((z, x, y), 0, 128), Group((y, z, x), 128, 256), Group((x, y, z), 384, 256)
    )
    matrix = shape(640, width)
    keep_d, keep_u, send = call(
        mlp_grad_kernel, (matrix, matrix, shape(width, width)), act, gt, mn, gp
    )
    both_got = core_swap(send)
    ghl, res_o, res_x, vec = call(
        hidden_grad_kernel,
        (shape(rows, width), shape(lat_rows, width), shape(lat_rows, width), shape(4, width, F32)),
        gp, w_up, wu_x, hidden, gt, mlp_gain,
        scratch=[pltpu.VMEM((rows, width), F32)], after=(send,),
    )
    keep, send = call(
        out_grad_kernel, (shape(768, width), shape(768, width)), att, ghl, res_o, res_x,
        after=(vec,),
    )
    o = (keep, core_swap(send))
    ga = call(attended_grad_kernel, shape(rows, width), ghl, w_out, wo_x, after=(send,))
    gq, gkv = call(
        attend_back_kernel, (shape(lats, 256), shape(toks, 2 * 768)), q, k, v, ga, after=(ga, both_got)
    )
    back, back_s, keep, send = call(
        byte_grad_kernel,
        (shape(tok_rows, in_width, F32), shape(tok_rows, in_width), matrix, matrix),
        item_lengths, gkv, w_key, w_value, wk_x, wv_x, raw, bn, in_gain, gq, vec, bsum,
        scalars=1, scratch=[pltpu.VMEM((toks, in_width), F32)] * 2, after=(gq, o[1]),
    )
    keys = (keep, core_swap(send))
    back_x = core_swap(back_s)
    enc, enc_s = call(
        encode_kernel,
        tuple(jax.ShapeDtypeStruct((lat_rows, items, width), BF16) for _ in range(2)),
        item_lengths, act, w_down, wd_x, hidden, b_down, scalars=1,
        scratch=[pltpu.VMEM((rows, width), BF16)], after=(send,),
    )
    enc_x = core_swap(enc_s)
    last = enc_s
    mains = ((*o, 0), (keep_u, both_got, 640), (keep_d, both_got, 0))
    for group, main in zip(groups, mains):
        last = group.first(*main, *keys, (last,))
    byte_grad = place(back, back_x, (last,))
    encoded = last = place(enc, enc_x, (byte_grad,))
    for n in (1, 2):
        for group in groups:
            last = group.halve(n, (last,))
    for n in (3, 4, 5):
        for group in groups:
            last = group.double(n, (last,))
    for group in groups:
        group.x = last = call(
            add_kernel, shape(*group.x.shape), group.x, group.r, limit=4, after=(last,)
        )
        group.r = pair_swap(group.x, group.dims[2])
    for n in (1, 0):
        for group in groups:
            last = group.gather(n, (last,))
    w_out_grad, res, rest = call(
        lambda *refs: last_out_kernel(half_kept(out.dims[0]), *refs),
        (shape(640, width, F32), shape(lat_rows, width, F32), shape(in_width, 128)),
        out.x, out.r, limit=8, after=(last,),
    )
    (
        w_query_grad, latent_grad, lat_gain_grad, lat_bias_grad, b_down_grad, mlp_gain_grad,
        mlp_bias_grad, b_out_grad, b_up_grad, in_gain_grad, in_bias_grad,
    ) = call(
        finish_kernel,
        (
            shape(width, 128, F32), shape(lat_rows, width, F32), *(line(width) for _ in range(6)),
            line(640), line(in_width), line(in_width),
        ),
        rest, latn, latent_array, lat_x, lat_gain, w_query, wq_x, res,
    )
    w_up_grad = call(
        lambda *refs: last_up_kernel(half_kept(up.dims[0]), *refs),
        shape(width, 640, F32), up.x, up.r, limit=8, after=(b_up_grad,),
    )

    def keys_kernel(*refs):
        halves = [half_kept(group.dims[0]) for group in groups]
        last_keys_kernel([group.low for group in groups], halves, *refs)

    w_down_grad, w_key_grad, w_value_grad = call(
        keys_kernel,
        (shape(640, width, F32), shape(in_width, 128, F32), shape(in_width, 640, F32)),
        *(a for group in groups for a in (group.x, group.r)), limit=8, after=(w_up_grad,),
    )
    return (
        encoded,
        byte_grad,
        latent_grad,
        in_gain_grad,
        in_bias_grad,
        lat_gain_grad,
        lat_bias_grad,
        w_query_grad,
        w_key_grad,
        w_value_grad,
        w_out_grad,
        b_out_grad,
        mlp_gain_grad,
        mlp_bias_grad,
        w_up_grad,
        b_up_grad,
        w_down_grad,
        b_down_grad,
    )


def solution(mesh):
    packs = P("dp", "tensor", None)
    columns = P(None, "tensor")
    lines = P("tensor", None)
    return jax.shard_map(
        per_device,
        mesh=mesh,
        in_specs=(
            packs, P("dp", None), lines, P(), P(), P(), P(), columns, columns, columns, lines,
            P(), P(), P(), columns, P("tensor"), lines, P(), P("dp", "tensor", None, None),
        ),
        out_specs=(
            P("dp", "tensor", None, None), packs, lines, P(), P(), P(), P(), columns, columns,
            columns, lines, P(), P(), P(), columns, P("tensor"), lines, P(),
        ),
        check_vma=False,
    )
```

```python
import jax
import jax.numpy as jnp
from jax import lax
from jax.experimental import pallas as pl
from jax.experimental.pallas import tpu as pltpu
from jax.sharding import PartitionSpec as P

F32 = jnp.float32
BF16 = jnp.bfloat16
EPS = 1e-05
HEAD_QK = 32
HEAD_V = 160
SCALE = HEAD_QK ** (-0.5)
MB = 1 << 20

SMEM = pl.BlockSpec(memory_space=pltpu.SMEM)
VMEM = pl.BlockSpec(memory_space=pltpu.VMEM)
HBM = pl.BlockSpec(memory_space=pltpu.HBM)


def shape(rows, columns, dtype=BF16):
    return jax.ShapeDtypeStruct((rows, columns), dtype)


def line(width):
    return jax.ShapeDtypeStruct((width,), F32)


def call(kernel, outs, *args, scalars=0, limit=12, scratch=(), after=(), far=(), place=None):
    if after:
        args = (*args[:-1], lax.optimization_barrier((args[-1], *after))[0])
    specs = [SMEM] * scalars + [HBM if n in far else VMEM for n in range(scalars, len(args))]
    return pl.pallas_call(
        kernel,
        out_shape=outs,
        in_specs=specs,
        out_specs=jax.tree.map(lambda _: VMEM, outs) if place is None else place,
        scratch_shapes=list(scratch),
        compiler_params=pltpu.CompilerParams(vmem_limit_bytes=limit * MB),
        cost_estimate=pl.CostEstimate(flops=0, bytes_accessed=0, transcendentals=0),
    )(*args)


def nn(a, b):
    return jnp.dot(a, b, preferred_element_type=F32)


def nt(a, b):
    return lax.dot_general(a, b, (((1,), (1,)), ((), ())), preferred_element_type=F32)


def tn(a, b):
    return lax.dot_general(a, b, (((0,), (0,)), ((), ())), preferred_element_type=F32)


def columns_of(o, x, lo, hi):
    width = o.shape[-1]
    if hi <= width:
        return o[:, lo:hi]
    if lo >= width:
        return x[:, lo - width : hi - width]
    return jnp.concatenate([o[:, lo:], x[:, : hi - width]], axis=1)


def rows_of(o, x, lo, hi):
    height = o.shape[0]
    if hi <= height:
        return o[lo:hi, :]
    if lo >= height:
        return x[lo - height : hi - height, :]
    return jnp.concatenate([o[lo:, :], x[: hi - height, :]], axis=0)


def store_columns(o, x, lo, hi, value):
    width = o.shape[-1]
    if hi <= width:
        o[:, lo:hi] = value
    elif lo >= width:
        x[:, lo - width : hi - width] = value
    else:
        o[:, lo:] = value[:, : width - lo]
        x[:, : hi - width] = value[:, width - lo :]


def norm(rows):
    average = jnp.mean(rows, axis=-1, keepdims=True)
    centered = rows - average
    variance = jnp.mean(centered * centered, axis=-1, keepdims=True)
    inverse = lax.rsqrt(variance + EPS)
    return centered * inverse, inverse


def norm_back(grad, normed, inverse, gain):
    scaled = grad * gain
    mean_term = jnp.mean(scaled, axis=-1, keepdims=True)
    cross_term = jnp.mean(scaled * normed, axis=-1, keepdims=True)
    return inverse * (scaled - mean_term - normed * cross_term)


def column_sum(x):
    return jnp.sum(x, axis=0, keepdims=True)


def flat(ref):
    return ref[...].reshape(1, -1)


def own_side():
    return lax.axis_index("tensor")


def long_second(lengths):
    side = own_side()
    return (lengths[side, 0] < lengths[side, 1]).astype(jnp.int32)


def place_kernel(own, got, packs, wide, sems):
    mine = pltpu.make_async_copy(own, packs.at[own_side()], sems.at[0])
    mine.start()
    if wide is None:
        source = got
    else:
        wide[...] = got[...].astype(wide.dtype)
        source = wide
    theirs = pltpu.make_async_copy(source, packs.at[1 - own_side()], sems.at[1])
    theirs.start()
    mine.wait()
    theirs.wait()


def place(own, got, after):
    wide = own.dtype != got.dtype

    def body(own, got, packs, *rest):
        place_kernel(own, got, packs, rest[0] if wide else None, rest[-1])

    return call(
        body, jax.ShapeDtypeStruct((2, *own.shape), own.dtype), own, got,
        limit=4, after=after, place=pl.BlockSpec(memory_space=pl.ANY),
        scratch=([pltpu.VMEM(own.shape, own.dtype)] if wide else []) + [sems(2)],
    )


def sems(count):
    return pltpu.SemaphoreType.DMA((count,))


def own_latent_kernel(lat, gain, bias, wq, packs, latn):
    u, _ = norm(lat[...].astype(F32))
    latn[...] = (u * flat(gain) + flat(bias)).astype(BF16)


def latent_kernel(latn_o, lat_x, gain, bias, wq_o, wq_x, latn, q):
    half = lat_x.shape[0]
    latn[:half, :] = latn_o[...]
    u, _ = norm(lat_x[...].astype(F32))
    latn[half:, :] = (u * flat(gain) + flat(bias)).astype(BF16)
    q[...] = nn(latn[...], columns_of(wq_o, wq_x, 0, q.shape[1])).astype(BF16)


def bytes_kernel(s, packs, packs_x, gain, bias, wk_o, wk_x, wv_o, wv_x, raw, bn, k, v):
    flip, side = long_second(s), own_side()
    for b in range(4):
        a = (b + flip) & 3
        off = pl.ds(pl.multiple_of((a & 1) * 128, 128), 128)
        mine = packs[side, off, :].astype(F32)
        other = packs_x[side, off, :].astype(F32)
        rows = jnp.where((a >> 1) == side, mine, other)
        here = slice(b * 128, (b + 1) * 128)
        raw[here, :] = rows.astype(BF16)
        u, _ = norm(rows)
        bn[here, :] = (u * flat(gain) + flat(bias)).astype(BF16)
    x = bn[...]
    k[...] = nn(x, columns_of(wk_o, wk_x, 0, k.shape[1])).astype(BF16)
    for lo in range(0, v.shape[1], 256):
        v[:, lo : lo + 256] = nn(x, columns_of(wv_o, wv_x, lo, lo + 256)).astype(BF16)


SEGMENTS = ((0, 384), (384, 512))


def join_heads(parts):
    rows = parts[0].shape[0]
    lane = lax.broadcasted_iota(jnp.int32, (rows, 128), 1)
    blocks = [parts[0][:, :128]]
    for c in range(1, 4):
        blocks.append(jnp.where(lane < 32 * c, parts[c - 1][:, 128:], parts[c][:, :128]))
    blocks.append(parts[3][:, 128:])
    return blocks


def attend_kernel(q, k, v, att):
    lats = q.shape[0]
    lane = lax.broadcasted_iota(jnp.int32, (lats, 128), 1)

    def scores(g, h):
        of_group = slice(g * 128, (g + 1) * 128)
        inside = (lane >= 32 * h) & (lane < 32 * h + 32)
        masked = jnp.where(inside, q[:, of_group].astype(F32), 0.0).astype(BF16)
        return nt(masked, k[:, of_group])

    heads = [(g, h) for g in range(2) for h in range(4)]
    following = scores(*heads[0])
    outs = [[], []]
    for n, (g, h) in enumerate(heads):
        s = following
        if n + 1 < len(heads):
            following = scores(*heads[n + 1])
        base = g * 640 + h * 128
        for i, (lo, hi) in enumerate(SEGMENTS):
            part = s[:, lo:hi]
            e = jnp.exp((part - jnp.max(part, axis=-1, keepdims=True)) * SCALE)
            total = jnp.sum(e, axis=-1, keepdims=True)
            outs[i].append(nn(e.astype(BF16), v[lo:hi, base : base + 256]) * (1.0 / total))
        if h == 3:
            for i in range(2):
                for c, block in enumerate(join_heads(outs[i])):
                    at = g * 640 + c * 128
                    att[i * lats : (i + 1) * lats, at : at + 128] = block.astype(BF16)
            outs = [[], []]


def out_kernel(att, wo_o, wo_x, lat_o, lat_x, b_out, gain, bias, hidden, mn):
    rows = lat_o.shape[0]

    @pl.loop(0, hidden.shape[1] // 640)
    def _(n):
        here = pl.ds(pl.multiple_of(n * 640, 128), 640)
        weight = jnp.concatenate([wo_o[:, here], wo_x[:, here]], axis=0)
        hidden[:, here] = nn(att[...], weight)

    for i in range(4):
        here = slice(i * rows, (i + 1) * rows)
        x = hidden[here, :] + (lat_x if i % 2 else lat_o)[...].astype(F32) + flat(b_out)
        hidden[here, :] = x
        u, _ = norm(x)
        mn[here, :] = (u * flat(gain) + flat(bias)).astype(BF16)


def top_kernel(s, tops, tops_x, gt):
    flip, side = long_second(s), own_side()
    half = tops.shape[1]
    row = lax.broadcasted_iota(jnp.int32, (half, 2 * half), 0)
    column = lax.broadcasted_iota(jnp.int32, (half, 2 * half), 1)
    for j, ref in enumerate((tops, tops_x)):
        pairs = ref[side].reshape(2 * half, ref.shape[3])
        for i in range(2):
            chosen = jnp.where(column == 2 * row + (i ^ flip), 1.0, 0.0).astype(BF16)
            at = (2 * i + j) * half
            gt[at : at + half, :] = nn(chosen, pairs).astype(BF16)


def gelu_parts(x):
    cumulative = 0.5 * (1.0 + lax.erf(x * 0.7071067811865476))
    return x * cumulative, cumulative + x * (jnp.exp(-0.5 * x * x) * 0.3989422804014327)


def up_kernel(mn, gt, wu_o, wu_x, bu_o, bu_x, wd_o, wd_x, act, gp, bsum):
    bias = jnp.concatenate([flat(bu_o), flat(bu_x)], axis=1)
    for lo in range(0, act.shape[1], 256):
        hi = lo + 256
        pre = nn(mn[...], columns_of(wu_o, wu_x, lo, hi)) + bias[:, lo:hi]
        back = nt(gt[...], rows_of(wd_o, wd_x, lo, hi))
        active, slope = gelu_parts(pre)
        act[:, lo:hi] = active.astype(BF16)
        low = (back * slope).astype(BF16)
        gp[:, lo:hi] = low
        bsum[:, lo:hi] = column_sum(low.astype(F32))


def mlp_grad_kernel(act, gt, mn, gp, down, up, send):
    half = down.shape[0]
    send[:half, :] = tn(act[:, half:], gt[...]).astype(BF16)
    send[half:, :] = tn(gp[:, half:], mn[...]).astype(BF16)
    down[...] = tn(act[:, :half], gt[...]).astype(BF16)
    up[...] = tn(gp[:, :half], mn[...]).astype(BF16)


def encode_kernel(s, act, wd_o, wd_x, hidden, b_down, enc_o, enc_x, low):
    flip = long_second(s)
    @pl.loop(0, low.shape[1] // 256)
    def _(n):
        here = pl.ds(pl.multiple_of(n * 256, 256), 256)
        weight = jnp.concatenate([wd_o[:, here], wd_x[:, here]], axis=0)
        out = nn(act[...], weight) + hidden[:, here] + b_down[here].reshape(1, 256)
        low[:, here] = out.astype(BF16)

    half = enc_o.shape[0]
    row = lax.broadcasted_iota(jnp.int32, (2 * half, 2 * half), 0)
    column = lax.broadcasted_iota(jnp.int32, (2 * half, 2 * half), 1)
    item = (column // half) ^ flip
    chosen = jnp.where(row == 2 * (column % half) + item, 1.0, 0.0).astype(BF16)
    for j, ref in enumerate((enc_o, enc_x)):
        at = j * half
        both = jnp.concatenate([low[at : at + half, :], low[at + 2 * half : at + 3 * half, :]], axis=0)
        ref[...] = nn(chosen, both).astype(BF16).reshape(ref.shape)


def hidden_grad_kernel(gp, wu_o, wu_x, hidden, gt, gain, ghl, res_o, res_x, vec, g):
    rows = res_o.shape[0]

    def product(half):
        here = slice(half * 2 * rows, (half + 1) * 2 * rows)
        for lo in range(0, g.shape[1], 256):
            weight = jnp.concatenate([wu_o[lo : lo + 256, :], wu_x[lo : lo + 256, :]], axis=1)
            g[here, lo : lo + 256] = nt(gp[here, :], weight)

    product(0)
    product(1)
    sums = [0.0, 0.0, 0.0, 0.0]
    res = [0.0, 0.0]
    for i in range(4):
        here = slice(i * rows, (i + 1) * rows)
        grad = g[here, :]
        top = gt[here, :].astype(F32)
        u, inverse = norm(hidden[here, :])
        total = top + norm_back(grad, u, inverse, flat(gain))
        ghl[here, :] = total.astype(BF16)
        res[i % 2] = res[i % 2] + total
        for n, x in enumerate((top, grad * u, grad, total)):
            sums[n] = sums[n] + column_sum(x)
    res_o[...] = res[0].astype(BF16)
    res_x[...] = res[1].astype(BF16)
    for n in range(4):
        vec[n : n + 1, :] = sums[n]


def out_grad_kernel(att, ghl, res_o, res_x, keep, send):
    half = att.shape[1] // 2
    keep[:half, :] = tn(att[:, :half], ghl[...]).astype(BF16)
    send[:half, :] = tn(att[:, half:], ghl[...]).astype(BF16)
    keep[half:, :] = res_o[...]
    send[half:, :] = res_x[...]


def attended_grad_kernel(ghl, wo_o, wo_x, ga):
    for lo in range(0, ga.shape[1], 256):
        ga[:, lo : lo + 256] = nt(ghl[...], rows_of(wo_o, wo_x, lo, lo + 256)).astype(BF16)


def attend_back_kernel(q, k, v, ga, gq, gkv):
    lats = q.shape[0]
    lane = lax.broadcasted_iota(jnp.int32, (lats, 128), 1)
    wide = lax.broadcasted_iota(jnp.int32, (lats, 256), 1)
    groups = [slice(g * 128, (g + 1) * 128) for g in range(2)]
    masked = [
        [
            jnp.where((lane >= 32 * h) & (lane < 32 * h + 32), q[:, of].astype(F32), 0.0).astype(BF16)
            for h in range(4)
        ]
        for of in groups
    ]
    turned = [k[:, of].astype(F32).T.astype(BF16) for of in groups]
    order = [(g, i, h) for g in range(2) for i in range(2) for h in range(4)]

    def begin(g, i, h):
        lo, hi = SEGMENTS[i]
        base = g * 640 + h * 128
        gw = ga[i * lats : (i + 1) * lats, base : base + 256]
        inside = (wide >= 32 * h) & (wide < 32 * h + 160)
        gm = jnp.where(inside, gw.astype(F32), 0.0).astype(BF16)
        return nt(k[lo:hi, groups[g]], masked[g][h]), nt(v[lo:hi, base : base + 256], gm), gw

    ahead = [begin(*order[n]) for n in range(2)]
    gq_rows = {}
    gv = []
    gk = None
    for n, (g, i, h) in enumerate(order):
        lo, hi = SEGMENTS[i]
        s, gp, gw = ahead.pop(0)
        if n + 2 < len(order):
            ahead.append(begin(*order[n + 2]))
        e = jnp.exp((s - jnp.max(s, axis=0, keepdims=True)) * SCALE)
        p = e * (1.0 / jnp.sum(e, axis=0, keepdims=True))
        pg = p * gp
        gs = (pg - p * jnp.sum(pg, axis=0, keepdims=True)).astype(BF16)
        gv.append(nn(p.astype(BF16), gw))
        part = nn(gs, masked[g][h])
        gk = part if h == 0 else gk + part
        row = nn(turned[g][32 * h : 32 * h + 32, lo:hi], gs)
        gq_rows[g, h] = row if i == 0 else gq_rows[g, h] + row
        if h == 3:
            at = g * 768
            gkv[lo:hi, at : at + 128] = (gk * SCALE).astype(BF16)
            for c, block in enumerate(join_heads(gv)):
                to = at + 128 + c * 128
                gkv[lo:hi, to : to + 128] = block.astype(BF16)
            gv = []
    rows = [gq_rows[g, h] for g in range(2) for h in range(4)]
    gq[...] = (jnp.concatenate(rows, axis=0).T * SCALE).astype(BF16)


def block_at(i, c):
    n = i if c == 6 else 6 + 6 * i + c
    return n // 10, n % 10


def put(ref, i, c, value):
    band, at = block_at(i, c)
    ref[band * 128 : (band + 1) * 128, at * 128 : (at + 1) * 128] = value


def byte_grad_kernel(
    s, gkv, wk_o, wv_o, wk_x, wv_x, raw, bn, gain, gq, vec, bsum,
    back_o, back_x, keep, send, g, room,
):
    flip, side = long_second(s), own_side()
    for lo in range(0, g.shape[1], 256):
        here = slice(lo, lo + 256)
        weight = jnp.concatenate([ref[here, :] for ref in (wk_o, wv_o, wk_x, wv_x)], axis=1)
        g[:, here] = nt(gkv[...], weight)
    x = bn[...]
    width = gkv.shape[1] // 2
    tiles = [(out, at, c) for out, at in ((send, width), (keep, 0)) for c in range(0, width, 256)]

    def weights_grad(out, at, c):
        grad = tn(x, gkv[:, at + c : at + c + 256]).astype(BF16)
        for i in range(6):
            for n in range(2):
                put(out, i, c // 128 + n, grad[i * 128 : (i + 1) * 128, n * 128 : (n + 1) * 128])

    gain_sum = 0.0
    bias_sum = 0.0
    half = back_o.shape[0]
    for b in range(4):
        for tile in tiles[b * 3 // 2 : (b + 1) * 3 // 2]:
            weights_grad(*tile)
        here = slice(b * 128, (b + 1) * 128)
        grad = g[here, :]
        u, inverse = norm(raw[here, :].astype(F32))
        gain_sum = gain_sum + column_sum(grad * u)
        bias_sum = bias_sum + column_sum(grad)
        a = (b + flip) & 3
        to = (a & 1) * 128 + jnp.where((a >> 1) == side, 0, half)
        room[pl.ds(pl.multiple_of(to, 128), 128), :] = norm_back(grad, u, inverse, flat(gain))
    back_o[...] = room[:half, :]
    back_x[...] = room[half:, :].astype(BF16)
    own_q, oth_q = gq[:, :128], gq[:, 128:]
    half = gq.shape[0] // 2
    for n, part in enumerate((own_q, oth_q)):
        put(keep, 2 * n, 6, part[:half, :])
        put(keep, 2 * n + 1, 6, part[half:, :])
    for n, part in enumerate((oth_q, own_q)):
        put(send, 2 * n, 6, part[half:, :])
        put(send, 2 * n + 1, 6, part[:half, :])
    for out in (send, keep):
        out[512:, 256:] = jnp.zeros((128, out.shape[1] - 256), BF16)
    both = [vec[n : n + 1, :] for n in range(4)]
    tail = [gain_sum, bias_sum]
    for ref, middle in (
        (keep, [bsum[:, :640], bsum[:, 640:]]),
        (send, [bsum[:, 640:], bsum[:, :640]]),
    ):
        lines = []
        for value in both + middle + tail:
            for c in range(value.shape[1] // 128):
                lines.append(value[:, c * 128 : (c + 1) * 128])
        lines += [jnp.zeros((1, 128), F32)] * (128 - len(lines))
        put(ref, 4, 6, jnp.concatenate(lines, axis=0).astype(BF16))
        put(ref, 5, 6, jnp.zeros((128, 128), BF16))


CHIPS = 4


def chip_axes(index):
    return (index // (CHIPS * CHIPS), (index // CHIPS) % CHIPS, index % CHIPS)


def partner_pairs(axis, mask):
    pairs = []
    for chip in range(CHIPS**3):
        for side in range(2):
            where = list(chip_axes(chip))
            where[axis] ^= mask ^ (2 * side)
            other = (where[0] * CHIPS + where[1]) * CHIPS + where[2]
            pairs.append((chip * 2 + side, other * 2 + side))
    return pairs


def half_kept(dim):
    axis, mask = dim
    chip = lax.axis_index("dp")
    place = (chip >> (4, 2, 0)[axis]) & 3
    low, high = (place ^ (place >> 1)) & 1, place >> 1
    first, second = (low, high) if mask == 1 else (high, low)
    return jnp.where(lax.axis_index("tensor") == 0, first, second)


def with_half(kernel, dim):
    return lambda *refs: kernel(half_kept(dim), *refs)


def pair_swap(x, dim):
    return lax.ppermute(x, ("dp", "tensor"), partner_pairs(*dim))


def core_swap(x):
    return lax.ppermute(x, "tensor", [(0, 1), (1, 0)])


def add_low(a, b):
    return (a.astype(F32) + b.astype(F32)).astype(BF16)


def halve_parts(b, parts, keep, send):
    for out, half in ((send, 1 - b), (keep, b)):
        to = 0
        for x, r, at, rows in parts:
            from_ = pl.ds(pl.multiple_of(at + half * (rows // 2), 16), rows // 2)
            out[to : to + rows // 2, :] = add_low(x[from_, :], r[from_, :])
            to += rows // 2


def add_kernel(x, r, out):
    out[...] = add_low(x[...], r[...])


def join_kernel(low, b, x, r, out):
    rows = x.shape[0] - low
    for ref, half in ((x, b), (r, 1 - b)):
        out[pl.ds(pl.multiple_of(half * rows, 16), rows), :] = ref[:rows, :]
        out[pl.ds(pl.multiple_of(2 * rows + half * low, 16), low), :] = ref[rows:, :]


def last_up_kernel(b, x, r, out):
    rows = out.shape[1] // 2
    for n in range(2):
        ours = jnp.where(b == n, x[:rows, :].astype(F32), r[:rows, :].astype(F32))
        out[:, n * rows : (n + 1) * rows] = ours.T


def last_out_kernel(b, x, r, weight, res, rest):
    split = weight.shape[0]
    rows = (split + res.shape[0]) // 2
    for n in range(2):
        ours = jnp.where(b == n, x[:rows, :].astype(F32), r[:rows, :].astype(F32))
        if n == 0:
            weight[:rows, :] = ours
        else:
            weight[rows:, :] = ours[: split - rows, :]
            res[...] = ours[split - rows :, :]
    low = x.shape[0] - rows
    for n in range(2):
        part = jnp.where(b == n, x[rows:, :768].astype(F32), r[rows:, :768].astype(F32))
        for i in range(6):
            at = i * 128 + n * low
            rest[at : at + low, :] = part[:, i * 128 : (i + 1) * 128].astype(BF16)


def last_keys_kernel(lows, halves, *refs):
    *groups, down, key, value = refs
    bands = []
    for n, b in enumerate(halves):
        x, r = groups[2 * n : 2 * n + 2]
        xs, rs = x[x.shape[0] - lows[n] :, :], r[r.shape[0] - lows[n] :, :]
        pair = [jnp.where(b == h, xs.astype(F32), rs.astype(F32)) for h in range(2)]
        bands += pair if lows[n] == 128 else [jnp.concatenate(pair, axis=0)]
    for i in range(6):
        here = slice(i * 128, (i + 1) * 128)
        for c in range(6):
            band, at = block_at(i, c)
            block = bands[band][:, at * 128 : (at + 1) * 128]
            if c == 0:
                key[here, :] = block
            else:
                value[here, (c - 1) * 128 : c * 128] = block
    rows = down.shape[0] // 2
    x, r = groups[-2:]
    down[pl.ds(pl.multiple_of(halves[-1] * rows, 16), rows), :] = x[:rows, :].astype(F32)
    down[pl.ds(pl.multiple_of((1 - halves[-1]) * rows, 16), rows), :] = r[:rows, :].astype(F32)


class Group:
    def __init__(self, order, band, bands):
        self.dims = [(axis, mask) for axis in order for mask in (1, 3)]
        self.band, self.low = band, bands

    def first(self, x, r, at, keys, keys_r, after):
        rows, width, low, band = x.shape[0], x.shape[1], self.low, self.band

        def kernel(x, r, kx, kr, keep, send):
            parts = ((x, r.at[at : at + rows, :], 0, rows), (kx, kr, band, low))
            halve_parts(half_kept(self.dims[0]), parts, keep, send)

        half = shape((rows + low) // 2, width)
        self.x, sent = call(kernel, (half, half), x, r, keys, keys_r, limit=4, after=after)
        self.low = low // 2
        self.r = pair_swap(sent, self.dims[0])
        return sent

    def halve(self, n, after):
        rows, low = self.x.shape[0] - self.low, self.low

        def kernel(x, r, keep, send):
            parts = ((x, r, 0, rows), (x, r, rows, low))
            halve_parts(half_kept(self.dims[n]), parts, keep, send)

        half = shape((rows + low) // 2, self.x.shape[1])
        self.x, sent = call(kernel, (half, half), self.x, self.r, limit=4, after=after)
        self.low = low // 2
        self.r = pair_swap(sent, self.dims[n])
        return sent

    def double(self, n, after):
        self.x = call(add_kernel, shape(*self.x.shape), self.x, self.r, limit=4, after=after)
        self.r = pair_swap(self.x, self.dims[n])
        return self.x

    def gather(self, n, after):
        rows, width = self.x.shape
        low = self.low

        def kernel(*refs):
            join_kernel(low, half_kept(self.dims[n + 1]), *refs)

        self.x = call(kernel, shape(2 * rows, width), self.x, self.r, limit=4, after=after)
        self.low = 2 * low
        self.r = pair_swap(self.x, self.dims[n])
        return self.x

    def end(self, kernel, outs, after):
        return call(with_half(kernel, self.dims[0]), outs, self.x, self.r, limit=8, after=after)


def finish_kernel(
    rest, latn, lat_o, lat_x, gain, wq_o, wq_x, res,
    wq_grad, lat_grad, lat_gain, lat_bias, b_down, mlp_gain, mlp_bias, b_out, b_up, in_gain, in_bias,
):
    lats = latn.shape[0]
    half = lats // 2
    own_q = rest[:lats, :]
    both_q = jnp.concatenate([own_q, rest[lats : 2 * lats, :]], axis=1)
    wq_grad[...] = tn(latn[...], own_q)
    g = nt(both_q, columns_of(wq_o, wq_x, 0, both_q.shape[1]))
    gain_sum = 0.0
    bias_sum = 0.0
    for i, ref in enumerate((lat_o, lat_x)):
        grad = g[i * half : (i + 1) * half, :]
        u, inverse = norm(ref[...].astype(F32))
        gain_sum = gain_sum + column_sum(grad * u)
        bias_sum = bias_sum + column_sum(grad)
        if i == 0:
            lat_grad[...] = res[...] + norm_back(grad, u, inverse, flat(gain))
    lat_gain[...] = gain_sum.reshape(lat_gain.shape)
    lat_bias[...] = bias_sum.reshape(lat_bias.shape)
    at = 2 * lats
    lines = rest[at : at + 64, :].astype(F32)
    at = 0
    for ref, count in (
        (b_down, 10), (mlp_gain, 10), (mlp_bias, 10), (b_out, 10), (b_up, 5), (None, 5),
        (in_gain, 6), (in_bias, 6),
    ):
        if ref is not None:
            parts = [lines[at + c : at + c + 1, :] for c in range(count)]
            ref[...] = jnp.concatenate(parts, axis=1).reshape(ref.shape)
        at += count


def per_device(
    byte_input, item_lengths, latent_array, in_gain, in_bias, lat_gain, lat_bias, w_query,
    w_key, w_value, w_out, b_out, mlp_gain, mlp_bias, w_up, b_up, w_down, b_down, grad_out,
):
    side = lax.axis_index("tensor")
    packs, tok_rows, in_width = byte_input.shape
    lat_rows, width = latent_array.shape
    items = item_lengths.shape[1]
    lats, toks, rows = 2 * lat_rows, 2 * tok_rows, 2 * lat_rows * items

    byte_x = core_swap(byte_input)
    def swap_after(x, *first):
        return core_swap(lax.optimization_barrier((x, *first))[0])

    wk_x = core_swap(w_key)
    wv_x = core_swap(w_value)
    lat_x = core_swap(latent_array)
    wq_x = core_swap(w_query)
    latn_o = call(
        own_latent_kernel, shape(lat_rows, width), latent_array, lat_gain, lat_bias, w_query,
        byte_input,
    )
    early = (byte_x, wk_x, wv_x, lat_x, wq_x, latn_o)
    wo_x = swap_after(w_out, *early)
    top_x = swap_after(grad_out, *early)
    wu_x = swap_after(w_up, *early)
    bu_x = swap_after(b_up, *early)
    wd_x = swap_after(w_down, *early)

    latn, q = call(
        latent_kernel, (shape(lats, width), shape(lats, 256)),
        latn_o, lat_x, lat_gain, lat_bias, w_query, wq_x,
    )
    raw, bn, k, v = call(
        bytes_kernel,
        (shape(toks, in_width), shape(toks, in_width), shape(toks, 256), shape(toks, width)),
        item_lengths, byte_input, byte_x, in_gain, in_bias, w_key, wk_x, w_value, wv_x,
        scalars=1,
    )
    gt = call(top_kernel, shape(rows, width), item_lengths, grad_out, top_x, scalars=1)
    att = call(attend_kernel, shape(rows, width), q, k, v)
    hidden, mn = call(
        out_kernel, (shape(rows, width, F32), shape(rows, width)),
        att, w_out, wo_x, latent_array, lat_x, b_out, mlp_gain, mlp_bias,
    )
    act, gp, bsum = call(
        up_kernel, (shape(rows, width), shape(rows, width), shape(1, width, F32)),
        mn, gt, w_up, wu_x, b_up, bu_x, w_down, wd_x,
    )

    z, y, x = 0, 1, 2
    out, up, down = groups = (
        Group((z, x, y), 0, 128), Group((y, z, x), 128, 256), Group((x, y, z), 384, 256)
    )
    matrix = shape(640, width)
    keep_d, keep_u, send = call(
        mlp_grad_kernel, (matrix, matrix, shape(width, width)), act, gt, mn, gp
    )
    both_got = core_swap(send)
    ghl, res_o, res_x, vec = call(
        hidden_grad_kernel,
        (shape(rows, width), shape(lat_rows, width), shape(lat_rows, width), shape(4, width, F32)),
        gp, w_up, wu_x, hidden, gt, mlp_gain,
        scratch=[pltpu.VMEM((rows, width), F32)], after=(send,),
    )
    keep, send = call(
        out_grad_kernel, (shape(768, width), shape(768, width)), att, ghl, res_o, res_x,
        after=(vec,),
    )
    o = (keep, core_swap(send))
    ga = call(attended_grad_kernel, shape(rows, width), ghl, w_out, wo_x, after=(send,))
    gq, gkv = call(
        attend_back_kernel, (shape(lats, 256), shape(toks, 2 * 768)), q, k, v, ga, after=(ga, both_got)
    )
    back, back_s, keep, send = call(
        byte_grad_kernel,
        (shape(tok_rows, in_width, F32), shape(tok_rows, in_width), matrix, matrix),
        item_lengths, gkv, w_key, w_value, wk_x, wv_x, raw, bn, in_gain, gq, vec, bsum,
        scalars=1, scratch=[pltpu.VMEM((toks, in_width), F32)] * 2, after=(gq, o[1]),
    )
    keys = (keep, core_swap(send))
    back_x = core_swap(back_s)
    enc, enc_s = call(
        encode_kernel,
        tuple(jax.ShapeDtypeStruct((lat_rows, items, width), BF16) for _ in range(2)),
        item_lengths, act, w_down, wd_x, hidden, b_down, scalars=1,
        scratch=[pltpu.VMEM((rows, width), BF16)], after=(send,),
    )
    enc_x = core_swap(enc_s)
    last = enc_s
    mains = ((*o, 0), (keep_u, both_got, 640), (keep_d, both_got, 0))
    for group, main in zip(groups, mains):
        last = group.first(*main, *keys, (last,))
    byte_grad = place(back, back_x, (last,))
    encoded = last = place(enc, enc_x, (byte_grad,))
    for n in (1, 2):
        for group in groups:
            last = group.halve(n, (last,))
    for n in (3, 4, 5):
        for group in groups:
            last = group.double(n, (last,))
    for group in groups:
        group.x = last = call(
            add_kernel, shape(*group.x.shape), group.x, group.r, limit=4, after=(last,)
        )
        group.r = pair_swap(group.x, group.dims[2])
    for n in (1, 0):
        for group in groups:
            last = group.gather(n, (last,))
    w_out_grad, res, rest = call(
        lambda *refs: last_out_kernel(half_kept(out.dims[0]), *refs),
        (shape(640, width, F32), shape(lat_rows, width, F32), shape(in_width, 128)),
        out.x, out.r, limit=8, after=(last,),
    )
    (
        w_query_grad, latent_grad, lat_gain_grad, lat_bias_grad, b_down_grad, mlp_gain_grad,
        mlp_bias_grad, b_out_grad, b_up_grad, in_gain_grad, in_bias_grad,
    ) = call(
        finish_kernel,
        (
            shape(width, 128, F32), shape(lat_rows, width, F32), *(line(width) for _ in range(6)),
            line(640), line(in_width), line(in_width),
        ),
        rest, latn, latent_array, lat_x, lat_gain, w_query, wq_x, res,
    )
    w_up_grad = call(
        lambda *refs: last_up_kernel(half_kept(up.dims[0]), *refs),
        shape(width, 640, F32), up.x, up.r, limit=8, after=(b_up_grad,),
    )

    def keys_kernel(*refs):
        halves = [half_kept(group.dims[0]) for group in groups]
        last_keys_kernel([group.low for group in groups], halves, *refs)

    w_down_grad, w_key_grad, w_value_grad = call(
        keys_kernel,
        (shape(640, width, F32), shape(in_width, 128, F32), shape(in_width, 640, F32)),
        *(a for group in groups for a in (group.x, group.r)), limit=8, after=(w_up_grad,),
    )
    return (
        encoded,
        byte_grad,
        latent_grad,
        in_gain_grad,
        in_bias_grad,
        lat_gain_grad,
        lat_bias_grad,
        w_query_grad,
        w_key_grad,
        w_value_grad,
        w_out_grad,
        b_out_grad,
        mlp_gain_grad,
        mlp_bias_grad,
        w_up_grad,
        b_up_grad,
        w_down_grad,
        b_down_grad,
    )


def solution(mesh):
    packs = P("dp", "tensor", None)
    columns = P(None, "tensor")
    lines = P("tensor", None)
    return jax.shard_map(
        per_device,
        mesh=mesh,
        in_specs=(
            packs, P("dp", None), lines, P(), P(), P(), P(), columns, columns, columns, lines,
            P(), P(), P(), columns, P("tensor"), lines, P(), P("dp", "tensor", None, None),
        ),
        out_specs=(
            P("dp", "tensor", None, None), packs, lines, P(), P(), P(), P(), columns, columns,
            columns, lines, P(), P(), P(), columns, P("tensor"), lines, P(),
        ),
        check_vma=False,
    )
```

```python
import jax
import jax.numpy as jnp
from jax import lax
from jax.experimental import pallas as pl
from jax.experimental.pallas import tpu as pltpu
from jax.sharding import PartitionSpec as P

F32 = jnp.float32
BF16 = jnp.bfloat16
EPS = 1e-05
HEAD_QK = 32
HEAD_V = 160
SCALE = HEAD_QK ** (-0.5)
MB = 1 << 20

SMEM = pl.BlockSpec(memory_space=pltpu.SMEM)
VMEM = pl.BlockSpec(memory_space=pltpu.VMEM)
HBM = pl.BlockSpec(memory_space=pltpu.HBM)


def shape(rows, columns, dtype=BF16):
    return jax.ShapeDtypeStruct((rows, columns), dtype)


def line(width):
    return jax.ShapeDtypeStruct((width,), F32)


def call(kernel, outs, *args, scalars=0, limit=12, scratch=(), after=(), far=(), place=None):
    if after:
        args = (*args[:-1], lax.optimization_barrier((args[-1], *after))[0])
    specs = [SMEM] * scalars + [HBM if n in far else VMEM for n in range(scalars, len(args))]
    return pl.pallas_call(
        kernel,
        out_shape=outs,
        in_specs=specs,
        out_specs=jax.tree.map(lambda _: VMEM, outs) if place is None else place,
        scratch_shapes=list(scratch),
        compiler_params=pltpu.CompilerParams(vmem_limit_bytes=limit * MB),
        cost_estimate=pl.CostEstimate(flops=0, bytes_accessed=0, transcendentals=0),
    )(*args)


def nn(a, b):
    return jnp.dot(a, b, preferred_element_type=F32)


def nt(a, b):
    return lax.dot_general(a, b, (((1,), (1,)), ((), ())), preferred_element_type=F32)


def tn(a, b):
    return lax.dot_general(a, b, (((0,), (0,)), ((), ())), preferred_element_type=F32)


def columns_of(o, x, lo, hi):
    width = o.shape[-1]
    if hi <= width:
        return o[:, lo:hi]
    if lo >= width:
        return x[:, lo - width : hi - width]
    return jnp.concatenate([o[:, lo:], x[:, : hi - width]], axis=1)


def rows_of(o, x, lo, hi):
    height = o.shape[0]
    if hi <= height:
        return o[lo:hi, :]
    if lo >= height:
        return x[lo - height : hi - height, :]
    return jnp.concatenate([o[lo:, :], x[: hi - height, :]], axis=0)


def store_columns(o, x, lo, hi, value):
    width = o.shape[-1]
    if hi <= width:
        o[:, lo:hi] = value
    elif lo >= width:
        x[:, lo - width : hi - width] = value
    else:
        o[:, lo:] = value[:, : width - lo]
        x[:, : hi - width] = value[:, width - lo :]


def norm(rows):
    average = jnp.mean(rows, axis=-1, keepdims=True)
    centered = rows - average
    variance = jnp.mean(centered * centered, axis=-1, keepdims=True)
    inverse = lax.rsqrt(variance + EPS)
    return centered * inverse, inverse


def norm_back(grad, normed, inverse, gain):
    scaled = grad * gain
    mean_term = jnp.mean(scaled, axis=-1, keepdims=True)
    cross_term = jnp.mean(scaled * normed, axis=-1, keepdims=True)
    return inverse * (scaled - mean_term - normed * cross_term)


def column_sum(x):
    return jnp.sum(x, axis=0, keepdims=True)


def flat(ref):
    return ref[...].reshape(1, -1)


def own_side():
    return lax.axis_index("tensor")


def long_second(lengths):
    side = own_side()
    return (lengths[side, 0] < lengths[side, 1]).astype(jnp.int32)


def place_kernel(own, got, packs, wide, sems):
    mine = pltpu.make_async_copy(own, packs.at[own_side()], sems.at[0])
    mine.start()
    if wide is None:
        source = got
    else:
        wide[...] = got[...].astype(wide.dtype)
        source = wide
    theirs = pltpu.make_async_copy(source, packs.at[1 - own_side()], sems.at[1])
    theirs.start()
    mine.wait()
    theirs.wait()


def place(own, got, after):
    wide = own.dtype != got.dtype

    def body(own, got, packs, *rest):
        place_kernel(own, got, packs, rest[0] if wide else None, rest[-1])

    return call(
        body, jax.ShapeDtypeStruct((2, *own.shape), own.dtype), own, got,
        limit=4, after=after, place=pl.BlockSpec(memory_space=pl.ANY),
        scratch=([pltpu.VMEM(own.shape, own.dtype)] if wide else []) + [sems(2)],
    )


def sems(count):
    return pltpu.SemaphoreType.DMA((count,))


def own_latent_kernel(lat, gain, bias, wq, packs, latn):
    u, _ = norm(lat[...].astype(F32))
    latn[...] = (u * flat(gain) + flat(bias)).astype(BF16)


def latent_kernel(latn_o, lat_x, gain, bias, wq_o, wq_x, latn, q):
    half = lat_x.shape[0]
    latn[:half, :] = latn_o[...]
    u, _ = norm(lat_x[...].astype(F32))
    latn[half:, :] = (u * flat(gain) + flat(bias)).astype(BF16)
    q[...] = nn(latn[...], columns_of(wq_o, wq_x, 0, q.shape[1])).astype(BF16)


def bytes_kernel(s, packs, packs_x, gain, bias, wk_o, wk_x, wv_o, wv_x, raw, bn, k, v):
    flip, side = long_second(s), own_side()
    for b in range(4):
        a = (b + flip) & 3
        off = pl.ds(pl.multiple_of((a & 1) * 128, 128), 128)
        mine = packs[side, off, :].astype(F32)
        other = packs_x[side, off, :].astype(F32)
        rows = jnp.where((a >> 1) == side, mine, other)
        here = slice(b * 128, (b + 1) * 128)
        raw[here, :] = rows.astype(BF16)
        u, _ = norm(rows)
        bn[here, :] = (u * flat(gain) + flat(bias)).astype(BF16)
    x = bn[...]
    k[...] = nn(x, columns_of(wk_o, wk_x, 0, k.shape[1])).astype(BF16)
    for lo in range(0, v.shape[1], 256):
        v[:, lo : lo + 256] = nn(x, columns_of(wv_o, wv_x, lo, lo + 256)).astype(BF16)


SEGMENTS = ((0, 384), (384, 512))


def join_heads(parts):
    rows = parts[0].shape[0]
    lane = lax.broadcasted_iota(jnp.int32, (rows, 128), 1)
    blocks = [parts[0][:, :128]]
    for c in range(1, 4):
        blocks.append(jnp.where(lane < 32 * c, parts[c - 1][:, 128:], parts[c][:, :128]))
    blocks.append(parts[3][:, 128:])
    return blocks


def attend_kernel(q, k, v, att):
    lats = q.shape[0]
    lane = lax.broadcasted_iota(jnp.int32, (lats, 128), 1)

    def scores(g, h):
        of_group = slice(g * 128, (g + 1) * 128)
        inside = (lane >= 32 * h) & (lane < 32 * h + 32)
        masked = jnp.where(inside, q[:, of_group].astype(F32), 0.0).astype(BF16)
        return nt(masked, k[:, of_group])

    heads = [(g, h) for g in range(2) for h in range(4)]
    following = scores(*heads[0])
    outs = [[], []]
    for n, (g, h) in enumerate(heads):
        s = following
        if n + 1 < len(heads):
            following = scores(*heads[n + 1])
        base = g * 640 + h * 128
        for i, (lo, hi) in enumerate(SEGMENTS):
            part = s[:, lo:hi]
            e = jnp.exp((part - jnp.max(part, axis=-1, keepdims=True)) * SCALE)
            total = jnp.sum(e, axis=-1, keepdims=True)
            outs[i].append(nn(e.astype(BF16), v[lo:hi, base : base + 256]) * (1.0 / total))
        if h == 3:
            for i in range(2):
                for c, block in enumerate(join_heads(outs[i])):
                    at = g * 640 + c * 128
                    att[i * lats : (i + 1) * lats, at : at + 128] = block.astype(BF16)
            outs = [[], []]


def out_kernel(att, wo_o, wo_x, lat_o, lat_x, b_out, gain, bias, hidden, mn):
    rows = lat_o.shape[0]

    @pl.loop(0, 2)
    def _(half):
        here = pl.ds(pl.multiple_of(half * 2 * rows, 256), 2 * rows)
        for lo in range(0, hidden.shape[1], 256):
            weight = jnp.concatenate([wo_o[:, lo : lo + 256], wo_x[:, lo : lo + 256]], axis=0)
            hidden[here, lo : lo + 256] = nn(att[here, :], weight)

    for i in range(4):
        here = slice(i * rows, (i + 1) * rows)
        x = hidden[here, :] + (lat_x if i % 2 else lat_o)[...].astype(F32) + flat(b_out)
        hidden[here, :] = x
        u, _ = norm(x)
        mn[here, :] = (u * flat(gain) + flat(bias)).astype(BF16)


def top_kernel(s, tops, tops_x, gt):
    flip, side = long_second(s), own_side()
    half = tops.shape[1]
    row = lax.broadcasted_iota(jnp.int32, (half, 2 * half), 0)
    column = lax.broadcasted_iota(jnp.int32, (half, 2 * half), 1)
    for j, ref in enumerate((tops, tops_x)):
        pairs = ref[side].reshape(2 * half, ref.shape[3])
        for i in range(2):
            chosen = jnp.where(column == 2 * row + (i ^ flip), 1.0, 0.0).astype(BF16)
            at = (2 * i + j) * half
            gt[at : at + half, :] = nn(chosen, pairs).astype(BF16)


def gelu_parts(x):
    cumulative = 0.5 * (1.0 + lax.erf(x * 0.7071067811865476))
    return x * cumulative, cumulative + x * (jnp.exp(-0.5 * x * x) * 0.3989422804014327)


def up_kernel(mn, gt, wu_o, wu_x, bu_o, bu_x, wd_o, wd_x, act, gp, bsum):
    bias = jnp.concatenate([flat(bu_o), flat(bu_x)], axis=1)
    for lo in range(0, act.shape[1], 256):
        hi = lo + 256
        pre = nn(mn[...], columns_of(wu_o, wu_x, lo, hi)) + bias[:, lo:hi]
        back = nt(gt[...], rows_of(wd_o, wd_x, lo, hi))
        active, slope = gelu_parts(pre)
        act[:, lo:hi] = active.astype(BF16)
        low = (back * slope).astype(BF16)
        gp[:, lo:hi] = low
        bsum[:, lo:hi] = column_sum(low.astype(F32))


def mlp_grad_kernel(act, gt, mn, gp, down, up, send):
    half = down.shape[0]
    send[:half, :] = tn(act[:, half:], gt[...]).astype(BF16)
    send[half:, :] = tn(gp[:, half:], mn[...]).astype(BF16)
    down[...] = tn(act[:, :half], gt[...]).astype(BF16)
    up[...] = tn(gp[:, :half], mn[...]).astype(BF16)


def encode_kernel(s, act, wd_o, wd_x, hidden, b_down, enc_o, enc_x, low):
    flip = long_second(s)
    @pl.loop(0, low.shape[1] // 256)
    def _(n):
        here = pl.ds(pl.multiple_of(n * 256, 256), 256)
        weight = jnp.concatenate([wd_o[:, here], wd_x[:, here]], axis=0)
        out = nn(act[...], weight) + hidden[:, here] + b_down[here].reshape(1, 256)
        low[:, here] = out.astype(BF16)

    half = enc_o.shape[0]
    row = lax.broadcasted_iota(jnp.int32, (2 * half, 2 * half), 0)
    column = lax.broadcasted_iota(jnp.int32, (2 * half, 2 * half), 1)
    item = (column // half) ^ flip
    chosen = jnp.where(row == 2 * (column % half) + item, 1.0, 0.0).astype(BF16)
    for j, ref in enumerate((enc_o, enc_x)):
        at = j * half
        both = jnp.concatenate([low[at : at + half, :], low[at + 2 * half : at + 3 * half, :]], axis=0)
        ref[...] = nn(chosen, both).astype(BF16).reshape(ref.shape)


def hidden_grad_kernel(gp, wu_o, wu_x, hidden, gt, gain, ghl, res_o, res_x, vec, g):
    rows = res_o.shape[0]

    def product(half):
        here = slice(half * 2 * rows, (half + 1) * 2 * rows)
        for lo in range(0, g.shape[1], 256):
            weight = jnp.concatenate([wu_o[lo : lo + 256, :], wu_x[lo : lo + 256, :]], axis=1)
            g[here, lo : lo + 256] = nt(gp[here, :], weight)

    product(0)
    product(1)
    sums = [0.0, 0.0, 0.0, 0.0]
    res = [0.0, 0.0]
    for i in range(4):
        here = slice(i * rows, (i + 1) * rows)
        grad = g[here, :]
        top = gt[here, :].astype(F32)
        u, inverse = norm(hidden[here, :])
        total = top + norm_back(grad, u, inverse, flat(gain))
        ghl[here, :] = total.astype(BF16)
        res[i % 2] = res[i % 2] + total
        for n, x in enumerate((top, grad * u, grad, total)):
            sums[n] = sums[n] + column_sum(x)
    res_o[...] = res[0].astype(BF16)
    res_x[...] = res[1].astype(BF16)
    for n in range(4):
        vec[n : n + 1, :] = sums[n]


def out_grad_kernel(att, ghl, res_o, res_x, keep, send):
    half = att.shape[1] // 2
    keep[:half, :] = tn(att[:, :half], ghl[...]).astype(BF16)
    send[:half, :] = tn(att[:, half:], ghl[...]).astype(BF16)
    keep[half:, :] = res_o[...]
    send[half:, :] = res_x[...]


def attended_grad_kernel(ghl, wo_o, wo_x, ga):
    for lo in range(0, ga.shape[1], 256):
        ga[:, lo : lo + 256] = nt(ghl[...], rows_of(wo_o, wo_x, lo, lo + 256)).astype(BF16)


def attend_back_kernel(q, k, v, ga, gq, gkv):
    lats = q.shape[0]
    lane = lax.broadcasted_iota(jnp.int32, (lats, 128), 1)
    wide = lax.broadcasted_iota(jnp.int32, (lats, 256), 1)
    groups = [slice(g * 128, (g + 1) * 128) for g in range(2)]
    masked = [
        [
            jnp.where((lane >= 32 * h) & (lane < 32 * h + 32), q[:, of].astype(F32), 0.0).astype(BF16)
            for h in range(4)
        ]
        for of in groups
    ]
    turned = [k[:, of].astype(F32).T.astype(BF16) for of in groups]
    order = [(g, i, h) for g in range(2) for i in range(2) for h in range(4)]

    def begin(g, i, h):
        lo, hi = SEGMENTS[i]
        base = g * 640 + h * 128
        gw = ga[i * lats : (i + 1) * lats, base : base + 256]
        inside = (wide >= 32 * h) & (wide < 32 * h + 160)
        gm = jnp.where(inside, gw.astype(F32), 0.0).astype(BF16)
        return nt(k[lo:hi, groups[g]], masked[g][h]), nt(v[lo:hi, base : base + 256], gm), gw

    ahead = [begin(*order[n]) for n in range(2)]
    gq_rows = {}
    gv = []
    gk = None
    for n, (g, i, h) in enumerate(order):
        lo, hi = SEGMENTS[i]
        s, gp, gw = ahead.pop(0)
        if n + 2 < len(order):
            ahead.append(begin(*order[n + 2]))
        e = jnp.exp((s - jnp.max(s, axis=0, keepdims=True)) * SCALE)
        p = e * (1.0 / jnp.sum(e, axis=0, keepdims=True))
        pg = p * gp
        gs = (pg - p * jnp.sum(pg, axis=0, keepdims=True)).astype(BF16)
        gv.append(nn(p.astype(BF16), gw))
        part = nn(gs, masked[g][h])
        gk = part if h == 0 else gk + part
        row = nn(turned[g][32 * h : 32 * h + 32, lo:hi], gs)
        gq_rows[g, h] = row if i == 0 else gq_rows[g, h] + row
        if h == 3:
            at = g * 768
            gkv[lo:hi, at : at + 128] = (gk * SCALE).astype(BF16)
            for c, block in enumerate(join_heads(gv)):
                to = at + 128 + c * 128
                gkv[lo:hi, to : to + 128] = block.astype(BF16)
            gv = []
    rows = [gq_rows[g, h] for g in range(2) for h in range(4)]
    gq[...] = (jnp.concatenate(rows, axis=0).T * SCALE).astype(BF16)


def block_at(i, c):
    n = i if c == 6 else 6 + 6 * i + c
    return n // 10, n % 10


def put(ref, i, c, value):
    band, at = block_at(i, c)
    ref[band * 128 : (band + 1) * 128, at * 128 : (at + 1) * 128] = value


def byte_grad_kernel(
    s, gkv, wk_o, wv_o, wk_x, wv_x, raw, bn, gain, gq, vec, bsum,
    back_o, back_x, keep, send, g, room,
):
    flip, side = long_second(s), own_side()
    for lo in range(0, g.shape[1], 256):
        here = slice(lo, lo + 256)
        weight = jnp.concatenate([ref[here, :] for ref in (wk_o, wv_o, wk_x, wv_x)], axis=1)
        g[:, here] = nt(gkv[...], weight)
    x = bn[...]
    width = gkv.shape[1] // 2
    tiles = [(out, at, c) for out, at in ((send, width), (keep, 0)) for c in range(0, width, 256)]

    def weights_grad(out, at, c):
        grad = tn(x, gkv[:, at + c : at + c + 256]).astype(BF16)
        for i in range(6):
            for n in range(2):
                put(out, i, c // 128 + n, grad[i * 128 : (i + 1) * 128, n * 128 : (n + 1) * 128])

    gain_sum = 0.0
    bias_sum = 0.0
    half = back_o.shape[0]
    for b in range(4):
        for tile in tiles[b * 3 // 2 : (b + 1) * 3 // 2]:
            weights_grad(*tile)
        here = slice(b * 128, (b + 1) * 128)
        grad = g[here, :]
        u, inverse = norm(raw[here, :].astype(F32))
        gain_sum = gain_sum + column_sum(grad * u)
        bias_sum = bias_sum + column_sum(grad)
        a = (b + flip) & 3
        to = (a & 1) * 128 + jnp.where((a >> 1) == side, 0, half)
        room[pl.ds(pl.multiple_of(to, 128), 128), :] = norm_back(grad, u, inverse, flat(gain))
    back_o[...] = room[:half, :]
    back_x[...] = room[half:, :].astype(BF16)
    own_q, oth_q = gq[:, :128], gq[:, 128:]
    half = gq.shape[0] // 2
    for n, part in enumerate((own_q, oth_q)):
        put(keep, 2 * n, 6, part[:half, :])
        put(keep, 2 * n + 1, 6, part[half:, :])
    for n, part in enumerate((oth_q, own_q)):
        put(send, 2 * n, 6, part[half:, :])
        put(send, 2 * n + 1, 6, part[:half, :])
    for out in (send, keep):
        out[512:, 256:] = jnp.zeros((128, out.shape[1] - 256), BF16)
    both = [vec[n : n + 1, :] for n in range(4)]
    tail = [gain_sum, bias_sum]
    for ref, middle in (
        (keep, [bsum[:, :640], bsum[:, 640:]]),
        (send, [bsum[:, 640:], bsum[:, :640]]),
    ):
        lines = []
        for value in both + middle + tail:
            for c in range(value.shape[1] // 128):
                lines.append(value[:, c * 128 : (c + 1) * 128])
        lines += [jnp.zeros((1, 128), F32)] * (128 - len(lines))
        put(ref, 4, 6, jnp.concatenate(lines, axis=0).astype(BF16))
        put(ref, 5, 6, jnp.zeros((128, 128), BF16))


CHIPS = 4


def chip_axes(index):
    return (index // (CHIPS * CHIPS), (index // CHIPS) % CHIPS, index % CHIPS)


def partner_pairs(axis, mask):
    pairs = []
    for chip in range(CHIPS**3):
        for side in range(2):
            where = list(chip_axes(chip))
            where[axis] ^= mask ^ (2 * side)
            other = (where[0] * CHIPS + where[1]) * CHIPS + where[2]
            pairs.append((chip * 2 + side, other * 2 + side))
    return pairs


def half_kept(dim):
    axis, mask = dim
    chip = lax.axis_index("dp")
    place = (chip >> (4, 2, 0)[axis]) & 3
    low, high = (place ^ (place >> 1)) & 1, place >> 1
    first, second = (low, high) if mask == 1 else (high, low)
    return jnp.where(lax.axis_index("tensor") == 0, first, second)


def with_half(kernel, dim):
    return lambda *refs: kernel(half_kept(dim), *refs)


def pair_swap(x, dim):
    return lax.ppermute(x, ("dp", "tensor"), partner_pairs(*dim))


def core_swap(x):
    return lax.ppermute(x, "tensor", [(0, 1), (1, 0)])


def add_low(a, b):
    return (a.astype(F32) + b.astype(F32)).astype(BF16)


def halve_parts(b, parts, keep, send):
    for out, half in ((send, 1 - b), (keep, b)):
        to = 0
        for x, r, at, rows in parts:
            from_ = pl.ds(pl.multiple_of(at + half * (rows // 2), 16), rows // 2)
            out[to : to + rows // 2, :] = add_low(x[from_, :], r[from_, :])
            to += rows // 2


def add_kernel(x, r, out):
    out[...] = add_low(x[...], r[...])


def join_kernel(low, b, x, r, out):
    rows = x.shape[0] - low
    for ref, half in ((x, b), (r, 1 - b)):
        out[pl.ds(pl.multiple_of(half * rows, 16), rows), :] = ref[:rows, :]
        out[pl.ds(pl.multiple_of(2 * rows + half * low, 16), low), :] = ref[rows:, :]


def last_up_kernel(b, x, r, out):
    rows = out.shape[1] // 2
    for n in range(2):
        ours = jnp.where(b == n, x[:rows, :].astype(F32), r[:rows, :].astype(F32))
        out[:, n * rows : (n + 1) * rows] = ours.T


def last_out_kernel(b, x, r, weight, res, rest):
    split = weight.shape[0]
    rows = (split + res.shape[0]) // 2
    for n in range(2):
        ours = jnp.where(b == n, x[:rows, :].astype(F32), r[:rows, :].astype(F32))
        if n == 0:
            weight[:rows, :] = ours
        else:
            weight[rows:, :] = ours[: split - rows, :]
            res[...] = ours[split - rows :, :]
    low = x.shape[0] - rows
    for n in range(2):
        part = jnp.where(b == n, x[rows:, :768].astype(F32), r[rows:, :768].astype(F32))
        for i in range(6):
            at = i * 128 + n * low
            rest[at : at + low, :] = part[:, i * 128 : (i + 1) * 128].astype(BF16)


def last_keys_kernel(lows, halves, *refs):
    *groups, down, key, value = refs
    bands = []
    for n, b in enumerate(halves):
        x, r = groups[2 * n : 2 * n + 2]
        xs, rs = x[x.shape[0] - lows[n] :, :], r[r.shape[0] - lows[n] :, :]
        pair = [jnp.where(b == h, xs.astype(F32), rs.astype(F32)) for h in range(2)]
        bands += pair if lows[n] == 128 else [jnp.concatenate(pair, axis=0)]
    for i in range(6):
        here = slice(i * 128, (i + 1) * 128)
        for c in range(6):
            band, at = block_at(i, c)
            block = bands[band][:, at * 128 : (at + 1) * 128]
            if c == 0:
                key[here, :] = block
            else:
                value[here, (c - 1) * 128 : c * 128] = block
    rows = down.shape[0] // 2
    x, r = groups[-2:]
    down[pl.ds(pl.multiple_of(halves[-1] * rows, 16), rows), :] = x[:rows, :].astype(F32)
    down[pl.ds(pl.multiple_of((1 - halves[-1]) * rows, 16), rows), :] = r[:rows, :].astype(F32)


class Group:
    def __init__(self, order, band, bands):
        self.dims = [(axis, mask) for axis in order for mask in (1, 3)]
        self.band, self.low = band, bands

    def first(self, x, r, at, keys, keys_r, after):
        rows, width, low, band = x.shape[0], x.shape[1], self.low, self.band

        def kernel(x, r, kx, kr, keep, send):
            parts = ((x, r.at[at : at + rows, :], 0, rows), (kx, kr, band, low))
            halve_parts(half_kept(self.dims[0]), parts, keep, send)

        half = shape((rows + low) // 2, width)
        self.x, sent = call(kernel, (half, half), x, r, keys, keys_r, limit=4, after=after)
        self.low = low // 2
        self.r = pair_swap(sent, self.dims[0])
        return sent

    def halve(self, n, after):
        rows, low = self.x.shape[0] - self.low, self.low

        def kernel(x, r, keep, send):
            parts = ((x, r, 0, rows), (x, r, rows, low))
            halve_parts(half_kept(self.dims[n]), parts, keep, send)

        half = shape((rows + low) // 2, self.x.shape[1])
        self.x, sent = call(kernel, (half, half), self.x, self.r, limit=4, after=after)
        self.low = low // 2
        self.r = pair_swap(sent, self.dims[n])
        return sent

    def double(self, n, after):
        self.x = call(add_kernel, shape(*self.x.shape), self.x, self.r, limit=4, after=after)
        self.r = pair_swap(self.x, self.dims[n])
        return self.x

    def gather(self, n, after):
        rows, width = self.x.shape
        low = self.low

        def kernel(*refs):
            join_kernel(low, half_kept(self.dims[n + 1]), *refs)

        self.x = call(kernel, shape(2 * rows, width), self.x, self.r, limit=4, after=after)
        self.low = 2 * low
        self.r = pair_swap(self.x, self.dims[n])
        return self.x

    def end(self, kernel, outs, after):
        return call(with_half(kernel, self.dims[0]), outs, self.x, self.r, limit=8, after=after)


def finish_kernel(
    rest, latn, lat_o, lat_x, gain, wq_o, wq_x, res,
    wq_grad, lat_grad, lat_gain, lat_bias, b_down, mlp_gain, mlp_bias, b_out, b_up, in_gain, in_bias,
):
    lats = latn.shape[0]
    half = lats // 2
    own_q = rest[:lats, :]
    both_q = jnp.concatenate([own_q, rest[lats : 2 * lats, :]], axis=1)
    wq_grad[...] = tn(latn[...], own_q)
    g = nt(both_q, columns_of(wq_o, wq_x, 0, both_q.shape[1]))
    gain_sum = 0.0
    bias_sum = 0.0
    for i, ref in enumerate((lat_o, lat_x)):
        grad = g[i * half : (i + 1) * half, :]
        u, inverse = norm(ref[...].astype(F32))
        gain_sum = gain_sum + column_sum(grad * u)
        bias_sum = bias_sum + column_sum(grad)
        if i == 0:
            lat_grad[...] = res[...] + norm_back(grad, u, inverse, flat(gain))
    lat_gain[...] = gain_sum.reshape(lat_gain.shape)
    lat_bias[...] = bias_sum.reshape(lat_bias.shape)
    at = 2 * lats
    lines = rest[at : at + 64, :].astype(F32)
    at = 0
    for ref, count in (
        (b_down, 10), (mlp_gain, 10), (mlp_bias, 10), (b_out, 10), (b_up, 5), (None, 5),
        (in_gain, 6), (in_bias, 6),
    ):
        if ref is not None:
            parts = [lines[at + c : at + c + 1, :] for c in range(count)]
            ref[...] = jnp.concatenate(parts, axis=1).reshape(ref.shape)
        at += count


def per_device(
    byte_input, item_lengths, latent_array, in_gain, in_bias, lat_gain, lat_bias, w_query,
    w_key, w_value, w_out, b_out, mlp_gain, mlp_bias, w_up, b_up, w_down, b_down, grad_out,
):
    side = lax.axis_index("tensor")
    packs, tok_rows, in_width = byte_input.shape
    lat_rows, width = latent_array.shape
    items = item_lengths.shape[1]
    lats, toks, rows = 2 * lat_rows, 2 * tok_rows, 2 * lat_rows * items

    byte_x = core_swap(byte_input)
    def swap_after(x, *first):
        return core_swap(lax.optimization_barrier((x, *first))[0])

    wk_x = core_swap(w_key)
    wv_x = core_swap(w_value)
    lat_x = core_swap(latent_array)
    wq_x = core_swap(w_query)
    latn_o = call(
        own_latent_kernel, shape(lat_rows, width), latent_array, lat_gain, lat_bias, w_query,
        byte_input,
    )
    early = (byte_x, wk_x, wv_x, lat_x, wq_x, latn_o)
    wo_x = swap_after(w_out, *early)
    top_x = swap_after(grad_out, *early)
    wu_x = swap_after(w_up, *early)
    bu_x = swap_after(b_up, *early)
    wd_x = swap_after(w_down, *early)

    latn, q = call(
        latent_kernel, (shape(lats, width), shape(lats, 256)),
        latn_o, lat_x, lat_gain, lat_bias, w_query, wq_x,
    )
    raw, bn, k, v = call(
        bytes_kernel,
        (shape(toks, in_width), shape(toks, in_width), shape(toks, 256), shape(toks, width)),
        item_lengths, byte_input, byte_x, in_gain, in_bias, w_key, wk_x, w_value, wv_x,
        scalars=1,
    )
    gt = call(top_kernel, shape(rows, width), item_lengths, grad_out, top_x, scalars=1)
    att = call(attend_kernel, shape(rows, width), q, k, v)
    hidden, mn = call(
        out_kernel, (shape(rows, width, F32), shape(rows, width)),
        att, w_out, wo_x, latent_array, lat_x, b_out, mlp_gain, mlp_bias,
    )
    act, gp, bsum = call(
        up_kernel, (shape(rows, width), shape(rows, width), shape(1, width, F32)),
        mn, gt, w_up, wu_x, b_up, bu_x, w_down, wd_x,
    )

    z, y, x = 0, 1, 2
    out, up, down = groups = (
        Group((z, x, y), 0, 128), Group((y, z, x), 128, 256), Group((x, y, z), 384, 256)
    )
    matrix = shape(640, width)
    keep_d, keep_u, send = call(
        mlp_grad_kernel, (matrix, matrix, shape(width, width)), act, gt, mn, gp
    )
    both_got = core_swap(send)
    ghl, res_o, res_x, vec = call(
        hidden_grad_kernel,
        (shape(rows, width), shape(lat_rows, width), shape(lat_rows, width), shape(4, width, F32)),
        gp, w_up, wu_x, hidden, gt, mlp_gain,
        scratch=[pltpu.VMEM((rows, width), F32)], after=(send,),
    )
    keep, send = call(
        out_grad_kernel, (shape(768, width), shape(768, width)), att, ghl, res_o, res_x,
        after=(vec,),
    )
    o = (keep, core_swap(send))
    ga = call(attended_grad_kernel, shape(rows, width), ghl, w_out, wo_x, after=(send,))
    gq, gkv = call(
        attend_back_kernel, (shape(lats, 256), shape(toks, 2 * 768)), q, k, v, ga, after=(ga, both_got)
    )
    back, back_s, keep, send = call(
        byte_grad_kernel,
        (shape(tok_rows, in_width, F32), shape(tok_rows, in_width), matrix, matrix),
        item_lengths, gkv, w_key, w_value, wk_x, wv_x, raw, bn, in_gain, gq, vec, bsum,
        scalars=1, scratch=[pltpu.VMEM((toks, in_width), F32)] * 2, after=(gq, o[1]),
    )
    keys = (keep, core_swap(send))
    back_x = core_swap(back_s)
    enc, enc_s = call(
        encode_kernel,
        tuple(jax.ShapeDtypeStruct((lat_rows, items, width), BF16) for _ in range(2)),
        item_lengths, act, w_down, wd_x, hidden, b_down, scalars=1,
        scratch=[pltpu.VMEM((rows, width), BF16)], after=(send,),
    )
    enc_x = core_swap(enc_s)
    last = enc_s
    mains = ((*o, 0), (keep_u, both_got, 640), (keep_d, both_got, 0))
    for group, main in zip(groups, mains):
        last = group.first(*main, *keys, (last,))
    byte_grad = place(back, back_x, (last,))
    encoded = last = place(enc, enc_x, (byte_grad,))
    for n in (1, 2):
        for group in groups:
            last = group.halve(n, (last,))
    for n in (3, 4, 5):
        for group in groups:
            last = group.double(n, (last,))
    for group in groups:
        group.x = last = call(
            add_kernel, shape(*group.x.shape), group.x, group.r, limit=4, after=(last,)
        )
        group.r = pair_swap(group.x, group.dims[2])
    for n in (1, 0):
        for group in groups:
            last = group.gather(n, (last,))
    w_out_grad, res, rest = call(
        lambda *refs: last_out_kernel(half_kept(out.dims[0]), *refs),
        (shape(640, width, F32), shape(lat_rows, width, F32), shape(in_width, 128)),
        out.x, out.r, limit=8, after=(last,),
    )
    (
        w_query_grad, latent_grad, lat_gain_grad, lat_bias_grad, b_down_grad, mlp_gain_grad,
        mlp_bias_grad, b_out_grad, b_up_grad, in_gain_grad, in_bias_grad,
    ) = call(
        finish_kernel,
        (
            shape(width, 128, F32), shape(lat_rows, width, F32), *(line(width) for _ in range(6)),
            line(640), line(in_width), line(in_width),
        ),
        rest, latn, latent_array, lat_x, lat_gain, w_query, wq_x, res,
    )
    w_up_grad = call(
        lambda *refs: last_up_kernel(half_kept(up.dims[0]), *refs),
        shape(width, 640, F32), up.x, up.r, limit=8, after=(b_up_grad,),
    )

    def keys_kernel(*refs):
        halves = [half_kept(group.dims[0]) for group in groups]
        last_keys_kernel([group.low for group in groups], halves, *refs)

    w_down_grad, w_key_grad, w_value_grad = call(
        keys_kernel,
        (shape(640, width, F32), shape(in_width, 128, F32), shape(in_width, 640, F32)),
        *(a for group in groups for a in (group.x, group.r)), limit=8, after=(w_up_grad,),
    )
    return (
        encoded,
        byte_grad,
        latent_grad,
        in_gain_grad,
        in_bias_grad,
        lat_gain_grad,
        lat_bias_grad,
        w_query_grad,
        w_key_grad,
        w_value_grad,
        w_out_grad,
        b_out_grad,
        mlp_gain_grad,
        mlp_bias_grad,
        w_up_grad,
        b_up_grad,
        w_down_grad,
        b_down_grad,
    )


def solution(mesh):
    packs = P("dp", "tensor", None)
    columns = P(None, "tensor")
    lines = P("tensor", None)
    return jax.shard_map(
        per_device,
        mesh=mesh,
        in_specs=(
            packs, P("dp", None), lines, P(), P(), P(), P(), columns, columns, columns, lines,
            P(), P(), P(), columns, P("tensor"), lines, P(), P("dp", "tensor", None, None),
        ),
        out_specs=(
            P("dp", "tensor", None, None), packs, lines, P(), P(), P(), P(), columns, columns,
            columns, lines, P(), P(), P(), columns, P("tensor"), lines, P(),
        ),
        check_vma=False,
    )
```
